128 devices in a mesh: row: 16 (over y, z_hi, core), col: 8 (over x, z_lo).
Axes of the slice: x: 4, y: 4, z: 4 (z_hi: 2, z_lo: 2; z = z_hi * 2 + z_lo), core: 2. Of those that a mesh axis runs over, the one named last changes fastest.
Arguments:
- pair_rep: bfloat16 [1024, 1024, 128], P('row', 'col'), may hold values from -6 to 6
- norm_gain: float32 [2, 128], replicated, may hold values from 0.1 to 1.9
- norm_bias: float32 [2, 128], replicated, may hold values from -3 to 3
- proj_weight: bfloat16 [2, 4, 128, 128], replicated, may hold values from -0.5 to 0.5
- gate_weight: bfloat16 [2, 128, 128], replicated, may hold values from -0.5 to 0.5
- out_gain: float32 [2, 128], replicated, may hold values from 0.1 to 1.9
- out_bias: float32 [2, 128], replicated, may hold values from -3 to 3
- out_weight: bfloat16 [2, 128, 128], replicated, may hold values from -0.5 to 0.5
Outputs:
- updated: bfloat16 [1024, 1024, 128], P('row', 'col')
The draws below stay inside these ranges and needn't reach their ends.
All inputs are finite; a program needn't handle non-finite values.
Results may differ from the reference program's by a relative error of at most 0.008.
Values may be sent and summed in bfloat16 or wider, within the bound.
A program may use at most 64 MiB of HBM per device.

```python
import jax
import jax.numpy as jnp
from jax import lax

C = 128
H = 128
N = 1024
N_ROW = 16


def levels(key, shape, cuts, low, high):
    def one(axis_at, blocks):
        heights = jax.random.uniform(jax.random.fold_in(jax.random.fold_in(key, 6), axis_at), (blocks,), jnp.float32, low / len(cuts), high / len(cuts))
        return jnp.repeat(jnp.exp(heights), shape[axis_at] // blocks).reshape((-1,) + (1,) * (len(shape) - axis_at - 1))

    gain = one(*cuts[0])
    for cut in cuts[1:]:
        gain = gain * one(*cut)
    return gain


def scatter_about(own_key, dims, deviation, most, cuts=(), kind=jnp.bfloat16):
    loudness = levels(own_key, dims, cuts, -0.22, 0.18) if cuts else 1.0
    values = jax.random.normal(own_key, dims, jnp.float32) * deviation * loudness
    return jnp.minimum(jnp.maximum(values, -most), most).astype(kind)


def setup_inputs(seed: int = 0) -> dict:
    arg_keys = jax.random.split(jax.random.key(seed), 9)
    return {
        "pair_rep": scatter_about(arg_keys[0], (N, N, C), 1.0, 6.0, ((0, 16), (1, 8))),
        "norm_gain": jnp.clip(1.0 + 0.18 * jax.random.normal(arg_keys[1], (2, C), jnp.float32), 0.1, 1.9),
        "norm_bias": scatter_about(arg_keys[2], (2, C), 0.5, 3.0, (), jnp.float32),
        "proj_weight": scatter_about(arg_keys[3], (2, 4, C, H), C ** -0.5, 0.5),
        "gate_weight": scatter_about(arg_keys[4], (2, C, C), C ** -0.5, 0.5),
        "out_gain": jnp.clip(1.0 + 0.18 * jax.random.normal(arg_keys[5], (2, H), jnp.float32), 0.1, 1.9),
        "out_bias": scatter_about(arg_keys[6], (2, H), 0.5, 3.0, (), jnp.float32),
        "out_weight": scatter_about(arg_keys[7], (2, H, C), H ** -0.5, 0.5),
    }


def layer_norm(values, gain_vec, bias_vec, axis_index):
    mean_val = lax.optimization_barrier(jnp.mean(values, axis=axis_index, keepdims=True))
    centred = values - mean_val
    variance = lax.optimization_barrier(jnp.mean(centred * centred, axis=axis_index, keepdims=True))
    return centred * lax.rsqrt(variance + 1e-05) * gain_vec + bias_vec

def normalise_rows(row_block, gain_vec, bias_vec):
    normed = layer_norm(row_block.astype(jnp.float32), gain_vec, bias_vec, -1).astype(jnp.bfloat16)
    return normed.astype(jnp.float32)

def reference(pair_rep, norm_gain, norm_bias, proj_weight, gate_weight, out_gain, out_bias, out_weight):
    blocks = N // N_ROW
    current = pair_rep
    for update_index in range(2):
        stacked = current.reshape(N_ROW, blocks, N, C)
        weights = proj_weight[update_index].astype(jnp.float32)

        def front(row_block):
            wide = normalise_rows(row_block, norm_gain[update_index], norm_bias[update_index])
            projected = jnp.einsum('ijc,kch->khij', wide, weights, precision=lax.Precision.HIGHEST)
            left_side = (jax.nn.sigmoid(projected[0]) * projected[1]).astype(jnp.bfloat16)
            right_side = (jax.nn.sigmoid(projected[2]) * projected[3]).astype(jnp.bfloat16)
            return (left_side, right_side)
        left_all, right_all = lax.map(front, stacked)
        left_all = left_all.transpose(1, 0, 2, 3).reshape(H, N, N)
        right_all = right_all.transpose(1, 0, 2, 3).reshape(H, N, N)

        def plane(pieces):
            left_wide = pieces[0].astype(jnp.float32)
            right_wide = pieces[1].astype(jnp.float32)
            if update_index == 0:
                result = jnp.dot(left_wide, right_wide.T, precision=lax.Precision.HIGHEST)
            else:
                result = jnp.dot(left_wide.T, right_wide, precision=lax.Precision.HIGHEST)
            return result.astype(jnp.bfloat16)
        mixed = lax.map(plane, (left_all, right_all))
        mixed_rows = mixed.reshape(H, N_ROW, blocks, N).transpose(1, 0, 2, 3)
        gate_w = gate_weight[update_index].astype(jnp.float32)
        out_w = out_weight[update_index].astype(jnp.float32)
        gain_mix = out_gain[update_index][:, None, None]
        bias_mix = out_bias[update_index][:, None, None]

        def back(items):
            row_block, mixed_block = items
            wide = normalise_rows(row_block, norm_gain[update_index], norm_bias[update_index])
            gate = jax.nn.sigmoid(jnp.einsum('ijc,cd->ijd', wide, gate_w, precision=lax.Precision.HIGHEST))
            normed_mix = layer_norm(mixed_block.astype(jnp.float32), gain_mix, bias_mix, 0).astype(jnp.bfloat16)
            change = jnp.einsum('hij,hc->ijc', normed_mix.astype(jnp.float32), out_w, precision=lax.Precision.HIGHEST)
            return (row_block.astype(jnp.float32) + gate * change).astype(jnp.bfloat16)
        current = lax.map(back, (stacked, mixed_rows)).reshape(N, N, C)
    return current
```

```python
import functools

import jax
import jax.numpy as jnp
from jax import lax
from jax.experimental import pallas as pl
from jax.experimental.pallas import tpu as pltpu
from jax.sharding import PartitionSpec as P

F32, BF16 = jnp.float32, jnp.bfloat16
ROWS, COLS, N_ROW, N_COL, CH = 64, 128, 16, 8, 128
DEV = N_ROW * N_COL
GROUP = 16
MIB = 1 << 20
NT = (((1,), (1,)), ((), ()))
TN = (((0,), (0,)), ((), ()))
NN = (((1,), (0,)), ((), ()))


def sigmoid(v):
    return 0.5 * jnp.tanh(0.5 * v) + 0.5


def layer_norm(v, gain, bias):
    mean = jnp.mean(v, axis=-1, keepdims=True)
    centred = v - mean
    var = jnp.mean(centred * centred, axis=-1, keepdims=True)
    return centred * lax.rsqrt(var + 1e-5) * gain + bias


def dot(a, b, dims):
    return lax.dot_general(a, b, dims, preferred_element_type=F32)


def front_group(u, read, ng, nb, pw, normed, left, right, tl, tr):
    wt = jnp.concatenate([pw[u, k].T for k in range(4)], axis=0)
    gain, bias = ng[pl.ds(u, 1), :], nb[pl.ds(u, 1), :]
    for i in range(0, GROUP, 2):
        x = jnp.concatenate([read(i), read(i + 1)], axis=0).astype(F32)
        n = layer_norm(x, gain, bias).astype(BF16)
        normed[i] = n[:COLS]
        normed[i + 1] = n[COLS:]
        p = dot(wt, n, NT)
        lo = sigmoid(p[0:128]) * p[128:256]
        ro = sigmoid(p[256:384]) * p[384:512]
        for k in range(2):
            part = slice(k * COLS, (k + 1) * COLS)
            tl[pl.ds(i + k, CH, stride=GROUP), :] = lo[:, part]
            tr[pl.ds(i + k, CH, stride=GROUP), :] = ro[:, part]
    left[...] = tl[...].reshape(CH, GROUP, COLS).astype(BF16)
    right[...] = tr[...].reshape(CH, GROUP, COLS).astype(BF16)


def back_group(u, mixed, cur, normed, gw, og, ob, ow, new, tm, ts):
    m = mixed[...].astype(F32)
    mean = jnp.mean(m, axis=0)
    centred = m - mean[None]
    var = jnp.mean(centred * centred, axis=0)
    ts[...] = lax.rsqrt(var + 1e-5)
    tm[...] = centred.reshape(CH * GROUP, COLS)
    gain = jnp.broadcast_to(og[pl.ds(u, 1), :], (CH, CH)).T
    bias = jnp.broadcast_to(ob[pl.ds(u, 1), :], (CH, CH)).T
    for i in range(GROUP):
        c = tm[pl.ds(i, CH, stride=GROUP), :]
        nm = (c * ts[pl.ds(i, 1), :] * gain + bias).astype(BF16)
        change = dot(nm, ow[u], TN)
        gate = sigmoid(dot(normed[i], gw[u], NN))
        new[i] = (cur[i].astype(F32) + gate * change).astype(BF16)


def front_kernel(cur, ng, nb, pw, normed, left, right, tl, tr):
    front_group(0, lambda i: cur[i], ng, nb, pw, normed, left, right, tl, tr)


def mid_kernel(
    mixed, cur, normed0, ng, nb, pw, gw, og, ob, ow, new, normed, left, right, tl, tr, ts
):
    back_group(0, mixed, cur, normed0, gw, og, ob, ow, new, tl, ts)
    front_group(1, lambda i: new[i], ng, nb, pw, normed, left, right, tl, tr)


def back_kernel(mixed, cur, normed, gw, og, ob, ow, new, tm, ts):
    back_group(1, mixed, cur, normed, gw, og, ob, ow, new, tm, ts)


def target(s, row, col):
    core, a, b, c = lax.rem(s, 2), lax.rem(s // 2, 4), lax.rem(s // 8, 4), s // 32
    dx = a
    dy = lax.rem(a + b, 4)
    dz = lax.rem(a + b + c, 4)
    y, zh, k = row // 4, lax.rem(row // 2, 2), lax.rem(row, 2)
    x, zl = col // 2, lax.rem(col, 2)
    z = lax.rem(zh * 2 + zl + dz, 4)
    row = lax.rem(y + dy, 4) * 4 + (z // 2) * 2 + lax.rem(k + core, 2)
    col = lax.rem(x + dx, 4) * 2 + lax.rem(z, 2)
    return row, col


def comm_kernel(u, left, right, mixed, l_all, r_all, m_all, send_sem, recv_sem):
    row, col = lax.axis_index("row"), lax.axis_index("col")
    me = row * N_COL + col
    slot = col * N_ROW + row

    barrier = pltpu.get_barrier_semaphore()

    def greet(s, carry):
        pl.semaphore_signal(
            barrier, inc=1, device_id=target(s, row, col), device_id_type=pl.DeviceIdType.MESH
        )
        return carry

    lax.fori_loop(1, DEV, greet, 0)
    pl.semaphore_wait(barrier, DEV - 1)

    def spread(src, src_at, dst, here, k):
        pltpu.make_async_copy(src.at[src_at(row, col)], dst.at[here], recv_sem.at[k]).start()

        def send(s, carry):
            r, c = target(s, row, col)
            pltpu.make_async_remote_copy(
                src_ref=src.at[src_at(r, c)],
                dst_ref=dst.at[here],
                send_sem=send_sem.at[k],
                recv_sem=recv_sem.at[k],
                device_id=(r, c),
                device_id_type=pl.DeviceIdType.MESH,
            ).start()
            return carry

        lax.fori_loop(1, DEV, send, 0)

    def arrived(buf, k):
        pltpu.make_async_copy(buf, buf, recv_sem.at[k]).wait()

    def sent(buf, k):
        part = buf.at[pl.ds(0, DEV - 1)]
        pltpu.make_async_copy(part, part, send_sem.at[k]).wait()

    spread(right, lambda r, c: r * N_COL + c, r_all, slot, 0)
    spread(left, lambda r, c: r * N_COL + c, l_all, slot, 1)
    arrived(r_all, 0)
    arrived(l_all, 1)

    if u == 0:

        def rows(buf, start):
            parts = [buf[pl.ds(c * N_ROW + start, 4)].reshape(256, COLS) for c in range(N_COL)]
            return jnp.concatenate(parts, axis=1)

        def block(ib, carry):
            a = rows(l_all, ib * 4)
            for jb in range(4):
                out = dot(a, rows(r_all, jb * 4), NT).astype(BF16)
                for k in range(2):
                    m_all[pl.ds((2 * jb + k) * N_ROW + ib * 4, 4)] = out[
                        :, k * COLS : (k + 1) * COLS
                    ].reshape(4, ROWS, COLS)
            return carry

    else:

        def plane(buf, c):
            return buf[pl.ds(c * N_ROW, N_ROW)].reshape(1024, COLS)

        def block(ib, carry):
            a = jnp.concatenate([plane(l_all, 2 * ib).T, plane(l_all, 2 * ib + 1).T], axis=0)
            for jb in range(4):
                b = jnp.concatenate([plane(r_all, 2 * jb), plane(r_all, 2 * jb + 1)], axis=1)
                out = dot(a, b, NN).astype(BF16)
                for k in range(2):
                    m_all[pl.ds((2 * jb + k) * N_ROW + ib * 4, 4)] = out[
                        :, k * COLS : (k + 1) * COLS
                    ].reshape(4, ROWS, COLS)
            return carry

    lax.fori_loop(0, 4, block, 0)

    spread(m_all, lambda r, c: c * N_ROW + r, mixed, me, 2)
    arrived(mixed, 2)
    sent(right, 0)
    sent(left, 1)
    sent(m_all, 2)


PIECES = jax.ShapeDtypeStruct((DEV, ROWS, COLS), BF16)
PAIR = jax.ShapeDtypeStruct((ROWS, COLS, CH), BF16)


def by_group(u_shape):
    if u_shape == PIECES.shape:
        return pl.BlockSpec((DEV, GROUP, COLS), lambda g: (0, g, 0))
    return pl.BlockSpec((GROUP, COLS, CH), lambda g: (g, 0, 0))


def whole(a):
    return pl.BlockSpec(a.shape, lambda g: (0,) * a.ndim)


def shards(
    pair_rep, norm_gain, norm_bias, proj_weight, gate_weight, out_gain, out_bias, out_weight
):
    params = pltpu.CompilerParams(vmem_limit_bytes=40 * MIB)
    tile = pl.BlockSpec((GROUP, COLS, CH), lambda g: (g, 0, 0))
    piece = pl.BlockSpec((DEV, GROUP, COLS), lambda g: (0, g, 0))
    wide = pltpu.VMEM((CH * GROUP, COLS), F32)
    stat = pltpu.VMEM((GROUP, COLS), F32)
    grid = (ROWS // GROUP,)

    def comm(u, left, right):
        return pl.pallas_call(
            functools.partial(comm_kernel, u),
            out_shape=PIECES,
            in_specs=[pl.BlockSpec(memory_space=pltpu.VMEM)] * 2,
            out_specs=pl.BlockSpec(memory_space=pltpu.VMEM),
            scratch_shapes=[pltpu.VMEM(PIECES.shape, BF16)] * 3
            + [pltpu.SemaphoreType.DMA((3,))] * 2,
            compiler_params=pltpu.CompilerParams(
                collective_id=u, has_side_effects=True, vmem_limit_bytes=40 * MIB
            ),
            name="exchange" + str(u),
        )(left, right)

    normed, left, right = pl.pallas_call(
        front_kernel,
        grid=grid,
        out_shape=[PAIR, PIECES, PIECES],
        in_specs=[tile, whole(norm_gain), whole(norm_bias), whole(proj_weight)],
        out_specs=[tile, piece, piece],
        scratch_shapes=[wide, wide],
        compiler_params=params,
        name="front",
    )(pair_rep, norm_gain, norm_bias, proj_weight)
    mixed = comm(0, left, right)
    current, normed, left, right = pl.pallas_call(
        mid_kernel,
        grid=grid,
        out_shape=[PAIR, PAIR, PIECES, PIECES],
        in_specs=[piece, tile, tile]
        + [
            whole(a)
            for a in (
                norm_gain, norm_bias, proj_weight, gate_weight, out_gain, out_bias, out_weight
            )
        ],
        out_specs=[tile, tile, piece, piece],
        scratch_shapes=[wide, wide, stat],
        compiler_params=params,
        name="middle",
    )(
        mixed, pair_rep, normed, norm_gain, norm_bias, proj_weight, gate_weight, out_gain,
        out_bias, out_weight,
    )
    mixed = comm(1, left, right)
    return pl.pallas_call(
        back_kernel,
        grid=grid,
        out_shape=PAIR,
        in_specs=[piece, tile, tile]
        + [whole(a) for a in (gate_weight, out_gain, out_bias, out_weight)],
        out_specs=tile,
        scratch_shapes=[wide, stat],
        compiler_params=params,
        name="back",
    )(mixed, current, normed, gate_weight, out_gain, out_bias, out_weight)


def solution(mesh):
    placed = (P("row", "col", None), P(), P(), P(), P(), P(), P(), P())
    return jax.shard_map(
        shards, mesh=mesh, in_specs=placed, out_specs=P("row", "col", None), check_vma=False
    )
```

```python
import jax
import jax.numpy as jnp
from jax import lax
from jax.experimental import pallas as pl
from jax.experimental.pallas import tpu as pltpu
from jax.sharding import PartitionSpec as P

F32, BF16 = jnp.float32, jnp.bfloat16
ROWS, COLS, N_ROW, N_COL, CH = 64, 128, 16, 8, 128
DEV = N_ROW * N_COL
GROUP, HALF = 16, 32
MIB = 1 << 20
NT = (((1,), (1,)), ((), ()))
TN = (((0,), (0,)), ((), ()))
NN = (((1,), (0,)), ((), ()))
RIGHT, LEFT, MIXED = 0, 1, 2


def sigmoid(v):
    return 0.5 * jnp.tanh(0.5 * v) + 0.5


def layer_norm(v, gain, bias):
    mean = jnp.mean(v, axis=-1, keepdims=True)
    centred = v - mean
    var = jnp.mean(centred * centred, axis=-1, keepdims=True)
    return centred * lax.rsqrt(var + 1e-5) * gain + bias


def dot(a, b, dims):
    return lax.dot_general(a, b, dims, preferred_element_type=F32)


def target(s, row, col):
    core, a, b, c = lax.rem(s, 2), lax.rem(s // 2, 4), lax.rem(s // 8, 4), s // 32
    dx = a
    dy = lax.rem(a + b, 4)
    dz = lax.rem(a + b + c, 4)
    y, zh, k = row // 4, lax.rem(row // 2, 2), lax.rem(row, 2)
    x, zl = col // 2, lax.rem(col, 2)
    z = lax.rem(zh * 2 + zl + dz, 4)
    row = lax.rem(y + dy, 4) * 4 + (z // 2) * 2 + lax.rem(k + core, 2)
    col = lax.rem(x + dx, 4) * 2 + lax.rem(z, 2)
    return row, col


def kernel(
    pair_h, ng_h, nb_h, pw_h, gw_h, og_h, ob_h, ow_h, out_h,
    cur, normed, gate, left, right, l_all, r_all, lt, m_all, m_in,
    ng, nb, pw, gw, og, ob, ow, wt, gain_t, bias_t, tl, tr, ts,
    load_sem, param_sem, send_sem, recv_sem, out_sem,
):
    row, col = lax.axis_index("row"), lax.axis_index("col")
    me = row * N_COL + col

    def load(g):
        rows = pl.ds(g * GROUP, GROUP)
        return pltpu.make_async_copy(pair_h.at[rows], cur.at[0, rows], load_sem.at[g])

    params = [
        pltpu.make_async_copy(src, dst, param_sem.at[k])
        for k, (src, dst) in enumerate(
            ((pw_h, pw), (ng_h, ng), (nb_h, nb), (gw_h, gw), (og_h, og), (ob_h, ob), (ow_h, ow))
        )
    ]
    load(0).start()
    for copy in params:
        copy.start()
    for g in range(1, ROWS // GROUP):
        load(g).start()

    barrier = pltpu.get_barrier_semaphore()

    def greet(s, carry):
        pl.semaphore_signal(
            barrier, inc=1, device_id=target(s, row, col), device_id_type=pl.DeviceIdType.MESH
        )
        return carry

    lax.fori_loop(1, DEV, greet, 0)
    for copy in params:
        copy.wait()
    for u in range(2):
        for k in range(4):
            wt[u, k * CH : (k + 1) * CH] = pw[u, k].T
        gain_t[u] = jnp.broadcast_to(og[u : u + 1], (CH, CH)).T
        bias_t[u] = jnp.broadcast_to(ob[u : u + 1], (CH, CH)).T

    def front_group(u, g):
        base = g * GROUP
        for i in range(0, GROUP, 2):
            x = cur[u, pl.ds(base + i, 2)].reshape(2 * COLS, CH).astype(F32)
            n = layer_norm(x, ng[u : u + 1], nb[u : u + 1]).astype(BF16)
            normed[pl.ds(base + i, 2)] = n.reshape(2, COLS, CH)
            p = dot(wt[u], n, NT)
            lo = sigmoid(p[0:128]) * p[128:256]
            ro = sigmoid(p[256:384]) * p[384:512]
            for k in range(2):
                part = slice(k * COLS, (k + 1) * COLS)
                tl[pl.ds(i + k, CH, stride=GROUP), :] = lo[:, part]
                tr[pl.ds(i + k, CH, stride=GROUP), :] = ro[:, part]
        rows = pl.ds(pl.multiple_of(base, GROUP), GROUP)
        left[u, :, rows, :] = tl[...].reshape(CH, GROUP, COLS).astype(BF16)
        right[u, :, rows, :] = tr[...].reshape(CH, GROUP, COLS).astype(BF16)

    def gate_rows(u, step):
        n = normed[pl.ds(step * 4, 4)].reshape(4 * COLS, CH)
        gate[pl.ds(step * 4, 4)] = sigmoid(dot(n, gw[u], NN)).reshape(4, COLS, CH)

    def back_group(u, g):
        base = g * GROUP
        m = m_in[u, :, pl.ds(pl.multiple_of(base, GROUP), GROUP), :].astype(F32)
        mean = jnp.mean(m, axis=0)
        centred = m - mean[None]
        var = jnp.mean(centred * centred, axis=0)
        ts[...] = lax.rsqrt(var + 1e-5)
        tl[...] = centred.reshape(CH * GROUP, COLS)
        for i in range(GROUP):
            c = tl[pl.ds(i, CH, stride=GROUP), :]
            nm = (c * ts[pl.ds(i, 1), :] * gain_t[u] + bias_t[u]).astype(BF16)
            change = dot(nm, ow[u], TN)
            now = cur[u, base + i].astype(F32) + gate[base + i] * change
            cur[1 - u, base + i] = now.astype(BF16)

    def loop(count, body):
        def step(i, carry):
            body(i)
            return carry

        lax.fori_loop(0, count, step, 0)

    def spread(u, k, half):
        part = pl.ds(half * HALF, HALF)
        flight = (u * 3 + k) * 2 + half
        if k == MIXED:
            src_at = lambda r, c: m_all.at[u, c, r, part]
            dst = m_in.at[u, me, part]
        else:
            src, all_ = ((right, r_all), (left, l_all))[k]
            src_at = lambda r, c: src.at[u, r * N_COL + c, part]
            dst = all_.at[u, col, row, part]
        pltpu.make_async_copy(src_at(row, col), dst, recv_sem.at[flight]).start()

        def send(s, carry):
            r, c = target(s, row, col)
            pltpu.make_async_remote_copy(
                src_ref=src_at(r, c),
                dst_ref=dst,
                send_sem=send_sem.at[flight],
                recv_sem=recv_sem.at[flight],
                device_id=(r, c),
                device_id_type=pl.DeviceIdType.MESH,
            ).start()
            return carry

        lax.fori_loop(1, DEV, send, 0)

    def arrived(u, k, half):
        size = m_in.at[u, pl.ds(0, DEV // 2)]
        pltpu.make_async_copy(size, size, recv_sem.at[(u * 3 + k) * 2 + half]).wait()

    def sent(u, k, half):
        flight = (u * 3 + k) * 2 + half
        size = m_in.at[u, pl.ds(0, DEV // 2 - 1)]
        pltpu.make_async_copy(size, size, send_sem.at[flight]).wait()
        size = m_in.at[u, 0, pl.ds(0, HALF)]
        pltpu.make_async_copy(size, size, send_sem.at[flight]).wait()

    def put_mixed(u, half, jb, out):
        out = out.astype(BF16)
        for k in range(2):
            m_all[u, 2 * jb + k, :, pl.ds(half * HALF, HALF), :] = out[
                :, k * COLS : (k + 1) * COLS
            ].reshape(N_ROW, HALF, COLS)

    def mix_outgoing(half):
        a = jnp.concatenate(
            [
                l_all[0, c, :, half * HALF : (half + 1) * HALF, :].reshape(512, COLS)
                for c in range(N_COL)
            ],
            axis=1,
        )

        def block(jb):
            b = jnp.concatenate(
                [r_all[0, c, pl.ds(4 * jb, 4)].reshape(256, COLS) for c in range(N_COL)], axis=1
            )
            put_mixed(0, half, jb, dot(a, b, NT))

        loop(4, block)

    def turn(half):
        def block(c):
            part = l_all[1, c, :, half * HALF : (half + 1) * HALF, :].reshape(512, COLS)
            lt[half, pl.ds(2 * c, 2)] = part.T.reshape(2, ROWS, 512)

        loop(N_COL, block)

    def mix_incoming(half):
        rows = slice(half * HALF, (half + 1) * HALF)
        a = jnp.concatenate([lt[k, :, rows, :].reshape(512, 512) for k in range(2)], axis=1)

        def block(jb):
            b = jnp.concatenate(
                [
                    jnp.concatenate(
                        [
                            r_all[1, 2 * jb + c, :, k * HALF : (k + 1) * HALF, :].reshape(512, COLS)
                            for k in range(2)
                        ],
                        axis=0,
                    )
                    for c in range(2)
                ],
                axis=1,
            )
            put_mixed(1, half, jb, dot(a, b, NN))

        loop(4, block)

    for half in range(2):
        for g in range(2):
            load(2 * half + g).wait()
        loop(2, lambda g: front_group(0, 2 * half + g))
        if half == 0:
            pl.semaphore_wait(barrier, DEV - 1)
            spread(0, RIGHT, 0)
    spread(0, RIGHT, 1)
    spread(0, LEFT, 0)
    spread(0, LEFT, 1)
    loop(ROWS // 4, lambda s: gate_rows(0, s))
    arrived(0, RIGHT, 0)
    arrived(0, RIGHT, 1)
    for half in range(2):
        arrived(0, LEFT, half)
        mix_outgoing(half)
        spread(0, MIXED, half)
    for half in range(2):
        arrived(0, MIXED, half)

        def turnover(g):
            back_group(0, 2 * half + g)
            front_group(1, 2 * half + g)

        loop(2, turnover)
        spread(1, RIGHT, half)
        spread(1, LEFT, half)
    loop(ROWS // 4, lambda s: gate_rows(1, s))
    for half in range(2):
        arrived(1, RIGHT, half)
        arrived(1, LEFT, half)
        turn(half)
    for half in range(2):
        mix_incoming(half)
        spread(1, MIXED, half)

    def store(half):
        rows = pl.ds(half * HALF, HALF)
        return pltpu.make_async_copy(cur.at[0, rows], out_h.at[rows], out_sem.at[half])

    for half in range(2):
        arrived(1, MIXED, half)
        loop(2, lambda g: back_group(1, 2 * half + g))
        store(half).start()
    for u in range(2):
        for k in range(3):
            for half in range(2):
                sent(u, k, half)
    for half in range(2):
        store(half).wait()


def shards(*args):
    pieces = (2, DEV, ROWS, COLS)
    planes = (2, N_COL, N_ROW, ROWS, COLS)
    vmem = pltpu.VMEM
    scratch = [
        vmem((2, ROWS, COLS, CH), BF16),
        vmem((ROWS, COLS, CH), BF16),
        vmem((ROWS, COLS, CH), F32),
        vmem(pieces, BF16),
        vmem(pieces, BF16),
        vmem(planes, BF16),
        vmem(planes, BF16),
        vmem((2, N_ROW, ROWS, 512), BF16),
        vmem(planes, BF16),
        vmem(pieces, BF16),
    ]
    scratch += [vmem(a.shape, a.dtype) for a in args[1:]]
    scratch += [
        vmem((2, 4 * CH, CH), BF16),
        vmem((2, CH, CH), F32),
        vmem((2, CH, CH), F32),
        vmem((CH * GROUP, COLS), F32),
        vmem((CH * GROUP, COLS), F32),
        vmem((GROUP, COLS), F32),
        pltpu.SemaphoreType.DMA((ROWS // GROUP,)),
        pltpu.SemaphoreType.DMA((7,)),
        pltpu.SemaphoreType.DMA((12,)),
        pltpu.SemaphoreType.DMA((12,)),
        pltpu.SemaphoreType.DMA((2,)),
    ]
    return pl.pallas_call(
        kernel,
        out_shape=jax.ShapeDtypeStruct((ROWS, COLS, CH), BF16),
        in_specs=[pl.BlockSpec(memory_space=pl.ANY)] * 8,
        out_specs=pl.BlockSpec(memory_space=pl.ANY),
        scratch_shapes=scratch,
        compiler_params=pltpu.CompilerParams(
            collective_id=0, has_side_effects=True, vmem_limit_bytes=60 * MIB
        ),
        name="triangle",
    )(*args)


def solution(mesh):
    placed = (P("row", "col", None), P(), P(), P(), P(), P(), P(), P())
    return jax.shard_map(
        shards, mesh=mesh, in_specs=placed, out_specs=P("row", "col", None), check_vma=False
    )
```

```python
import jax
import jax.numpy as jnp
from jax import lax
from jax.experimental import pallas as pl
from jax.experimental.pallas import tpu as pltpu
from jax.sharding import PartitionSpec as P

F32, BF16 = jnp.float32, jnp.bfloat16
ROWS, COLS, N_ROW, N_COL, CH = 64, 128, 16, 8, 128
DEV = N_ROW * N_COL
GROUP, HALF = 16, 32
MIB = 1 << 20
NT = (((1,), (1,)), ((), ()))
TN = (((0,), (0,)), ((), ()))
NN = (((1,), (0,)), ((), ()))
RIGHT, LEFT, MIXED = 0, 1, 2


def sigmoid(v):
    return 0.5 * jnp.tanh(0.5 * v) + 0.5


def layer_norm(v, gain, bias):
    mean = jnp.mean(v, axis=-1, keepdims=True)
    centred = v - mean
    var = jnp.mean(centred * centred, axis=-1, keepdims=True)
    return centred * lax.rsqrt(var + 1e-5) * gain + bias


def dot(a, b, dims):
    return lax.dot_general(a, b, dims, preferred_element_type=F32)


def target(s, row, col):
    core, a, b, c = s // 64, lax.rem(s, 4), lax.rem(s // 4, 4), lax.rem(s // 16, 4)
    y, zh, k = row // 4, lax.rem(row // 2, 2), lax.rem(row, 2)
    x, zl = col // 2, lax.rem(col, 2)
    sign = 1 - 2 * k
    x = lax.rem(x + sign * a + 16, 4)
    y = lax.rem(y + sign * (a + b) + 16, 4)
    z = lax.rem(zh * 2 + zl + sign * (a + b + c) + 16, 4)
    row = y * 4 + (z // 2) * 2 + lax.rem(k + core, 2)
    col = x * 2 + lax.rem(z, 2)
    return row, col


def kernel(
    pair_h, ng_h, nb_h, pw_h, gw_h, og_h, ob_h, ow_h, out_h,
    cur, normed, gate, left, right, l_all, r_all, lt, m_all, m_in,
    ng, nb, pw, gw, og, ob, ow, wt, gain_t, bias_t, tl, tr, ts,
    load_sem, param_sem, send_sem, recv_sem, out_sem,
):
    row, col = lax.axis_index("row"), lax.axis_index("col")
    me = row * N_COL + col

    def load(g):
        rows = pl.ds(g * GROUP, GROUP)
        return pltpu.make_async_copy(pair_h.at[rows], cur.at[0, rows], load_sem.at[g])

    params = [
        pltpu.make_async_copy(src, dst, param_sem.at[k])
        for k, (src, dst) in enumerate(
            ((pw_h, pw), (ng_h, ng), (nb_h, nb), (gw_h, gw), (og_h, og), (ob_h, ob), (ow_h, ow))
        )
    ]
    load(0).start()
    for copy in params:
        copy.start()
    for g in range(1, ROWS // GROUP):
        load(g).start()

    barrier = pltpu.get_barrier_semaphore()

    def greet(s, carry):
        pl.semaphore_signal(
            barrier, inc=1, device_id=target(s, row, col), device_id_type=pl.DeviceIdType.MESH
        )
        return carry

    lax.fori_loop(1, DEV, greet, 0)
    for copy in params:
        copy.wait()
    for u in range(2):
        for k in range(4):
            wt[u, k * CH : (k + 1) * CH] = pw[u, k].T
        gain_t[u] = jnp.broadcast_to(og[u : u + 1], (CH, CH)).T
        bias_t[u] = jnp.broadcast_to(ob[u : u + 1], (CH, CH)).T

    def front_group(u, g):
        base = g * GROUP
        for i in range(0, GROUP, 2):
            x = cur[u, pl.ds(base + i, 2)].reshape(2 * COLS, CH).astype(F32)
            n = layer_norm(x, ng[u : u + 1], nb[u : u + 1]).astype(BF16)
            normed[pl.ds(base + i, 2)] = n.reshape(2, COLS, CH)
            p = dot(wt[u], n, NT)
            lo = sigmoid(p[0:128]) * p[128:256]
            ro = sigmoid(p[256:384]) * p[384:512]
            for k in range(2):
                part = slice(k * COLS, (k + 1) * COLS)
                tl[pl.ds(i + k, CH, stride=GROUP), :] = lo[:, part]
                tr[pl.ds(i + k, CH, stride=GROUP), :] = ro[:, part]
        rows = pl.ds(pl.multiple_of(base, GROUP), GROUP)
        left[u, :, rows, :] = tl[...].reshape(CH, GROUP, COLS).astype(BF16)
        right[u, :, rows, :] = tr[...].reshape(CH, GROUP, COLS).astype(BF16)

    def gate_rows(u, step):
        n = normed[pl.ds(step * 4, 4)].reshape(4 * COLS, CH)
        gate[pl.ds(step * 4, 4)] = sigmoid(dot(n, gw[u], NN)).reshape(4, COLS, CH)

    def back_group(u, g):
        base = g * GROUP
        m = m_in[u, :, pl.ds(pl.multiple_of(base, GROUP), GROUP), :].astype(F32)
        mean = jnp.mean(m, axis=0)
        centred = m - mean[None]
        var = jnp.mean(centred * centred, axis=0)
        ts[...] = lax.rsqrt(var + 1e-5)
        tl[...] = centred.reshape(CH * GROUP, COLS)
        for i in range(GROUP):
            c = tl[pl.ds(i, CH, stride=GROUP), :]
            nm = (c * ts[pl.ds(i, 1), :] * gain_t[u] + bias_t[u]).astype(BF16)
            change = dot(nm, ow[u], TN)
            now = cur[u, base + i].astype(F32) + gate[base + i] * change
            cur[1 - u, base + i] = now.astype(BF16)

    def loop(count, body):
        def step(i, carry):
            body(i)
            return carry

        lax.fori_loop(0, count, step, 0)

    def spread(u, k, half):
        part = pl.ds(half * HALF, HALF)
        flight = (u * 3 + k) * 2 + half
        if k == MIXED:
            src_at = lambda r, c: m_all.at[u, c, r, part]
            dst = m_in.at[u, me, part]
        else:
            src, all_ = ((right, r_all), (left, l_all))[k]
            src_at = lambda r, c: src.at[u, r * N_COL + c, part]
            dst = all_.at[u, col, row, part]
        pltpu.make_async_copy(src_at(row, col), dst, recv_sem.at[flight]).start()

        def send(s, carry):
            r, c = target(s, row, col)
            pltpu.make_async_remote_copy(
                src_ref=src_at(r, c),
                dst_ref=dst,
                send_sem=send_sem.at[flight],
                recv_sem=recv_sem.at[flight],
                device_id=(r, c),
                device_id_type=pl.DeviceIdType.MESH,
            ).start()
            return carry

        lax.fori_loop(1, DEV, send, 0)

    def arrived(u, k, half):
        size = m_in.at[u, pl.ds(0, DEV // 2)]
        pltpu.make_async_copy(size, size, recv_sem.at[(u * 3 + k) * 2 + half]).wait()

    def sent(u, k, half):
        flight = (u * 3 + k) * 2 + half
        size = m_in.at[u, pl.ds(0, DEV // 2 - 1)]
        pltpu.make_async_copy(size, size, send_sem.at[flight]).wait()
        size = m_in.at[u, 0, pl.ds(0, HALF)]
        pltpu.make_async_copy(size, size, send_sem.at[flight]).wait()

    def put_mixed(u, half, jb, out):
        out = out.astype(BF16)
        for k in range(2):
            m_all[u, 2 * jb + k, :, pl.ds(half * HALF, HALF), :] = out[
                :, k * COLS : (k + 1) * COLS
            ].reshape(N_ROW, HALF, COLS)

    def mix_outgoing(half):
        a = jnp.concatenate(
            [
                l_all[0, c, :, half * HALF : (half + 1) * HALF, :].reshape(512, COLS)
                for c in range(N_COL)
            ],
            axis=1,
        )

        def block(jb):
            b = jnp.concatenate(
                [r_all[0, c, pl.ds(4 * jb, 4)].reshape(256, COLS) for c in range(N_COL)], axis=1
            )
            put_mixed(0, half, jb, dot(a, b, NT))

        loop(4, block)

    def turn(half):
        def block(c):
            part = l_all[1, c, :, half * HALF : (half + 1) * HALF, :].reshape(512, COLS)
            lt[half, pl.ds(2 * c, 2)] = part.T.reshape(2, ROWS, 512)

        loop(N_COL, block)

    def mix_incoming(half):
        rows = slice(half * HALF, (half + 1) * HALF)
        a = jnp.concatenate([lt[k, :, rows, :].reshape(512, 512) for k in range(2)], axis=1)

        def block(jb):
            b = jnp.concatenate(
                [
                    jnp.concatenate(
                        [
                            r_all[1, 2 * jb + c, :, k * HALF : (k + 1) * HALF, :].reshape(512, COLS)
                            for k in range(2)
                        ],
                        axis=0,
                    )
                    for c in range(2)
                ],
                axis=1,
            )
            put_mixed(1, half, jb, dot(a, b, NN))

        loop(4, block)

    for half in range(2):
        for g in range(2):
            load(2 * half + g).wait()
        loop(2, lambda g: front_group(0, 2 * half + g))
        if half == 0:
            pl.semaphore_wait(barrier, DEV - 1)
            spread(0, RIGHT, 0)
    spread(0, RIGHT, 1)
    spread(0, LEFT, 0)
    spread(0, LEFT, 1)
    loop(ROWS // 4, lambda s: gate_rows(0, s))
    arrived(0, RIGHT, 0)
    arrived(0, RIGHT, 1)
    for half in range(2):
        arrived(0, LEFT, half)
        mix_outgoing(half)
        spread(0, MIXED, half)
    for half in range(2):
        arrived(0, MIXED, half)

        def turnover(g):
            back_group(0, 2 * half + g)
            front_group(1, 2 * half + g)

        loop(2, turnover)
        for k in (RIGHT, LEFT) if half == 0 else (LEFT, RIGHT):
            spread(1, k, half)
    loop(ROWS // 4, lambda s: gate_rows(1, s))
    for half in range(2):
        arrived(1, LEFT, half)
        turn(half)
    for half in range(2):
        arrived(1, RIGHT, half)
    for half in range(2):
        mix_incoming(half)
        spread(1, MIXED, half)

    def store(half):
        rows = pl.ds(half * HALF, HALF)
        return pltpu.make_async_copy(cur.at[0, rows], out_h.at[rows], out_sem.at[half])

    for half in range(2):
        arrived(1, MIXED, half)
        loop(2, lambda g: back_group(1, 2 * half + g))
        store(half).start()
    for u in range(2):
        for k in range(3):
            for half in range(2):
                sent(u, k, half)
    for half in range(2):
        store(half).wait()


def hand_over(src, dst):
    dst[...] = src[...]


def shards(*args):
    pieces = (2, DEV, ROWS, COLS)
    planes = (2, N_COL, N_ROW, ROWS, COLS)
    vmem = pltpu.VMEM
    scratch = [
        vmem((2, ROWS, COLS, CH), BF16),
        vmem((ROWS, COLS, CH), BF16),
        vmem((ROWS, COLS, CH), F32),
        vmem(pieces, BF16),
        vmem(pieces, BF16),
        vmem(planes, BF16),
        vmem(planes, BF16),
        vmem((2, N_ROW, ROWS, 512), BF16),
        vmem(planes, BF16),
        vmem(pieces, BF16),
    ]
    scratch += [vmem(a.shape, a.dtype) for a in args[1:]]
    scratch += [
        vmem((2, 4 * CH, CH), BF16),
        vmem((2, CH, CH), F32),
        vmem((2, CH, CH), F32),
        vmem((CH * GROUP, COLS), F32),
        vmem((CH * GROUP, COLS), F32),
        vmem((GROUP, COLS), F32),
        pltpu.SemaphoreType.DMA((ROWS // GROUP,)),
        pltpu.SemaphoreType.DMA((7,)),
        pltpu.SemaphoreType.DMA((12,)),
        pltpu.SemaphoreType.DMA((12,)),
        pltpu.SemaphoreType.DMA((2,)),
    ]
    updated = pl.pallas_call(
        kernel,
        out_shape=jax.ShapeDtypeStruct((ROWS, COLS, CH), BF16),
        in_specs=[pl.BlockSpec(memory_space=pl.ANY)] * 8,
        out_specs=pl.BlockSpec(memory_space=pl.ANY),
        scratch_shapes=scratch,
        compiler_params=pltpu.CompilerParams(
            collective_id=0, has_side_effects=True, vmem_limit_bytes=60 * MIB
        ),
        name="triangle",
    )(*args)
    tile = pl.BlockSpec((GROUP, COLS, CH), lambda g: (g, 0, 0))
    return pl.pallas_call(
        hand_over,
        grid=(ROWS // GROUP,),
        out_shape=jax.ShapeDtypeStruct((ROWS, COLS, CH), BF16),
        in_specs=[tile],
        out_specs=tile,
        name="hand_over",
    )(updated)


def solution(mesh):
    placed = (P("row", "col", None), P(), P(), P(), P(), P(), P(), P())
    return jax.shard_map(
        shards, mesh=mesh, in_specs=placed, out_specs=P("row", "col", None), check_vma=False
    )
```

```python
import jax
import jax.numpy as jnp
from jax import lax
from jax.experimental import pallas as pl
from jax.experimental.pallas import tpu as pltpu
from jax.sharding import PartitionSpec as P

F32, BF16 = jnp.float32, jnp.bfloat16
ROWS, COLS, N_ROW, N_COL, CH = 64, 128, 16, 8, 128
DEV = N_ROW * N_COL
GROUP, HALF = 16, 32
MIB = 1 << 20
NT = (((1,), (1,)), ((), ()))
TN = (((0,), (0,)), ((), ()))
NN = (((1,), (0,)), ((), ()))
RIGHT, LEFT, MIXED = 0, 1, 2


def sigmoid(v):
    return 0.5 * jnp.tanh(0.5 * v) + 0.5


def layer_norm(v, gain, bias):
    mean = jnp.mean(v, axis=-1, keepdims=True)
    centred = v - mean
    var = jnp.mean(centred * centred, axis=-1, keepdims=True)
    return centred * lax.rsqrt(var + 1e-5) * gain + bias


def dot(a, b, dims):
    return lax.dot_general(a, b, dims, preferred_element_type=F32)


def target(s, row, col):
    core, a, b, c = s // 64, lax.rem(s, 4), lax.rem(s // 4, 4), lax.rem(s // 16, 4)
    y, zh, k = row // 4, lax.rem(row // 2, 2), lax.rem(row, 2)
    x, zl = col // 2, lax.rem(col, 2)
    sign = 1 - 2 * k
    x = lax.rem(x + sign * (3 * a + b + 2 * c) + 32, 4)
    y = lax.rem(y + sign * (2 * a + b + 3 * c) + 32, 4)
    z = lax.rem(zh * 2 + zl + sign * (2 * a + 3 * b) + 32, 4)
    row = y * 4 + (z // 2) * 2 + lax.rem(k + core, 2)
    col = x * 2 + lax.rem(z, 2)
    return row, col


def kernel(
    pair_h, ng_h, nb_h, pw_h, gw_h, og_h, ob_h, ow_h, out_h,
    cur, normed, gate, left, right, l_all, r_all, lt, acc, m_all, m_in,
    ng, nb, pw, gw, og, ob, ow, wt, gain_t, bias_t, tl, tr, ts,
    load_sem, param_sem, send_sem, recv_sem, out_sem,
):
    row, col = lax.axis_index("row"), lax.axis_index("col")
    me = row * N_COL + col

    def load(g):
        rows = pl.ds(g * GROUP, GROUP)
        return pltpu.make_async_copy(pair_h.at[rows], cur.at[0, rows], load_sem.at[g])

    params = [
        pltpu.make_async_copy(src, dst, param_sem.at[k])
        for k, (src, dst) in enumerate(
            ((pw_h, pw), (ng_h, ng), (nb_h, nb), (gw_h, gw), (og_h, og), (ob_h, ob), (ow_h, ow))
        )
    ]
    load(0).start()
    for copy in params:
        copy.start()
    for g in range(1, ROWS // GROUP):
        load(g).start()

    barrier = pltpu.get_barrier_semaphore()

    def greet(s, carry):
        pl.semaphore_signal(
            barrier, inc=1, device_id=target(s, row, col), device_id_type=pl.DeviceIdType.MESH
        )
        return carry

    lax.fori_loop(1, DEV, greet, 0)
    for copy in params:
        copy.wait()
    for k in range(4):
        wt[0, k * CH : (k + 1) * CH] = pw[0, k].T

    def norm_rows(u, base):
        x = cur[u, pl.ds(base, 2)].reshape(2 * COLS, CH).astype(F32)
        n = layer_norm(x, ng[u : u + 1], nb[u : u + 1]).astype(BF16)
        normed[pl.ds(base, 2)] = n.reshape(2, COLS, CH)
        return n

    def project(u, k, n, i):
        first = 256 * (1 - k)
        p = dot(wt[u, first : first + 256], n, NT)
        side = sigmoid(p[0:128]) * p[128:256]
        wide = (tr, tl)[k]
        for r in range(2):
            wide[pl.ds(i + r, CH, stride=GROUP), :] = side[:, r * COLS : (r + 1) * COLS]

    def keep(u, k, g):
        rows = pl.ds(pl.multiple_of(g * GROUP, GROUP), GROUP)
        side, wide = ((right, tr), (left, tl))[k]
        side[u, :, rows, :] = wide[...].reshape(CH, GROUP, COLS).astype(BF16)

    def front_group(u, g, sides=(RIGHT, LEFT), fresh=True):
        base = g * GROUP
        for i in range(0, GROUP, 2):
            if fresh:
                n = norm_rows(u, base + i)
            else:
                n = normed[pl.ds(base + i, 2)].reshape(2 * COLS, CH)
            for k in sides:
                project(u, k, n, i)
        for k in sides:
            keep(u, k, g)

    def gate_rows(u, step):
        n = normed[pl.ds(step * 4, 4)].reshape(4 * COLS, CH)
        gate[pl.ds(step * 4, 4)] = sigmoid(dot(n, gw[u], NN)).reshape(4, COLS, CH)

    def back_group(u, g):
        base = g * GROUP
        m = m_in[u, :, pl.ds(pl.multiple_of(base, GROUP), GROUP), :].astype(F32)
        mean = jnp.mean(m, axis=0)
        centred = m - mean[None]
        var = jnp.mean(centred * centred, axis=0)
        ts[...] = lax.rsqrt(var + 1e-5)
        tl[...] = centred.reshape(CH * GROUP, COLS)
        for i in range(GROUP):
            c = tl[pl.ds(i, CH, stride=GROUP), :]
            nm = (c * ts[pl.ds(i, 1), :] * gain_t[u] + bias_t[u]).astype(BF16)
            change = dot(nm, ow[u], TN)
            now = cur[u, base + i].astype(F32) + gate[base + i] * change
            cur[1 - u, base + i] = now.astype(BF16)

    def loop(count, body):
        def step(i, carry):
            body(i)
            return carry

        lax.fori_loop(0, count, step, 0)

    def spread(u, k, half):
        part = pl.ds(half * HALF, HALF)
        flight = (u * 3 + k) * 2 + half
        if k == MIXED:
            src_at = lambda r, c: m_all.at[u, c, r, part]
            dst = m_in.at[u, me, part]
        else:
            src, all_ = ((right, r_all), (left, l_all))[k]
            src_at = lambda r, c: src.at[u, r * N_COL + c, part]
            dst = all_.at[u, col, row, part]
        pltpu.make_async_copy(src_at(row, col), dst, recv_sem.at[flight]).start()

        def send(s, carry):
            r, c = target(s, row, col)
            pltpu.make_async_remote_copy(
                src_ref=src_at(r, c),
                dst_ref=dst,
                send_sem=send_sem.at[flight],
                recv_sem=recv_sem.at[flight],
                device_id=(r, c),
                device_id_type=pl.DeviceIdType.MESH,
            ).start()
            return carry

        lax.fori_loop(1, DEV, send, 0)

    def arrived(u, k, half):
        size = m_in.at[u, pl.ds(0, DEV // 2)]
        pltpu.make_async_copy(size, size, recv_sem.at[(u * 3 + k) * 2 + half]).wait()

    def sent(u, k, half):
        flight = (u * 3 + k) * 2 + half
        size = m_in.at[u, pl.ds(0, DEV // 2 - 1)]
        pltpu.make_async_copy(size, size, send_sem.at[flight]).wait()
        size = m_in.at[u, 0, pl.ds(0, HALF)]
        pltpu.make_async_copy(size, size, send_sem.at[flight]).wait()

    def put_mixed(u, half, jb, out):
        out = out.astype(BF16)
        for k in range(2):
            m_all[u, 2 * jb + k, :, pl.ds(half * HALF, HALF), :] = out[
                :, k * COLS : (k + 1) * COLS
            ].reshape(N_ROW, HALF, COLS)

    def mix_outgoing(half):
        a = jnp.concatenate(
            [
                l_all[0, c, :, half * HALF : (half + 1) * HALF, :].reshape(512, COLS)
                for c in range(N_COL)
            ],
            axis=1,
        )

        def block(jb):
            b = jnp.concatenate(
                [r_all[0, c, pl.ds(4 * jb, 4)].reshape(256, COLS) for c in range(N_COL)], axis=1
            )
            put_mixed(0, half, jb, dot(a, b, NT))

        loop(4, block)

    def turn(half):
        def block(c):
            part = l_all[1, c, :, half * HALF : (half + 1) * HALF, :].reshape(512, COLS)
            lt[half, pl.ds(2 * c, 2)] = part.T.reshape(2, ROWS, 512)

        loop(N_COL, block)

    def mix_incoming(half, k):
        a = lt[k, :, half * HALF : (half + 1) * HALF, :].reshape(512, 512)

        def block(jb):
            b = jnp.concatenate(
                [
                    r_all[1, 2 * jb + c, :, k * HALF : (k + 1) * HALF, :].reshape(512, COLS)
                    for c in range(2)
                ],
                axis=1,
            )
            if k == 0:
                acc[half, jb] = dot(a, b, NN)
            else:
                put_mixed(1, half, jb, acc[half, jb] + dot(a, b, NN))

        loop(4, block)

    for g in range(2):
        load(g).wait()
    loop(2, lambda g: front_group(0, g, (RIGHT,)))
    pl.semaphore_wait(barrier, DEV - 1)
    spread(0, RIGHT, 0)
    for g in range(2, 4):
        load(g).wait()
    loop(2, lambda g: front_group(0, 2 + g))
    spread(0, RIGHT, 1)
    loop(2, lambda g: front_group(0, g, (LEFT,), False))
    spread(0, LEFT, 0)
    spread(0, LEFT, 1)
    for k in range(4):
        wt[1, k * CH : (k + 1) * CH] = pw[1, k].T
    for u in range(2):
        gain_t[u] = jnp.broadcast_to(og[u : u + 1], (CH, CH)).T
        bias_t[u] = jnp.broadcast_to(ob[u : u + 1], (CH, CH)).T
    loop(ROWS // 4, lambda s: gate_rows(0, s))
    arrived(0, RIGHT, 0)
    arrived(0, RIGHT, 1)
    for half in range(2):
        arrived(0, LEFT, half)
        mix_outgoing(half)
        spread(0, MIXED, half)
    for half in range(2):
        arrived(0, MIXED, half)

        def turnover(g):
            back_group(0, 2 * half + g)
            front_group(1, 2 * half + g)

        loop(2, turnover)
        for k in (RIGHT, LEFT) if half == 0 else (LEFT, RIGHT):
            spread(1, k, half)
    loop(ROWS // 4, lambda s: gate_rows(1, s))
    arrived(1, RIGHT, 0)
    arrived(1, LEFT, 0)
    turn(0)
    for half in range(2):
        mix_incoming(half, 0)
    arrived(1, LEFT, 1)
    turn(1)
    arrived(1, RIGHT, 1)
    for half in range(2):
        mix_incoming(half, 1)
        spread(1, MIXED, half)

    def store(half):
        rows = pl.ds(half * HALF, HALF)
        return pltpu.make_async_copy(cur.at[0, rows], out_h.at[rows], out_sem.at[half])

    for half in range(2):
        arrived(1, MIXED, half)
        loop(2, lambda g: back_group(1, 2 * half + g))
        store(half).start()
    for u in range(2):
        for k in range(3):
            for half in range(2):
                sent(u, k, half)
    for half in range(2):
        store(half).wait()


def hand_over(src, dst, sem):
    copies = [
        pltpu.make_async_copy(src.at[pl.ds(8 * k, 8)], dst.at[pl.ds(8 * k, 8)], sem.at[k])
        for k in range(8)
    ]
    for copy in copies:
        copy.start()
    for copy in copies:
        copy.wait()


def shards(*args):
    pieces = (2, DEV, ROWS, COLS)
    planes = (2, N_COL, N_ROW, ROWS, COLS)
    vmem = pltpu.VMEM
    scratch = [
        vmem((2, ROWS, COLS, CH), BF16),
        vmem((ROWS, COLS, CH), BF16),
        vmem((ROWS, COLS, CH), F32),
        vmem(pieces, BF16),
        vmem(pieces, BF16),
        vmem(planes, BF16),
        vmem(planes, BF16),
        vmem((2, N_ROW, ROWS, 512), BF16),
        vmem((2, 4, 512, 256), F32),
        vmem(planes, BF16),
        vmem(pieces, BF16),
    ]
    scratch += [vmem(a.shape, a.dtype) for a in args[1:]]
    scratch += [
        vmem((2, 4 * CH, CH), BF16),
        vmem((2, CH, CH), F32),
        vmem((2, CH, CH), F32),
        vmem((CH * GROUP, COLS), F32),
        vmem((CH * GROUP, COLS), F32),
        vmem((GROUP, COLS), F32),
        pltpu.SemaphoreType.DMA((ROWS // GROUP,)),
        pltpu.SemaphoreType.DMA((7,)),
        pltpu.SemaphoreType.DMA((12,)),
        pltpu.SemaphoreType.DMA((12,)),
        pltpu.SemaphoreType.DMA((2,)),
    ]
    updated = pl.pallas_call(
        kernel,
        out_shape=jax.ShapeDtypeStruct((ROWS, COLS, CH), BF16),
        in_specs=[pl.BlockSpec(memory_space=pl.ANY)] * 8,
        out_specs=pl.BlockSpec(memory_space=pl.ANY),
        scratch_shapes=scratch,
        compiler_params=pltpu.CompilerParams(
            collective_id=0, has_side_effects=True, vmem_limit_bytes=60 * MIB
        ),
        name="triangle",
    )(*args)
    return pl.pallas_call(
        hand_over,
        out_shape=jax.ShapeDtypeStruct((ROWS, COLS, CH), BF16),
        in_specs=[pl.BlockSpec(memory_space=pl.ANY)],
        out_specs=pl.BlockSpec(memory_space=pl.ANY),
        scratch_shapes=[pltpu.SemaphoreType.DMA((8,))],
        compiler_params=pltpu.CompilerParams(vmem_limit_bytes=60 * MIB),
        name="hand_over",
    )(updated)


def solution(mesh):
    placed = (P("row", "col", None), P(), P(), P(), P(), P(), P(), P())
    return jax.shard_map(
        shards, mesh=mesh, in_specs=placed, out_specs=P("row", "col", None), check_vma=False
    )
```

```python
import jax
import jax.numpy as jnp
from jax import lax
from jax.experimental import pallas as pl
from jax.experimental.pallas import tpu as pltpu
from jax.sharding import PartitionSpec as P

F32, BF16 = jnp.float32, jnp.bfloat16
ROWS, COLS, N_ROW, N_COL, CH = 64, 128, 16, 8, 128
DEV = N_ROW * N_COL
GROUP, HALF = 16, 32
MIB = 1 << 20
NT = (((1,), (1,)), ((), ()))
TN = (((0,), (0,)), ((), ()))
NN = (((1,), (0,)), ((), ()))
RIGHT, LEFT, MIXED = 0, 1, 2


def sigmoid(v):
    return 0.5 * jnp.tanh(0.5 * v) + 0.5


def layer_norm(v, gain, bias):
    mean = jnp.mean(v, axis=-1, keepdims=True)
    centred = v - mean
    var = jnp.mean(centred * centred, axis=-1, keepdims=True)
    return centred * lax.rsqrt(var + 1e-5) * gain + bias


def dot(a, b, dims):
    return lax.dot_general(a, b, dims, preferred_element_type=F32)


def target(s, row, col):
    core, a, b, c = s // 64, lax.rem(s, 4), lax.rem(s // 4, 4), lax.rem(s // 16, 4)
    y, zh, k = row // 4, lax.rem(row // 2, 2), lax.rem(row, 2)
    x, zl = col // 2, lax.rem(col, 2)
    sign = 1 - 2 * k
    x = lax.rem(x + sign * a + 16, 4)
    y = lax.rem(y + sign * (a + b) + 16, 4)
    z = lax.rem(zh * 2 + zl + sign * (a + b + c) + 16, 4)
    row = y * 4 + (z // 2) * 2 + lax.rem(k + core, 2)
    col = x * 2 + lax.rem(z, 2)
    return row, col


def kernel(
    pair_h, ng_h, nb_h, pw_h, gw_h, og_h, ob_h, ow_h, out_h,
    cur, normed, gate, left, right, l_all, r_all, lt, acc, m_all, m_in,
    ng, nb, pw, gw, og, ob, ow, wt, gain_t, bias_t, tl, tr, ts,
    load_sem, param_sem, send_sem, recv_sem, out_sem,
):
    row, col = lax.axis_index("row"), lax.axis_index("col")
    me = row * N_COL + col

    def load(g):
        rows = pl.ds(g * GROUP, GROUP)
        return pltpu.make_async_copy(pair_h.at[rows], cur.at[0, rows], load_sem.at[g])

    params = [
        pltpu.make_async_copy(src, dst, param_sem.at[k])
        for k, (src, dst) in enumerate(
            ((pw_h, pw), (ng_h, ng), (nb_h, nb), (gw_h, gw), (og_h, og), (ob_h, ob), (ow_h, ow))
        )
    ]
    load(0).start()
    for copy in params:
        copy.start()
    for g in range(1, ROWS // GROUP):
        load(g).start()

    barrier = pltpu.get_barrier_semaphore()

    def greet(s, carry):
        pl.semaphore_signal(
            barrier, inc=1, device_id=target(s, row, col), device_id_type=pl.DeviceIdType.MESH
        )
        return carry

    lax.fori_loop(1, DEV, greet, 0)
    for copy in params:
        copy.wait()
    for k in range(4):
        wt[0, k * CH : (k + 1) * CH] = pw[0, k].T

    def norm_rows(u, base):
        x = cur[u, pl.ds(base, 2)].reshape(2 * COLS, CH).astype(F32)
        n = layer_norm(x, ng[u : u + 1], nb[u : u + 1]).astype(BF16)
        normed[pl.ds(base, 2)] = n.reshape(2, COLS, CH)
        return n

    def project(u, k, n, i):
        first = 256 * (1 - k)
        p = dot(wt[u, first : first + 256], n, NT)
        side = sigmoid(p[0:128]) * p[128:256]
        wide = (tr, tl)[k]
        for r in range(2):
            wide[pl.ds(i + r, CH, stride=GROUP), :] = side[:, r * COLS : (r + 1) * COLS]

    def keep(u, k, g):
        rows = pl.ds(pl.multiple_of(g * GROUP, GROUP), GROUP)
        side, wide = ((right, tr), (left, tl))[k]
        side[u, :, rows, :] = wide[...].reshape(CH, GROUP, COLS).astype(BF16)

    def front_group(u, g, sides=(RIGHT, LEFT), fresh=True):
        base = g * GROUP
        for i in range(0, GROUP, 2):
            if fresh:
                n = norm_rows(u, base + i)
            else:
                n = normed[pl.ds(base + i, 2)].reshape(2 * COLS, CH)
            for k in sides:
                project(u, k, n, i)
        for k in sides:
            keep(u, k, g)

    def gate_rows(u, step):
        n = normed[pl.ds(step * 4, 4)].reshape(4 * COLS, CH)
        gate[pl.ds(step * 4, 4)] = sigmoid(dot(n, gw[u], NN)).reshape(4, COLS, CH)

    def back_group(u, g):
        base = g * GROUP
        m = m_in[u, :, pl.ds(pl.multiple_of(base, GROUP), GROUP), :].astype(F32)
        mean = jnp.mean(m, axis=0)
        centred = m - mean[None]
        var = jnp.mean(centred * centred, axis=0)
        ts[...] = lax.rsqrt(var + 1e-5)
        tl[...] = centred.reshape(CH * GROUP, COLS)
        for i in range(GROUP):
            c = tl[pl.ds(i, CH, stride=GROUP), :]
            nm = (c * ts[pl.ds(i, 1), :] * gain_t[u] + bias_t[u]).astype(BF16)
            change = dot(nm, ow[u], TN)
            now = cur[u, base + i].astype(F32) + gate[base + i] * change
            cur[1 - u, base + i] = now.astype(BF16)

    def loop(count, body):
        def step(i, carry):
            body(i)
            return carry

        lax.fori_loop(0, count, step, 0)

    def spread(u, k, half):
        part = pl.ds(half * HALF, HALF)
        flight = (u * 3 + k) * 2 + half
        if k == MIXED:
            src_at = lambda r, c: m_all.at[u, c, r, part]
            dst = m_in.at[u, me, part]
        else:
            src, all_ = ((right, r_all), (left, l_all))[k]
            src_at = lambda r, c: src.at[u, r * N_COL + c, part]
            dst = all_.at[u, col, row, part]
        pltpu.make_async_copy(src_at(row, col), dst, recv_sem.at[flight]).start()

        def send(s, carry):
            r, c = target(s, row, col)
            pltpu.make_async_remote_copy(
                src_ref=src_at(r, c),
                dst_ref=dst,
                send_sem=send_sem.at[flight],
                recv_sem=recv_sem.at[flight],
                device_id=(r, c),
                device_id_type=pl.DeviceIdType.MESH,
            ).start()
            return carry

        lax.fori_loop(1, DEV, send, 0)

    def arrived(u, k, half):
        size = m_in.at[u, pl.ds(0, DEV // 2)]
        pltpu.make_async_copy(size, size, recv_sem.at[(u * 3 + k) * 2 + half]).wait()

    def sent(u, k, half):
        flight = (u * 3 + k) * 2 + half
        size = m_in.at[u, pl.ds(0, DEV // 2 - 1)]
        pltpu.make_async_copy(size, size, send_sem.at[flight]).wait()
        size = m_in.at[u, 0, pl.ds(0, HALF)]
        pltpu.make_async_copy(size, size, send_sem.at[flight]).wait()

    def put_mixed(u, half, jb, out):
        out = out.astype(BF16)
        for k in range(2):
            m_all[u, 2 * jb + k, :, pl.ds(half * HALF, HALF), :] = out[
                :, k * COLS : (k + 1) * COLS
            ].reshape(N_ROW, HALF, COLS)

    def mix_outgoing(half):
        a = jnp.concatenate(
            [
                l_all[0, c, :, half * HALF : (half + 1) * HALF, :].reshape(512, COLS)
                for c in range(N_COL)
            ],
            axis=1,
        )

        def block(jb):
            b = jnp.concatenate(
                [r_all[0, c, pl.ds(4 * jb, 4)].reshape(256, COLS) for c in range(N_COL)], axis=1
            )
            put_mixed(0, half, jb, dot(a, b, NT))

        loop(4, block)

    def turn(half):
        def block(c):
            part = l_all[1, c, :, half * HALF : (half + 1) * HALF, :].reshape(512, COLS)
            lt[half, pl.ds(2 * c, 2)] = part.T.reshape(2, ROWS, 512)

        loop(N_COL, block)

    def mix_incoming(half, k):
        a = lt[k, :, half * HALF : (half + 1) * HALF, :].reshape(512, 512)

        def block(jb):
            b = jnp.concatenate(
                [
                    r_all[1, 2 * jb + c, :, k * HALF : (k + 1) * HALF, :].reshape(512, COLS)
                    for c in range(2)
                ],
                axis=1,
            )
            if k == 0:
                acc[half, jb] = dot(a, b, NN)
            else:
                put_mixed(1, half, jb, acc[half, jb] + dot(a, b, NN))

        loop(4, block)

    for g in range(2):
        load(g).wait()
    loop(2, lambda g: front_group(0, g, (RIGHT,)))
    pl.semaphore_wait(barrier, DEV - 1)
    spread(0, RIGHT, 0)
    for g in range(2, 4):
        load(g).wait()
    loop(2, lambda g: front_group(0, 2 + g))
    spread(0, RIGHT, 1)
    loop(2, lambda g: front_group(0, g, (LEFT,), False))
    spread(0, LEFT, 0)
    spread(0, LEFT, 1)
    for k in range(4):
        wt[1, k * CH : (k + 1) * CH] = pw[1, k].T
    for u in range(2):
        gain_t[u] = jnp.broadcast_to(og[u : u + 1], (CH, CH)).T
        bias_t[u] = jnp.broadcast_to(ob[u : u + 1], (CH, CH)).T
    loop(ROWS // 4, lambda s: gate_rows(0, s))
    arrived(0, RIGHT, 0)
    arrived(0, RIGHT, 1)
    for half in range(2):
        arrived(0, LEFT, half)
        mix_outgoing(half)
        spread(0, MIXED, half)
    for half in range(2):
        arrived(0, MIXED, half)

        def turnover(g):
            back_group(0, 2 * half + g)
            front_group(1, 2 * half + g)

        loop(2, turnover)
        for k in (RIGHT, LEFT) if half == 0 else (LEFT, RIGHT):
            spread(1, k, half)
    loop(ROWS // 4, lambda s: gate_rows(1, s))
    arrived(1, RIGHT, 0)
    arrived(1, LEFT, 0)
    turn(0)
    for half in range(2):
        mix_incoming(half, 0)
    arrived(1, LEFT, 1)
    turn(1)
    arrived(1, RIGHT, 1)
    for half in range(2):
        mix_incoming(half, 1)
        spread(1, MIXED, half)

    def store(half):
        rows = pl.ds(half * HALF, HALF)
        return pltpu.make_async_copy(cur.at[0, rows], out_h.at[rows], out_sem.at[half])

    for half in range(2):
        arrived(1, MIXED, half)
        loop(2, lambda g: back_group(1, 2 * half + g))
        store(half).start()
    for u in range(2):
        for k in range(3):
            for half in range(2):
                sent(u, k, half)
    for half in range(2):
        store(half).wait()


def shards(*args):
    pieces = (2, DEV, ROWS, COLS)
    planes = (2, N_COL, N_ROW, ROWS, COLS)
    vmem = pltpu.VMEM
    scratch = [
        vmem((2, ROWS, COLS, CH), BF16),
        vmem((ROWS, COLS, CH), BF16),
        vmem((ROWS, COLS, CH), F32),
        vmem(pieces, BF16),
        vmem(pieces, BF16),
        vmem(planes, BF16),
        vmem(planes, BF16),
        vmem((2, N_ROW, ROWS, 512), BF16),
        vmem((2, 4, 512, 256), F32),
        vmem(planes, BF16),
        vmem(pieces, BF16),
    ]
    scratch += [vmem(a.shape, a.dtype) for a in args[1:]]
    scratch += [
        vmem((2, 4 * CH, CH), BF16),
        vmem((2, CH, CH), F32),
        vmem((2, CH, CH), F32),
        vmem((CH * GROUP, COLS), F32),
        vmem((CH * GROUP, COLS), F32),
        vmem((GROUP, COLS), F32),
        pltpu.SemaphoreType.DMA((ROWS // GROUP,)),
        pltpu.SemaphoreType.DMA((7,)),
        pltpu.SemaphoreType.DMA((12,)),
        pltpu.SemaphoreType.DMA((12,)),
        pltpu.SemaphoreType.DMA((2,)),
    ]
    return pl.pallas_call(
        kernel,
        out_shape=jax.ShapeDtypeStruct((ROWS, COLS, CH), BF16),
        in_specs=[pl.BlockSpec(memory_space=pl.ANY)] * 8,
        out_specs=pl.BlockSpec(memory_space=pl.ANY),
        scratch_shapes=scratch,
        compiler_params=pltpu.CompilerParams(
            collective_id=0, has_side_effects=True, vmem_limit_bytes=60 * MIB
        ),
        name="triangle",
    )(*args)


def solution(mesh):
    placed = (P("row", "col", None), P(), P(), P(), P(), P(), P(), P())
    return jax.shard_map(
        shards, mesh=mesh, in_specs=placed, out_specs=P("row", "col", None), check_vma=False
    )
```

```python
import jax
import jax.numpy as jnp
from jax import lax
from jax.experimental import pallas as pl
from jax.experimental.pallas import tpu as pltpu
from jax.sharding import PartitionSpec as P

F32, BF16 = jnp.float32, jnp.bfloat16
ROWS, COLS, N_ROW, N_COL, CH = 64, 128, 16, 8, 128
DEV = N_ROW * N_COL
GROUP, HALF = 16, 32
MIB = 1 << 20
NT = (((1,), (1,)), ((), ()))
TN = (((0,), (0,)), ((), ()))
NN = (((1,), (0,)), ((), ()))
RIGHT, LEFT, MIXED = 0, 1, 2


def sigmoid(v):
    return 0.5 * jnp.tanh(0.5 * v) + 0.5


def layer_norm(v, gain, bias):
    mean = jnp.mean(v, axis=-1, keepdims=True)
    centred = v - mean
    var = jnp.mean(centred * centred, axis=-1, keepdims=True)
    return centred * lax.rsqrt(var + 1e-5) * gain + bias


def dot(a, b, dims):
    return lax.dot_general(a, b, dims, preferred_element_type=F32)


def each_target(row, col, body):
    y, zh, k = row // 4, lax.rem(row // 2, 2), lax.rem(row, 2)
    x, zl = col // 2, lax.rem(col, 2)
    sign = 1 - 2 * k
    turns = [sign * a for a in range(5)]
    columns = [lax.rem(x + turns[a] + 4, 4) * 2 for a in range(4)]

    def eight(core, c, b, skip):
        core_at = lax.rem(k + core, 2)
        y_at = y + sign * b + 8
        z_at = zh * 2 + zl + sign * (b + c) + 16
        for later in range(2):
            for a in range(4):
                if skip and later == 0 and a == 0:
                    continue
                to_y = lax.rem(y_at + turns[a + later], 4)
                to_z = lax.rem(z_at + turns[a + later], 4)
                body(to_y * 4 + (to_z // 2) * 2 + core_at, columns[a] + lax.rem(to_z, 2))

    def step(p, carry):
        eight(p // 8, lax.rem(p // 2, 4), lax.rem(p, 2) * 2, False)
        return carry

    eight(0, 0, 0, True)
    lax.fori_loop(1, 16, step, 0)


def kernel(
    pair_h, ng_h, nb_h, pw_h, gw_h, og_h, ob_h, ow_h, out_h,
    cur, normed, gate, left, right, l_all, r_all, lt, acc, m_all, m_in,
    ng, nb, pw, gw, og, ob, ow, wt, gain_t, bias_t, tl, tr, ts,
    load_sem, param_sem, send_sem, recv_sem, out_sem,
):
    row, col = lax.axis_index("row"), lax.axis_index("col")
    me = row * N_COL + col

    def load(g):
        rows = pl.ds(g * GROUP, GROUP)
        return pltpu.make_async_copy(pair_h.at[rows], cur.at[0, rows], load_sem.at[g])

    params = [
        pltpu.make_async_copy(src, dst, param_sem.at[k])
        for k, (src, dst) in enumerate(
            ((pw_h, pw), (ng_h, ng), (nb_h, nb), (gw_h, gw), (og_h, og), (ob_h, ob), (ow_h, ow))
        )
    ]
    load(0).start()
    for copy in params:
        copy.start()
    for g in range(1, ROWS // GROUP):
        load(g).start()

    barrier = pltpu.get_barrier_semaphore()

    def greet(r, c):
        pl.semaphore_signal(
            barrier, inc=1, device_id=(r, c), device_id_type=pl.DeviceIdType.MESH
        )

    each_target(row, col, greet)
    for copy in params:
        copy.wait()
    for k in range(4):
        wt[0, k * CH : (k + 1) * CH] = pw[0, k].T

    def norm_rows(u, base):
        x = cur[u, pl.ds(base, 2)].reshape(2 * COLS, CH).astype(F32)
        n = layer_norm(x, ng[u : u + 1], nb[u : u + 1]).astype(BF16)
        normed[pl.ds(base, 2)] = n.reshape(2, COLS, CH)
        return n

    def project(u, k, n, i):
        first = 256 * (1 - k)
        p = dot(wt[u, first : first + 256], n, NT)
        side = sigmoid(p[0:128]) * p[128:256]
        wide = (tr, tl)[k]
        for r in range(2):
            wide[pl.ds(i + r, CH, stride=GROUP), :] = side[:, r * COLS : (r + 1) * COLS]

    def keep(u, k, g):
        rows = pl.ds(pl.multiple_of(g * GROUP, GROUP), GROUP)
        side, wide = ((right, tr), (left, tl))[k]
        side[u, :, rows, :] = wide[...].reshape(CH, GROUP, COLS).astype(BF16)

    def front_group(u, g, sides=(RIGHT, LEFT), fresh=True):
        base = g * GROUP
        for i in range(0, GROUP, 2):
            if fresh:
                n = norm_rows(u, base + i)
            else:
                n = normed[pl.ds(base + i, 2)].reshape(2 * COLS, CH)
            for k in sides:
                project(u, k, n, i)
        for k in sides:
            keep(u, k, g)

    def gate_rows(u, step):
        n = normed[pl.ds(step * 4, 4)].reshape(4 * COLS, CH)
        gate[pl.ds(step * 4, 4)] = sigmoid(dot(n, gw[u], NN)).reshape(4, COLS, CH)

    def back_group(u, g):
        base = g * GROUP
        m = m_in[u, :, pl.ds(pl.multiple_of(base, GROUP), GROUP), :].astype(F32)
        mean = jnp.mean(m, axis=0)
        centred = m - mean[None]
        var = jnp.mean(centred * centred, axis=0)
        ts[...] = lax.rsqrt(var + 1e-5)
        tl[...] = centred.reshape(CH * GROUP, COLS)
        for i in range(GROUP):
            c = tl[pl.ds(i, CH, stride=GROUP), :]
            nm = (c * ts[pl.ds(i, 1), :] * gain_t[u] + bias_t[u]).astype(BF16)
            change = dot(nm, ow[u], TN)
            now = cur[u, base + i].astype(F32) + gate[base + i] * change
            cur[1 - u, base + i] = now.astype(BF16)

    def loop(count, body):
        def step(i, carry):
            body(i)
            return carry

        lax.fori_loop(0, count, step, 0)

    def spread(u, k, half):
        part = pl.ds(half * HALF, HALF)
        flight = (u * 3 + k) * 2 + half
        if k == MIXED:
            src_at = lambda r, c: m_all.at[u, c, r, part]
            dst = m_in.at[u, me, part]
        else:
            src, all_ = ((right, r_all), (left, l_all))[k]
            src_at = lambda r, c: src.at[u, r * N_COL + c, part]
            dst = all_.at[u, col, row, part]
        pltpu.make_async_copy(src_at(row, col), dst, recv_sem.at[flight]).start()

        def send(r, c):
            pltpu.make_async_remote_copy(
                src_ref=src_at(r, c),
                dst_ref=dst,
                send_sem=send_sem.at[flight],
                recv_sem=recv_sem.at[flight],
                device_id=(r, c),
                device_id_type=pl.DeviceIdType.MESH,
            ).start()

        each_target(row, col, send)

    def arrived(u, k, half):
        size = m_in.at[u, pl.ds(0, DEV // 2)]
        pltpu.make_async_copy(size, size, recv_sem.at[(u * 3 + k) * 2 + half]).wait()

    def sent(u, k, half):
        flight = (u * 3 + k) * 2 + half
        size = m_in.at[u, pl.ds(0, DEV // 2 - 1)]
        pltpu.make_async_copy(size, size, send_sem.at[flight]).wait()
        size = m_in.at[u, 0, pl.ds(0, HALF)]
        pltpu.make_async_copy(size, size, send_sem.at[flight]).wait()

    def put_mixed(u, half, jb, out):
        out = out.astype(BF16)
        for k in range(2):
            m_all[u, 2 * jb + k, :, pl.ds(half * HALF, HALF), :] = out[
                :, k * COLS : (k + 1) * COLS
            ].reshape(N_ROW, HALF, COLS)

    def mix_outgoing(half):
        a = jnp.concatenate(
            [
                l_all[0, c, :, half * HALF : (half + 1) * HALF, :].reshape(512, COLS)
                for c in range(N_COL)
            ],
            axis=1,
        )

        def block(jb):
            b = jnp.concatenate(
                [r_all[0, c, pl.ds(4 * jb, 4)].reshape(256, COLS) for c in range(N_COL)], axis=1
            )
            put_mixed(0, half, jb, dot(a, b, NT))

        loop(4, block)

    def turn(half):
        def block(c):
            part = l_all[1, c, :, half * HALF : (half + 1) * HALF, :].reshape(512, COLS)
            lt[half, pl.ds(2 * c, 2)] = part.T.reshape(2, ROWS, 512)

        loop(N_COL, block)

    def mix_incoming(half, k):
        a = lt[k, :, half * HALF : (half + 1) * HALF, :].reshape(512, 512)

        def block(jb):
            b = jnp.concatenate(
                [
                    r_all[1, 2 * jb + c, :, k * HALF : (k + 1) * HALF, :].reshape(512, COLS)
                    for c in range(2)
                ],
                axis=1,
            )
            if k == 0:
                acc[half, jb] = dot(a, b, NN)
            else:
                put_mixed(1, half, jb, acc[half, jb] + dot(a, b, NN))

        loop(4, block)

    for g in range(2):
        load(g).wait()
    loop(2, lambda g: front_group(0, g, (RIGHT,)))
    pl.semaphore_wait(barrier, DEV - 1)
    spread(0, RIGHT, 0)
    for g in range(2, 4):
        load(g).wait()
    loop(2, lambda g: front_group(0, 2 + g))
    spread(0, RIGHT, 1)
    loop(2, lambda g: front_group(0, g, (LEFT,), False))
    spread(0, LEFT, 0)
    spread(0, LEFT, 1)
    for k in range(4):
        wt[1, k * CH : (k + 1) * CH] = pw[1, k].T
    for u in range(2):
        gain_t[u] = jnp.broadcast_to(og[u : u + 1], (CH, CH)).T
        bias_t[u] = jnp.broadcast_to(ob[u : u + 1], (CH, CH)).T
    loop(ROWS // 4, lambda s: gate_rows(0, s))
    arrived(0, RIGHT, 0)
    arrived(0, RIGHT, 1)
    for half in range(2):
        arrived(0, LEFT, half)
        mix_outgoing(half)
        spread(0, MIXED, half)
    for half in range(2):
        arrived(0, MIXED, half)

        def turnover(g):
            back_group(0, 2 * half + g)
            front_group(1, 2 * half + g)

        loop(2, turnover)
        for k in (RIGHT, LEFT) if half == 0 else (LEFT, RIGHT):
            spread(1, k, half)
    loop(ROWS // 4, lambda s: gate_rows(1, s))
    arrived(1, RIGHT, 0)
    arrived(1, LEFT, 0)
    turn(0)
    for half in range(2):
        mix_incoming(half, 0)
    arrived(1, LEFT, 1)
    turn(1)
    arrived(1, RIGHT, 1)
    for half in range(2):
        mix_incoming(half, 1)
        spread(1, MIXED, half)

    def store(half):
        rows = pl.ds(half * HALF, HALF)
        return pltpu.make_async_copy(cur.at[0, rows], out_h.at[rows], out_sem.at[half])

    for half in range(2):
        arrived(1, MIXED, half)
        loop(2, lambda g: back_group(1, 2 * half + g))
        store(half).start()
    for u in range(2):
        for k in range(3):
            for half in range(2):
                sent(u, k, half)
    for half in range(2):
        store(half).wait()


def shards(*args):
    pieces = (2, DEV, ROWS, COLS)
    planes = (2, N_COL, N_ROW, ROWS, COLS)
    vmem = pltpu.VMEM
    scratch = [
        vmem((2, ROWS, COLS, CH), BF16),
        vmem((ROWS, COLS, CH), BF16),
        vmem((ROWS, COLS, CH), F32),
        vmem(pieces, BF16),
        vmem(pieces, BF16),
        vmem(planes, BF16),
        vmem(planes, BF16),
        vmem((2, N_ROW, ROWS, 512), BF16),
        vmem((2, 4, 512, 256), F32),
        vmem(planes, BF16),
        vmem(pieces, BF16),
    ]
    scratch += [vmem(a.shape, a.dtype) for a in args[1:]]
    scratch += [
        vmem((2, 4 * CH, CH), BF16),
        vmem((2, CH, CH), F32),
        vmem((2, CH, CH), F32),
        vmem((CH * GROUP, COLS), F32),
        vmem((CH * GROUP, COLS), F32),
        vmem((GROUP, COLS), F32),
        pltpu.SemaphoreType.DMA((ROWS // GROUP,)),
        pltpu.SemaphoreType.DMA((7,)),
        pltpu.SemaphoreType.DMA((12,)),
        pltpu.SemaphoreType.DMA((12,)),
        pltpu.SemaphoreType.DMA((2,)),
    ]
    return pl.pallas_call(
        kernel,
        out_shape=jax.ShapeDtypeStruct((ROWS, COLS, CH), BF16),
        in_specs=[pl.BlockSpec(memory_space=pl.ANY)] * 8,
        out_specs=pl.BlockSpec(memory_space=pl.ANY),
        scratch_shapes=scratch,
        compiler_params=pltpu.CompilerParams(
            collective_id=0, has_side_effects=True, vmem_limit_bytes=60 * MIB
        ),
        name="triangle",
    )(*args)


def solution(mesh):
    placed = (P("row", "col", None), P(), P(), P(), P(), P(), P(), P())
    return jax.shard_map(
        shards, mesh=mesh, in_specs=placed, out_specs=P("row", "col", None), check_vma=False
    )
```

```python
import jax
import jax.numpy as jnp
from jax import lax
from jax.experimental import pallas as pl
from jax.experimental.pallas import tpu as pltpu
from jax.sharding import PartitionSpec as P

F32, BF16 = jnp.float32, jnp.bfloat16
ROWS, COLS, N_ROW, N_COL, CH = 64, 128, 16, 8, 128
DEV = N_ROW * N_COL
GROUP, HALF = 16, 32
MIB = 1 << 20
NT = (((1,), (1,)), ((), ()))
TN = (((0,), (0,)), ((), ()))
NN = (((1,), (0,)), ((), ()))
RIGHT, LEFT, MIXED = 0, 1, 2
STEPS = ((3, 1, 2), (2, 1, 3), (2, 3, 0))


def sigmoid(v):
    return 0.5 * jnp.tanh(0.5 * v) + 0.5


def layer_norm(v, gain, bias):
    mean = jnp.mean(v, axis=-1, keepdims=True)
    centred = v - mean
    var = jnp.mean(centred * centred, axis=-1, keepdims=True)
    return centred * lax.rsqrt(var + 1e-5) * gain + bias


def dot(a, b, dims):
    return lax.dot_general(a, b, dims, preferred_element_type=F32)


def each_target(row, col, body):
    y, zh, k = row // 4, lax.rem(row // 2, 2), lax.rem(row, 2)
    x, zl = col // 2, lax.rem(col, 2)
    sign = 1 - 2 * k
    turns = [sign * a for a in range(4)]

    def eight(core, c, b, skip):
        core_at = lax.rem(k + core, 2)
        starts = [
            at + sign * (of_b * b + of_c * c) + 32
            for at, (_, of_b, of_c) in zip((x, y, zh * 2 + zl), STEPS)
        ]
        for later in range(2):
            for a in range(4):
                if skip and later == 0 and a == 0:
                    continue
                to_x, to_y, to_z = (
                    lax.rem(start + turns[(of_a * a + of_b * later) % 4], 4)
                    for start, (of_a, of_b, _) in zip(starts, STEPS)
                )
                body(to_y * 4 + (to_z // 2) * 2 + core_at, to_x * 2 + lax.rem(to_z, 2))

    def step(p, carry):
        eight(p // 8, lax.rem(p // 2, 4), lax.rem(p, 2) * 2, False)
        return carry

    eight(0, 0, 0, True)
    lax.fori_loop(1, 16, step, 0)


def kernel(
    pair_h, ng_h, nb_h, pw_h, gw_h, og_h, ob_h, ow_h, out_h,
    cur, normed, gate, left, right, l_all, r_all, lt, acc, m_all, m_in,
    ng, nb, pw, gw, og, ob, ow, wt, gain_t, bias_t, tl, tr, ts,
    load_sem, param_sem, send_sem, recv_sem, out_sem,
):
    row, col = lax.axis_index("row"), lax.axis_index("col")
    me = row * N_COL + col

    def load(g):
        rows = pl.ds(g * GROUP, GROUP)
        return pltpu.make_async_copy(pair_h.at[rows], cur.at[0, rows], load_sem.at[g])

    params = [
        pltpu.make_async_copy(src, dst, param_sem.at[k])
        for k, (src, dst) in enumerate(
            ((pw_h, pw), (ng_h, ng), (nb_h, nb), (gw_h, gw), (og_h, og), (ob_h, ob), (ow_h, ow))
        )
    ]
    load(0).start()
    for copy in params:
        copy.start()
    for g in range(1, ROWS // GROUP):
        load(g).start()

    barrier = pltpu.get_barrier_semaphore()

    def greet(r, c):
        pl.semaphore_signal(
            barrier, inc=1, device_id=(r, c), device_id_type=pl.DeviceIdType.MESH
        )

    each_target(row, col, greet)
    for copy in params:
        copy.wait()
    for k in range(4):
        wt[0, k * CH : (k + 1) * CH] = pw[0, k].T

    def norm_rows(u, base):
        x = cur[u, pl.ds(base, 2)].reshape(2 * COLS, CH).astype(F32)
        n = layer_norm(x, ng[u : u + 1], nb[u : u + 1]).astype(BF16)
        normed[pl.ds(base, 2)] = n.reshape(2, COLS, CH)
        return n

    def project(u, k, n, i):
        first = 256 * (1 - k)
        p = dot(wt[u, first : first + 256], n, NT)
        side = sigmoid(p[0:128]) * p[128:256]
        wide = (tr, tl)[k]
        for r in range(2):
            wide[pl.ds(i + r, CH, stride=GROUP), :] = side[:, r * COLS : (r + 1) * COLS]

    def keep(u, k, g):
        rows = pl.ds(pl.multiple_of(g * GROUP, GROUP), GROUP)
        side, wide = ((right, tr), (left, tl))[k]
        side[u, :, rows, :] = wide[...].reshape(CH, GROUP, COLS).astype(BF16)

    def front_group(u, g, sides=(RIGHT, LEFT), fresh=True):
        base = g * GROUP
        for i in range(0, GROUP, 2):
            if fresh:
                n = norm_rows(u, base + i)
            else:
                n = normed[pl.ds(base + i, 2)].reshape(2 * COLS, CH)
            for k in sides:
                project(u, k, n, i)
        for k in sides:
            keep(u, k, g)

    def gate_rows(u, step):
        n = normed[pl.ds(step * 4, 4)].reshape(4 * COLS, CH)
        gate[pl.ds(step * 4, 4)] = sigmoid(dot(n, gw[u], NN)).reshape(4, COLS, CH)

    def back_group(u, g):
        base = g * GROUP
        m = m_in[u, :, pl.ds(pl.multiple_of(base, GROUP), GROUP), :].astype(F32)
        mean = jnp.mean(m, axis=0)
        centred = m - mean[None]
        var = jnp.mean(centred * centred, axis=0)
        ts[...] = lax.rsqrt(var + 1e-5)
        tl[...] = centred.reshape(CH * GROUP, COLS)
        for i in range(GROUP):
            c = tl[pl.ds(i, CH, stride=GROUP), :]
            nm = (c * ts[pl.ds(i, 1), :] * gain_t[u] + bias_t[u]).astype(BF16)
            change = dot(nm, ow[u], TN)
            now = cur[u, base + i].astype(F32) + gate[base + i] * change
            cur[1 - u, base + i] = now.astype(BF16)

    def loop(count, body):
        def step(i, carry):
            body(i)
            return carry

        lax.fori_loop(0, count, step, 0)

    def spread(u, k, half, quarter=None):
        part = pl.ds(half * HALF, HALF)
        flight = (u * 3 + k) * 2 + half
        if quarter is not None:
            part = pl.ds(half * HALF + quarter * GROUP, GROUP)
            flight += quarter
        if k == MIXED:
            src_at = lambda r, c: m_all.at[u, c, r, part]
            dst = m_in.at[u, me, part]
        else:
            src, all_ = ((right, r_all), (left, l_all))[k]
            src_at = lambda r, c: src.at[u, r * N_COL + c, part]
            dst = all_.at[u, col, row, part]
        pltpu.make_async_copy(src_at(row, col), dst, recv_sem.at[flight]).start()

        def send(r, c):
            pltpu.make_async_remote_copy(
                src_ref=src_at(r, c),
                dst_ref=dst,
                send_sem=send_sem.at[flight],
                recv_sem=recv_sem.at[flight],
                device_id=(r, c),
                device_id_type=pl.DeviceIdType.MESH,
            ).start()

        each_target(row, col, send)

    def arrived(u, k, half, quarter=None):
        flight, rows = (u * 3 + k) * 2 + half, HALF
        if quarter is not None:
            flight, rows = flight + quarter, GROUP
        size = m_in.at[u, :, pl.ds(0, rows)]
        pltpu.make_async_copy(size, size, recv_sem.at[flight]).wait()

    def sent(u, k, half, quarter=None):
        flight, rows = (u * 3 + k) * 2 + half, HALF
        if quarter is not None:
            flight, rows = flight + quarter, GROUP
        size = m_in.at[u, pl.ds(0, DEV - 1), pl.ds(0, rows)]
        pltpu.make_async_copy(size, size, send_sem.at[flight]).wait()

    def put_mixed(u, half, jb, out):
        out = out.astype(BF16)
        for k in range(2):
            m_all[u, 2 * jb + k, :, pl.ds(half * HALF, HALF), :] = out[
                :, k * COLS : (k + 1) * COLS
            ].reshape(N_ROW, HALF, COLS)

    def mix_outgoing(half):
        a = jnp.concatenate(
            [
                l_all[0, c, :, half * HALF : (half + 1) * HALF, :].reshape(512, COLS)
                for c in range(N_COL)
            ],
            axis=1,
        )

        def block(jb):
            b = jnp.concatenate(
                [r_all[0, c, pl.ds(4 * jb, 4)].reshape(256, COLS) for c in range(N_COL)], axis=1
            )
            put_mixed(0, half, jb, dot(a, b, NT))

        loop(4, block)

    def turn(half):
        def block(c):
            part = l_all[1, c, :, half * HALF : (half + 1) * HALF, :].reshape(512, COLS)
            lt[half, pl.ds(2 * c, 2)] = part.T.reshape(2, ROWS, 512)

        loop(N_COL, block)

    def mix_incoming(half, k):
        a = lt[k, :, half * HALF : (half + 1) * HALF, :].reshape(512, 512)

        def block(jb):
            b = jnp.concatenate(
                [
                    r_all[1, 2 * jb + c, :, k * HALF : (k + 1) * HALF, :].reshape(512, COLS)
                    for c in range(2)
                ],
                axis=1,
            )
            if k == 0:
                acc[half, jb] = dot(a, b, NN)
            else:
                put_mixed(1, half, jb, acc[half, jb] + dot(a, b, NN))

        loop(4, block)

    for g in range(2):
        load(g).wait()
    loop(2, lambda g: front_group(0, g, (RIGHT,)))
    pl.semaphore_wait(barrier, DEV - 1)
    spread(0, RIGHT, 0)
    for g in range(2, 4):
        load(g).wait()
    loop(2, lambda g: front_group(0, 2 + g))
    spread(0, RIGHT, 1)
    loop(2, lambda g: front_group(0, g, (LEFT,), False))
    spread(0, LEFT, 0)
    spread(0, LEFT, 1)
    for k in range(4):
        wt[1, k * CH : (k + 1) * CH] = pw[1, k].T
    for u in range(2):
        gain_t[u] = jnp.broadcast_to(og[u : u + 1], (CH, CH)).T
        bias_t[u] = jnp.broadcast_to(ob[u : u + 1], (CH, CH)).T
    loop(ROWS // 4, lambda s: gate_rows(0, s))
    arrived(0, RIGHT, 0)
    arrived(0, RIGHT, 1)
    for half in range(2):
        arrived(0, LEFT, half)
        mix_outgoing(half)
        spread(0, MIXED, half)
    for half in range(2):
        arrived(0, MIXED, half)

        def turnover(g):
            back_group(0, 2 * half + g)
            front_group(1, 2 * half + g)

        loop(2, turnover)
        for k in (RIGHT, LEFT) if half == 0 else (LEFT, RIGHT):
            spread(1, k, half)
    loop(ROWS // 4, lambda s: gate_rows(1, s))
    arrived(1, RIGHT, 0)
    arrived(1, LEFT, 0)
    turn(0)
    for half in range(2):
        mix_incoming(half, 0)
    arrived(1, LEFT, 1)
    turn(1)
    arrived(1, RIGHT, 1)
    mix_incoming(0, 1)
    spread(1, MIXED, 0)
    mix_incoming(1, 1)
    spread(1, MIXED, 1, 0)
    spread(1, MIXED, 1, 1)

    def store(k, first, count):
        rows = pl.ds(first, count)
        return pltpu.make_async_copy(cur.at[0, rows], out_h.at[rows], out_sem.at[k])

    stores = [store(0, 0, HALF), store(1, HALF, GROUP), store(2, HALF + GROUP, GROUP)]
    arrived(1, MIXED, 0)
    loop(2, lambda g: back_group(1, g))
    stores[0].start()
    for quarter in range(2):
        arrived(1, MIXED, 1, quarter)
        loop(1, lambda g: back_group(1, 2 + quarter))
        stores[1 + quarter].start()
    for u in range(2):
        for k in range(3):
            for half in range(2):
                if (u, k, half) != (1, MIXED, 1):
                    sent(u, k, half)
    for quarter in range(2):
        sent(1, MIXED, 1, quarter)
    for copy in stores:
        copy.wait()


def shards(*args):
    pieces = (2, DEV, ROWS, COLS)
    planes = (2, N_COL, N_ROW, ROWS, COLS)
    vmem = pltpu.VMEM
    scratch = [
        vmem((2, ROWS, COLS, CH), BF16),
        vmem((ROWS, COLS, CH), BF16),
        vmem((ROWS, COLS, CH), F32),
        vmem(pieces, BF16),
        vmem(pieces, BF16),
        vmem(planes, BF16),
        vmem(planes, BF16),
        vmem((2, N_ROW, ROWS, 512), BF16),
        vmem((2, 4, 512, 256), F32),
        vmem(planes, BF16),
        vmem(pieces, BF16),
    ]
    scratch += [vmem(a.shape, a.dtype) for a in args[1:]]
    scratch += [
        vmem((2, 4 * CH, CH), BF16),
        vmem((2, CH, CH), F32),
        vmem((2, CH, CH), F32),
        vmem((CH * GROUP, COLS), F32),
        vmem((CH * GROUP, COLS), F32),
        vmem((GROUP, COLS), F32),
        pltpu.SemaphoreType.DMA((ROWS // GROUP,)),
        pltpu.SemaphoreType.DMA((7,)),
        pltpu.SemaphoreType.DMA((13,)),
        pltpu.SemaphoreType.DMA((13,)),
        pltpu.SemaphoreType.DMA((3,)),
    ]
    return pl.pallas_call(
        kernel,
        out_shape=jax.ShapeDtypeStruct((ROWS, COLS, CH), BF16),
        in_specs=[pl.BlockSpec(memory_space=pl.ANY)] * 8,
        out_specs=pl.BlockSpec(memory_space=pl.ANY),
        scratch_shapes=scratch,
        compiler_params=pltpu.CompilerParams(
            collective_id=0, has_side_effects=True, vmem_limit_bytes=60 * MIB
        ),
        name="triangle",
    )(*args)


def solution(mesh):
    placed = (P("row", "col", None), P(), P(), P(), P(), P(), P(), P())
    return jax.shard_map(
        shards, mesh=mesh, in_specs=placed, out_specs=P("row", "col", None), check_vma=False
    )
```

```python
import jax
import jax.numpy as jnp
from jax import lax
from jax.experimental import pallas as pl
from jax.experimental.pallas import tpu as pltpu
from jax.sharding import PartitionSpec as P

F32, BF16 = jnp.float32, jnp.bfloat16
ROWS, COLS, N_ROW, N_COL, CH = 64, 128, 16, 8, 128
DEV = N_ROW * N_COL
GROUP, HALF = 16, 32
MIB = 1 << 20
NT = (((1,), (1,)), ((), ()))
TN = (((0,), (0,)), ((), ()))
NN = (((1,), (0,)), ((), ()))
RIGHT, LEFT = 0, 1
SLOTS = (
    {(RIGHT, 0): 0, (RIGHT, 1): 1, (LEFT, 0): 2, (LEFT, 1): 3},
    {(RIGHT, 0): 0, (LEFT, 0): 1, (LEFT, 1): 2, (RIGHT, 1): 3},
)
SIDES = ((0, 0, 1), (0, 1, 2), (0, 3, 1), (1, 0, 2), (1, 2, 1), (1, 3, 1))
MIXED = ((0, 0, 32), (0, 32, 32), (1, 0, 32), (1, 32, 16), (1, 48, 16))
FLIGHTS = len(SIDES) + len(MIXED)
STEPS = ((3, 1, 2), (2, 1, 3), (2, 3, 0))


def sigmoid(v):
    return 0.5 * jnp.tanh(0.5 * v) + 0.5


def layer_norm(v, gain, bias):
    mean = jnp.mean(v, axis=-1, keepdims=True)
    centred = v - mean
    var = jnp.mean(centred * centred, axis=-1, keepdims=True)
    return centred * lax.rsqrt(var + 1e-5) * gain + bias


def dot(a, b, dims):
    return lax.dot_general(a, b, dims, preferred_element_type=F32)


def each_target(row, col, body):
    y, zh, k = row // 4, lax.rem(row // 2, 2), lax.rem(row, 2)
    x, zl = col // 2, lax.rem(col, 2)
    sign = 1 - 2 * k
    turns = [sign * a for a in range(4)]

    def eight(core, c, b, skip):
        core_at = lax.rem(k + core, 2)
        starts = [
            at + sign * (of_b * b + of_c * c) + 32
            for at, (_, of_b, of_c) in zip((x, y, zh * 2 + zl), STEPS)
        ]
        for later in range(2):
            for a in range(4):
                if skip and later == 0 and a == 0:
                    continue
                to_x, to_y, to_z = (
                    lax.rem(start + turns[(of_a * a + of_b * later) % 4], 4)
                    for start, (of_a, of_b, _) in zip(starts, STEPS)
                )
                body(to_y * 4 + (to_z // 2) * 2 + core_at, to_x * 2 + lax.rem(to_z, 2))

    def step(p, carry):
        eight(p // 8, lax.rem(p // 2, 4), lax.rem(p, 2) * 2, False)
        return carry

    eight(0, 0, 0, True)
    lax.fori_loop(1, 16, step, 0)


def kernel(
    pair_h, ng_h, nb_h, pw_h, gw_h, og_h, ob_h, ow_h, out_h,
    cur, normed, gate, sides, all_sides, lt, acc, m_all, m_in,
    ng, nb, pw, gw, og, ob, ow, wt, gain_t, bias_t, tl, tr, ts,
    load_sem, param_sem, send_sem, recv_sem, out_sem,
):
    row, col = lax.axis_index("row"), lax.axis_index("col")
    me = row * N_COL + col

    def load(g):
        rows = pl.ds(g * GROUP, GROUP)
        return pltpu.make_async_copy(pair_h.at[rows], cur.at[0, rows], load_sem.at[g])

    params = [
        pltpu.make_async_copy(src, dst, param_sem.at[k])
        for k, (src, dst) in enumerate(
            ((pw_h, pw), (ng_h, ng), (nb_h, nb), (gw_h, gw), (og_h, og), (ob_h, ob), (ow_h, ow))
        )
    ]
    load(0).start()
    for copy in params:
        copy.start()
    for g in range(1, ROWS // GROUP):
        load(g).start()

    barrier = pltpu.get_barrier_semaphore()

    def greet(r, c):
        pl.semaphore_signal(
            barrier, inc=1, device_id=(r, c), device_id_type=pl.DeviceIdType.MESH
        )

    each_target(row, col, greet)
    for copy in params:
        copy.wait()
    for k in range(4):
        wt[0, k * CH : (k + 1) * CH] = pw[0, k].T

    def norm_rows(u, base):
        x = cur[u, pl.ds(base, 2)].reshape(2 * COLS, CH).astype(F32)
        n = layer_norm(x, ng[u : u + 1], nb[u : u + 1]).astype(BF16)
        normed[pl.ds(base, 2)] = n.reshape(2, COLS, CH)
        return n

    def project(u, k, n, i):
        first = 256 * (1 - k)
        p = dot(wt[u, first : first + 256], n, NT)
        side = sigmoid(p[0:128]) * p[128:256]
        wide = (tr, tl)[k]
        for r in range(2):
            wide[pl.ds(i + r, CH, stride=GROUP), :] = side[:, r * COLS : (r + 1) * COLS]

    def keep(u, k, half, g):
        rows = pl.ds(pl.multiple_of(g * GROUP, GROUP), GROUP)
        wide = (tr, tl)[k]
        sides[u, :, SLOTS[u][k, half], rows, :] = (
            wide[...].reshape(CH, GROUP, COLS).astype(BF16)
        )

    def front_group(u, half, g, which=(RIGHT, LEFT), fresh=True):
        base = half * HALF + g * GROUP
        for i in range(0, GROUP, 2):
            if fresh:
                n = norm_rows(u, base + i)
            else:
                n = normed[pl.ds(base + i, 2)].reshape(2 * COLS, CH)
            for k in which:
                project(u, k, n, i)
        for k in which:
            keep(u, k, half, g)

    def gate_rows(u, step):
        n = normed[pl.ds(step * 4, 4)].reshape(4 * COLS, CH)
        gate[pl.ds(step * 4, 4)] = sigmoid(dot(n, gw[u], NN)).reshape(4, COLS, CH)

    def back_group(u, g):
        base = g * GROUP
        m = m_in[u, :, pl.ds(pl.multiple_of(base, GROUP), GROUP), :].astype(F32)
        mean = jnp.mean(m, axis=0)
        centred = m - mean[None]
        var = jnp.mean(centred * centred, axis=0)
        ts[...] = lax.rsqrt(var + 1e-5)
        tl[...] = centred.reshape(CH * GROUP, COLS)
        for i in range(GROUP):
            c = tl[pl.ds(i, CH, stride=GROUP), :]
            nm = (c * ts[pl.ds(i, 1), :] * gain_t[u] + bias_t[u]).astype(BF16)
            change = dot(nm, ow[u], TN)
            now = cur[u, base + i].astype(F32) + gate[base + i] * change
            cur[1 - u, base + i] = now.astype(BF16)

    def loop(count, body):
        def step(i, carry):
            body(i)
            return carry

        lax.fori_loop(0, count, step, 0)

    def flight_of(flight):
        if flight < len(SIDES):
            u, first, count = SIDES[flight]
            part, rows = pl.ds(first, count), count * HALF
            dst = all_sides.at[u, col, row, part]
            return lambda r, c: sides.at[u, r * N_COL + c, part], dst, rows
        u, first, rows = MIXED[flight - len(SIDES)]
        part = pl.ds(first, rows)
        return lambda r, c: m_all.at[u, c, r, part], m_in.at[u, me, part], rows

    def spread(flight):
        src_at, dst, _ = flight_of(flight)
        pltpu.make_async_copy(src_at(row, col), dst, recv_sem.at[flight]).start()

        def send(r, c):
            pltpu.make_async_remote_copy(
                src_ref=src_at(r, c),
                dst_ref=dst,
                send_sem=send_sem.at[flight],
                recv_sem=recv_sem.at[flight],
                device_id=(r, c),
                device_id_type=pl.DeviceIdType.MESH,
            ).start()

        each_target(row, col, send)

    def arrived(flight):
        size = m_in.at[0, :, pl.ds(0, flight_of(flight)[2])]
        pltpu.make_async_copy(size, size, recv_sem.at[flight]).wait()

    def sent(flight):
        size = m_in.at[0, pl.ds(0, DEV - 1), pl.ds(0, flight_of(flight)[2])]
        pltpu.make_async_copy(size, size, send_sem.at[flight]).wait()

    def put_mixed(u, half, jb, out):
        out = out.astype(BF16)
        for k in range(2):
            m_all[u, 2 * jb + k, :, pl.ds(half * HALF, HALF), :] = out[
                :, k * COLS : (k + 1) * COLS
            ].reshape(N_ROW, HALF, COLS)

    def mix_outgoing(half):
        a = jnp.concatenate(
            [
                all_sides[0, c, :, SLOTS[0][LEFT, half]].reshape(512, COLS)
                for c in range(N_COL)
            ],
            axis=1,
        )

        def block(jb):
            b = jnp.concatenate(
                [all_sides[0, c, pl.ds(4 * jb, 4), 0:2].reshape(256, COLS) for c in range(N_COL)],
                axis=1,
            )
            put_mixed(0, half, jb, dot(a, b, NT))

        loop(4, block)

    def turn(half):
        def block(c):
            part = all_sides[1, c, :, SLOTS[1][LEFT, half]].reshape(512, COLS)
            lt[half, pl.ds(2 * c, 2)] = part.T.reshape(2, ROWS, 512)

        loop(N_COL, block)

    def mix_incoming(half, k):
        a = lt[k, :, half * HALF : (half + 1) * HALF, :].reshape(512, 512)

        def block(jb):
            b = jnp.concatenate(
                [
                    all_sides[1, 2 * jb + c, :, SLOTS[1][RIGHT, k]].reshape(512, COLS)
                    for c in range(2)
                ],
                axis=1,
            )
            if k == 0:
                acc[half, jb] = dot(a, b, NN)
            else:
                put_mixed(1, half, jb, acc[half, jb] + dot(a, b, NN))

        loop(4, block)

    for g in range(2):
        load(g).wait()
    loop(2, lambda g: front_group(0, 0, g, (RIGHT,)))
    pl.semaphore_wait(barrier, DEV - 1)
    spread(0)
    for g in range(2, 4):
        load(g).wait()
    loop(2, lambda g: front_group(0, 0, g, (LEFT,), False))
    loop(2, lambda g: front_group(0, 1, g))
    spread(1)
    spread(2)
    for k in range(4):
        wt[1, k * CH : (k + 1) * CH] = pw[1, k].T
    for u in range(2):
        gain_t[u] = jnp.broadcast_to(og[u : u + 1], (CH, CH)).T
        bias_t[u] = jnp.broadcast_to(ob[u : u + 1], (CH, CH)).T
    loop(ROWS // 4, lambda s: gate_rows(0, s))
    arrived(0)
    for half in range(2):
        arrived(1 + half)
        mix_outgoing(half)
        spread(6 + half)
    for half in range(2):
        arrived(6 + half)

        def turnover(g):
            back_group(0, 2 * half + g)
            front_group(1, half, g)

        loop(2, turnover)
        if half == 0:
            spread(3)
    spread(4)
    spread(5)
    loop(ROWS // 4, lambda s: gate_rows(1, s))
    arrived(3)
    turn(0)
    for half in range(2):
        mix_incoming(half, 0)
    arrived(4)
    turn(1)
    arrived(5)
    mix_incoming(0, 1)
    spread(8)
    mix_incoming(1, 1)
    spread(9)
    spread(10)

    def store(k, first, count):
        rows = pl.ds(first, count)
        return pltpu.make_async_copy(cur.at[0, rows], out_h.at[rows], out_sem.at[k])

    stores = [store(0, 0, HALF), store(1, HALF, GROUP), store(2, HALF + GROUP, GROUP)]
    arrived(8)
    loop(2, lambda g: back_group(1, g))
    stores[0].start()
    for quarter in range(2):
        arrived(9 + quarter)
        loop(1, lambda g: back_group(1, 2 + quarter))
        stores[1 + quarter].start()
    for flight in range(FLIGHTS):
        sent(flight)
    for copy in stores:
        copy.wait()


def shards(*args):
    pieces = (2, DEV, ROWS, COLS)
    planes = (2, N_COL, N_ROW, ROWS, COLS)
    vmem = pltpu.VMEM
    scratch = [
        vmem((2, ROWS, COLS, CH), BF16),
        vmem((ROWS, COLS, CH), BF16),
        vmem((ROWS, COLS, CH), F32),
        vmem((2, DEV, 4, HALF, COLS), BF16),
        vmem((2, N_COL, N_ROW, 4, HALF, COLS), BF16),
        vmem((2, N_ROW, ROWS, 512), BF16),
        vmem((2, 4, 512, 256), F32),
        vmem(planes, BF16),
        vmem(pieces, BF16),
    ]
    scratch += [vmem(a.shape, a.dtype) for a in args[1:]]
    scratch += [
        vmem((2, 4 * CH, CH), BF16),
        vmem((2, CH, CH), F32),
        vmem((2, CH, CH), F32),
        vmem((CH * GROUP, COLS), F32),
        vmem((CH * GROUP, COLS), F32),
        vmem((GROUP, COLS), F32),
        pltpu.SemaphoreType.DMA((ROWS // GROUP,)),
        pltpu.SemaphoreType.DMA((7,)),
        pltpu.SemaphoreType.DMA((FLIGHTS,)),
        pltpu.SemaphoreType.DMA((FLIGHTS,)),
        pltpu.SemaphoreType.DMA((3,)),
    ]
    return pl.pallas_call(
        kernel,
        out_shape=jax.ShapeDtypeStruct((ROWS, COLS, CH), BF16),
        in_specs=[pl.BlockSpec(memory_space=pl.ANY)] * 8,
        out_specs=pl.BlockSpec(memory_space=pl.ANY),
        scratch_shapes=scratch,
        compiler_params=pltpu.CompilerParams(
            collective_id=0, has_side_effects=True, vmem_limit_bytes=60 * MIB
        ),
        name="triangle",
    )(*args)


def solution(mesh):
    placed = (P("row", "col", None), P(), P(), P(), P(), P(), P(), P())
    return jax.shard_map(
        shards, mesh=mesh, in_specs=placed, out_specs=P("row", "col", None), check_vma=False
    )
```

```python
import jax
import jax.numpy as jnp
from jax import lax
from jax.experimental import pallas as pl
from jax.experimental.pallas import tpu as pltpu
from jax.sharding import PartitionSpec as P

F32, BF16 = jnp.float32, jnp.bfloat16
ROWS, COLS, N_ROW, N_COL, CH = 64, 128, 16, 8, 128
DEV = N_ROW * N_COL
GROUP, HALF = 16, 32
MIB = 1 << 20
NT = (((1,), (1,)), ((), ()))
TN = (((0,), (0,)), ((), ()))
NN = (((1,), (0,)), ((), ()))
RIGHT, LEFT = 0, 1
PLACE = (
    {(RIGHT, 0): 0, (RIGHT, 1): 32, (LEFT, 0): 64, (LEFT, 1): 96},
    {(RIGHT, 0): 0, (LEFT, 0): 32, (RIGHT, 1): 64, (LEFT, 1): 96},
)
SIDES = ((0, 0, 16), (0, 16, 48), (0, 64, 32), (0, 96, 32), (1, 0, 64), (1, 64, 48), (1, 112, 16))
MIXED = ((0, 0, 32), (0, 32, 32), (1, 0, 32), (1, 32, 16), (1, 48, 16))
FLIGHTS = len(SIDES) + len(MIXED)
STEPS = ((3, 1, 2), (2, 1, 3), (2, 3, 0))


def sigmoid(v):
    return 0.5 * jnp.tanh(0.5 * v) + 0.5


def layer_norm(v, gain, bias):
    mean = jnp.mean(v, axis=-1, keepdims=True)
    centred = v - mean
    var = jnp.mean(centred * centred, axis=-1, keepdims=True)
    return centred * lax.rsqrt(var + 1e-5) * gain + bias


def dot(a, b, dims):
    return lax.dot_general(a, b, dims, preferred_element_type=F32)


def each_target(row, col, body):
    y, zh, k = row // 4, lax.rem(row // 2, 2), lax.rem(row, 2)
    x, zl = col // 2, lax.rem(col, 2)
    sign = 1 - 2 * k
    turns = [sign * a for a in range(4)]

    def eight(core, c, b, skip):
        core_at = lax.rem(k + core, 2)
        starts = [
            at + sign * (of_b * b + of_c * c) + 32
            for at, (_, of_b, of_c) in zip((x, y, zh * 2 + zl), STEPS)
        ]
        for later in range(2):
            for a in range(4):
                if skip and later == 0 and a == 0:
                    continue
                to_x, to_y, to_z = (
                    lax.rem(start + turns[(of_a * a + of_b * later) % 4], 4)
                    for start, (of_a, of_b, _) in zip(starts, STEPS)
                )
                body(to_y * 4 + (to_z // 2) * 2 + core_at, to_x * 2 + lax.rem(to_z, 2))

    def step(p, carry):
        eight(p // 8, lax.rem(p // 2, 4), lax.rem(p, 2) * 2, False)
        return carry

    eight(0, 0, 0, True)
    lax.fori_loop(1, 16, step, 0)


def kernel(
    pair_h, ng_h, nb_h, pw_h, gw_h, og_h, ob_h, ow_h, out_h,
    cur, normed, gate, sides, all_sides, lt, acc, m_all, m_in,
    ng, nb, pw, gw, og, ob, ow, wt, gain_t, bias_t, tl, tr, ts,
    load_sem, param_sem, send_sem, recv_sem, out_sem,
):
    row, col = lax.axis_index("row"), lax.axis_index("col")
    me = row * N_COL + col

    def load(g):
        rows = pl.ds(g * GROUP, GROUP)
        return pltpu.make_async_copy(pair_h.at[rows], cur.at[0, rows], load_sem.at[g])

    params = [
        pltpu.make_async_copy(src, dst, param_sem.at[k])
        for k, (src, dst) in enumerate(
            ((pw_h, pw), (ng_h, ng), (nb_h, nb), (gw_h, gw), (og_h, og), (ob_h, ob), (ow_h, ow))
        )
    ]
    load(0).start()
    for copy in params:
        copy.start()
    for g in range(1, ROWS // GROUP):
        load(g).start()

    barrier = pltpu.get_barrier_semaphore()

    def greet(r, c):
        pl.semaphore_signal(
            barrier, inc=1, device_id=(r, c), device_id_type=pl.DeviceIdType.MESH
        )

    each_target(row, col, greet)
    for copy in params:
        copy.wait()
    for k in range(4):
        wt[0, k * CH : (k + 1) * CH] = pw[0, k].T

    def norm_rows(u, base):
        x = cur[u, pl.ds(base, 2)].reshape(2 * COLS, CH).astype(F32)
        n = layer_norm(x, ng[u : u + 1], nb[u : u + 1]).astype(BF16)
        normed[pl.ds(base, 2)] = n.reshape(2, COLS, CH)
        return n

    def project(u, k, n):
        first = 256 * (1 - k)
        p = dot(wt[u, first : first + 256], n, NT)
        return sigmoid(p[0:128]) * p[128:256]

    def keep(u, k, half, g, wide):
        rows = pl.ds(pl.multiple_of(PLACE[u][k, half] + g * GROUP, GROUP), GROUP)
        sides[u, :, rows, :] = wide[...].reshape(CH, GROUP, COLS).astype(BF16)

    def front_group(u, k, half, g, fresh=True):
        base = half * HALF + g * GROUP
        for i in range(0, GROUP, 2):
            if fresh:
                n = norm_rows(u, base + i)
            else:
                n = normed[pl.ds(base + i, 2)].reshape(2 * COLS, CH)
            side = project(u, k, n)
            for r in range(2):
                (tr, tl)[k][pl.ds(i + r, CH, stride=GROUP), :] = side[:, r * COLS : (r + 1) * COLS]
        keep(u, k, half, g, (tr, tl)[k])

    def left_by_parts(half):
        def eight(p):
            for q in range(8):
                rows = [half * HALF + p * 8 + q + r * GROUP for r in range(2)]
                order = [(r, c) for part in range(2) for r in rows for c in (part, part + 2)]
                n = jnp.concatenate([normed[r, c * 32 : (c + 1) * 32] for r, c in order], axis=0)
                side = project(1, LEFT, n)
                for part, wide in enumerate((tl, tr)):
                    wide[pl.ds(p * 8 + q, CH, stride=GROUP), :] = side[
                        :, part * COLS : (part + 1) * COLS
                    ]

        loop(2, eight)
        keep(1, LEFT, half, 0, tl)
        keep(1, LEFT, half, 1, tr)

    def gate_rows(u, step):
        n = normed[pl.ds(step * 4, 4)].reshape(4 * COLS, CH)
        gate[pl.ds(step * 4, 4)] = sigmoid(dot(n, gw[u], NN)).reshape(4, COLS, CH)

    def back_group(u, g):
        base = g * GROUP
        m = m_in[u, :, pl.ds(pl.multiple_of(base, GROUP), GROUP), :].astype(F32)
        mean = jnp.mean(m, axis=0)
        centred = m - mean[None]
        var = jnp.mean(centred * centred, axis=0)
        ts[...] = lax.rsqrt(var + 1e-5)
        tl[...] = centred.reshape(CH * GROUP, COLS)
        for i in range(GROUP):
            c = tl[pl.ds(i, CH, stride=GROUP), :]
            nm = (c * ts[pl.ds(i, 1), :] * gain_t[u] + bias_t[u]).astype(BF16)
            change = dot(nm, ow[u], TN)
            now = cur[u, base + i].astype(F32) + gate[base + i] * change
            cur[1 - u, base + i] = now.astype(BF16)

    def loop(count, body):
        def step(i, carry):
            body(i)
            return carry

        lax.fori_loop(0, count, step, 0)

    def flight_of(flight):
        if flight < len(SIDES):
            u, first, rows = SIDES[flight]
            part = pl.ds(first, rows)
            dst = all_sides.at[u, col, row, part]
            return lambda r, c: sides.at[u, r * N_COL + c, part], dst, rows
        u, first, rows = MIXED[flight - len(SIDES)]
        part = pl.ds(first, rows)
        return lambda r, c: m_all.at[u, c, r, part], m_in.at[u, me, part], rows

    def spread(flight):
        src_at, dst, _ = flight_of(flight)
        pltpu.make_async_copy(src_at(row, col), dst, recv_sem.at[flight]).start()

        def send(r, c):
            pltpu.make_async_remote_copy(
                src_ref=src_at(r, c),
                dst_ref=dst,
                send_sem=send_sem.at[flight],
                recv_sem=recv_sem.at[flight],
                device_id=(r, c),
                device_id_type=pl.DeviceIdType.MESH,
            ).start()

        each_target(row, col, send)

    def arrived(flight):
        size = m_in.at[0, :, pl.ds(0, flight_of(flight)[2])]
        pltpu.make_async_copy(size, size, recv_sem.at[flight]).wait()

    def sent(flight):
        size = m_in.at[0, pl.ds(0, DEV - 1), pl.ds(0, flight_of(flight)[2])]
        pltpu.make_async_copy(size, size, send_sem.at[flight]).wait()

    def put_mixed(u, half, jb, out):
        out = out.astype(BF16)
        for k in range(2):
            m_all[u, 2 * jb + k, :, pl.ds(half * HALF, HALF), :] = out[
                :, k * COLS : (k + 1) * COLS
            ].reshape(N_ROW, HALF, COLS)

    def side_rows(u, c, k, half, first=0, rows=HALF):
        first += PLACE[u][k, half]
        return all_sides[u, c, :, first : first + rows, :]

    def mix_outgoing(half):
        a = jnp.concatenate(
            [
                side_rows(0, c, LEFT, half).reshape(512, COLS)
                for c in range(N_COL)
            ],
            axis=1,
        )

        def block(jb):
            b = jnp.concatenate(
                [all_sides[0, c, pl.ds(4 * jb, 4), 0:64].reshape(256, COLS) for c in range(N_COL)],
                axis=1,
            )
            put_mixed(0, half, jb, dot(a, b, NT))

        loop(4, block)

    def turn(half, part):
        def block(c):
            t = side_rows(1, c, LEFT, half, part * GROUP, GROUP).reshape(256, COLS).T
            for r in range(2):
                lt[half, pl.ds(2 * c, 2), part * HALF : (part + 1) * HALF, r * 256 : r * 256 + 256] = (
                    t[r * 64 : (r + 1) * 64].reshape(2, HALF, 256)
                )

        loop(N_COL, block)

    def mix_incoming(half, k):
        a = lt[k, :, half * HALF : (half + 1) * HALF, :].reshape(512, 512)

        def block(jb):
            b = jnp.concatenate(
                [
                    jnp.concatenate(
                        [
                            side_rows(1, 2 * jb + c, RIGHT, k, r * GROUP, GROUP).reshape(256, COLS)
                            for r in range(2)
                        ],
                        axis=0,
                    )
                    for c in range(2)
                ],
                axis=1,
            )
            if k == 0:
                acc[half, jb] = dot(a, b, NN)
            else:
                put_mixed(1, half, jb, acc[half, jb] + dot(a, b, NN))

        loop(4, block)

    load(0).wait()
    front_group(0, RIGHT, 0, 0)
    pl.semaphore_wait(barrier, DEV - 1)
    spread(0)
    for g in range(1, 4):
        load(g).wait()
    front_group(0, RIGHT, 0, 1)
    loop(2, lambda g: front_group(0, RIGHT, 1, g))
    spread(1)
    for half in range(2):
        loop(2, lambda g: front_group(0, LEFT, half, g, False))
        spread(2 + half)
    for k in range(4):
        wt[1, k * CH : (k + 1) * CH] = pw[1, k].T
    for u in range(2):
        gain_t[u] = jnp.broadcast_to(og[u : u + 1], (CH, CH)).T
        bias_t[u] = jnp.broadcast_to(ob[u : u + 1], (CH, CH)).T
    loop(ROWS // 4, lambda s: gate_rows(0, s))
    arrived(0)
    arrived(1)
    for half in range(2):
        arrived(2 + half)
        mix_outgoing(half)
        spread(7 + half)
    for half in range(2):
        arrived(7 + half)

        def turnover(g):
            back_group(0, 2 * half + g)
            front_group(1, RIGHT, half, g)

        loop(2, turnover)
        left_by_parts(half)
        spread(4 + half)
    spread(6)
    loop(ROWS // 4, lambda s: gate_rows(1, s))
    arrived(4)
    for part in range(2):
        turn(0, part)
        mix_incoming(part, 0)
    for part in range(2):
        arrived(5 + part)
        turn(1, part)
        mix_incoming(part, 1)
        if part == 0:
            spread(9)
    spread(10)
    spread(11)

    def store(k, first, count):
        rows = pl.ds(first, count)
        return pltpu.make_async_copy(cur.at[0, rows], out_h.at[rows], out_sem.at[k])

    stores = [store(0, 0, HALF), store(1, HALF, GROUP), store(2, HALF + GROUP, GROUP)]
    arrived(9)
    loop(2, lambda g: back_group(1, g))
    stores[0].start()
    for quarter in range(2):
        arrived(10 + quarter)
        loop(1, lambda g: back_group(1, 2 + quarter))
        stores[1 + quarter].start()
    for flight in range(FLIGHTS):
        sent(flight)
    for copy in stores:
        copy.wait()


def shards(*args):
    pieces = (2, DEV, ROWS, COLS)
    planes = (2, N_COL, N_ROW, ROWS, COLS)
    vmem = pltpu.VMEM
    scratch = [
        vmem((2, ROWS, COLS, CH), BF16),
        vmem((ROWS, COLS, CH), BF16),
        vmem((ROWS, COLS, CH), F32),
        vmem((2, DEV, 2 * ROWS, COLS), BF16),
        vmem((2, N_COL, N_ROW, 2 * ROWS, COLS), BF16),
        vmem((2, N_ROW, ROWS, 512), BF16),
        vmem((2, 4, 512, 256), F32),
        vmem(planes, BF16),
        vmem(pieces, BF16),
    ]
    scratch += [vmem(a.shape, a.dtype) for a in args[1:]]
    scratch += [
        vmem((2, 4 * CH, CH), BF16),
        vmem((2, CH, CH), F32),
        vmem((2, CH, CH), F32),
        vmem((CH * GROUP, COLS), F32),
        vmem((CH * GROUP, COLS), F32),
        vmem((GROUP, COLS), F32),
        pltpu.SemaphoreType.DMA((ROWS // GROUP,)),
        pltpu.SemaphoreType.DMA((7,)),
        pltpu.SemaphoreType.DMA((FLIGHTS,)),
        pltpu.SemaphoreType.DMA((FLIGHTS,)),
        pltpu.SemaphoreType.DMA((3,)),
    ]
    return pl.pallas_call(
        kernel,
        out_shape=jax.ShapeDtypeStruct((ROWS, COLS, CH), BF16),
        in_specs=[pl.BlockSpec(memory_space=pl.ANY)] * 8,
        out_specs=pl.BlockSpec(memory_space=pl.ANY),
        scratch_shapes=scratch,
        compiler_params=pltpu.CompilerParams(
            collective_id=0, has_side_effects=True, vmem_limit_bytes=60 * MIB
        ),
        name="triangle",
    )(*args)


def solution(mesh):
    placed = (P("row", "col", None), P(), P(), P(), P(), P(), P(), P())
    return jax.shard_map(
        shards, mesh=mesh, in_specs=placed, out_specs=P("row", "col", None), check_vma=False
    )
```

```python
import jax
import jax.numpy as jnp
from jax import lax
from jax.experimental import pallas as pl
from jax.experimental.pallas import tpu as pltpu
from jax.sharding import PartitionSpec as P

F32, BF16 = jnp.float32, jnp.bfloat16
ROWS, COLS, N_ROW, N_COL, CH = 64, 128, 16, 8, 128
DEV = N_ROW * N_COL
GROUP, HALF = 16, 32
MIB = 1 << 20
NT = (((1,), (1,)), ((), ()))
TN = (((0,), (0,)), ((), ()))
NN = (((1,), (0,)), ((), ()))
RIGHT, LEFT = 0, 1
PLACE = (
    {(k, half, g): 64 * k + 32 * half + 16 * g for k in range(2) for half in range(2) for g in range(2)},
    {
        (RIGHT, 0, 0): 0,
        (RIGHT, 0, 1): 16,
        (LEFT, 0, 0): 32,
        (RIGHT, 1, 0): 48,
        (RIGHT, 1, 1): 64,
        (LEFT, 1, 0): 80,
        (LEFT, 0, 1): 96,
        (LEFT, 1, 1): 112,
    },
)
SIDES = (
    (0, 0, 16), (0, 16, 16), (0, 32, 32), (0, 64, 32), (0, 96, 32),
    (1, 0, 32), (1, 32, 16), (1, 48, 48), (1, 96, 32),
)
MIXED = ((0, 0, 32), (0, 32, 32), (1, 0, 32), (1, 32, 16), (1, 48, 16))
FLIGHTS = len(SIDES) + len(MIXED)


def sigmoid(v):
    return 0.5 * jnp.tanh(0.5 * v) + 0.5


def layer_norm(v, gain, bias):
    mean = jnp.mean(v, axis=-1, keepdims=True)
    centred = v - mean
    var = jnp.mean(centred * centred, axis=-1, keepdims=True)
    return centred * lax.rsqrt(var + 1e-5) * gain + bias


def dot(a, b, dims):
    return lax.dot_general(a, b, dims, preferred_element_type=F32)


def each_target(row, col, body):
    y, zh, k = row // 4, lax.rem(row // 2, 2), lax.rem(row, 2)
    x, zl = col // 2, lax.rem(col, 2)
    sign = 1 - 2 * k
    turns = [sign * a + 4 for a in range(4)]
    xs = [lax.rem(x + turn, 4) * 2 for turn in turns]
    ys = [lax.rem(y + turn, 4) * 4 for turn in turns]

    def sixteen(core, c, skip):
        core_at = lax.rem(k + core, 2)
        z = [lax.rem(zh * 2 + zl + sign * c + 4 + turn, 4) for turn in turns]
        z_rows = [(at // 2) * 2 + core_at for at in z]
        z_cols = [lax.rem(at, 2) for at in z]
        for b in range(4):
            for a in range(4):
                if not (skip and a == 0 and b == 0):
                    ab = (a + b) % 4
                    body(ys[ab] + z_rows[ab], xs[a] + z_cols[ab])

    def step(p, carry):
        sixteen(p // 4, lax.rem(p, 4), False)
        return carry

    sixteen(0, 0, True)
    lax.fori_loop(1, 8, step, 0)


def kernel(
    pair_h, ng_h, nb_h, pw_h, gw_h, og_h, ob_h, ow_h, out_h,
    cur, normed, gate, sides, all_sides, lt, acc, m_all, m_in,
    ng, nb, pw, gw, og, ob, ow, wt, gain_t, bias_t, tl, tr, ts,
    load_sem, param_sem, send_sem, recv_sem, out_sem,
):
    row, col = lax.axis_index("row"), lax.axis_index("col")
    me = row * N_COL + col

    def load(g):
        rows = pl.ds(g * GROUP, GROUP)
        return pltpu.make_async_copy(pair_h.at[rows], cur.at[0, rows], load_sem.at[g])

    params = [
        pltpu.make_async_copy(src, dst, param_sem.at[k])
        for k, (src, dst) in enumerate(
            ((pw_h, pw), (ng_h, ng), (nb_h, nb), (gw_h, gw), (og_h, og), (ob_h, ob), (ow_h, ow))
        )
    ]
    load(0).start()
    for copy in params:
        copy.start()
    for g in range(1, ROWS // GROUP):
        load(g).start()

    barrier = pltpu.get_barrier_semaphore()

    def greet(r, c):
        pl.semaphore_signal(
            barrier, inc=1, device_id=(r, c), device_id_type=pl.DeviceIdType.MESH
        )

    each_target(row, col, greet)
    for copy in params:
        copy.wait()
    for k in range(2, 4):
        wt[0, k * CH : (k + 1) * CH] = pw[0, k].T

    def norm_rows(u, base):
        x = cur[u, pl.ds(base, 2)].reshape(2 * COLS, CH).astype(F32)
        n = layer_norm(x, ng[u : u + 1], nb[u : u + 1]).astype(BF16)
        normed[pl.ds(base, 2)] = n.reshape(2, COLS, CH)
        return n

    def project(u, k, n):
        first = 256 * (1 - k)
        p = dot(wt[u, first : first + 256], n, NT)
        return sigmoid(p[0:128]) * p[128:256]

    def keep(u, k, half, g, wide):
        first = PLACE[u][k, half, 0] + g * GROUP
        if (u, k) == (1, LEFT):
            first = PLACE[u][k, half, g]
        rows = pl.ds(pl.multiple_of(first, GROUP), GROUP)
        sides[u, :, rows, :] = wide[...].reshape(CH, GROUP, COLS).astype(BF16)

    def front_group(u, k, half, g, fresh=True):
        base = half * HALF + g * GROUP
        for i in range(0, GROUP, 2):
            if fresh:
                n = norm_rows(u, base + i)
            else:
                n = normed[pl.ds(base + i, 2)].reshape(2 * COLS, CH)
            side = project(u, k, n)
            for r in range(2):
                (tr, tl)[k][pl.ds(i + r, CH, stride=GROUP), :] = side[:, r * COLS : (r + 1) * COLS]
        keep(u, k, half, g, (tr, tl)[k])

    def left_by_parts(half):
        def eight(p):
            for q in range(8):
                rows = [half * HALF + p * 8 + q + r * GROUP for r in range(2)]
                order = [(r, c) for part in range(2) for r in rows for c in (part, part + 2)]
                n = jnp.concatenate([normed[r, c * 32 : (c + 1) * 32] for r, c in order], axis=0)
                side = project(1, LEFT, n)
                for part, wide in enumerate((tl, tr)):
                    wide[pl.ds(p * 8 + q, CH, stride=GROUP), :] = side[
                        :, part * COLS : (part + 1) * COLS
                    ]

        loop(2, eight)
        keep(1, LEFT, half, 0, tl)
        keep(1, LEFT, half, 1, tr)

    def gate_rows(u, step):
        n = normed[pl.ds(step * 4, 4)].reshape(4 * COLS, CH)
        gate[pl.ds(step * 4, 4)] = sigmoid(dot(n, gw[u], NN)).reshape(4, COLS, CH)

    def back_group(u, g):
        base = g * GROUP
        m = m_in[u, :, pl.ds(pl.multiple_of(base, GROUP), GROUP), :].astype(F32)
        mean = jnp.mean(m, axis=0)
        centred = m - mean[None]
        var = jnp.mean(centred * centred, axis=0)
        ts[...] = lax.rsqrt(var + 1e-5)
        tl[...] = centred.reshape(CH * GROUP, COLS)
        for i in range(GROUP):
            c = tl[pl.ds(i, CH, stride=GROUP), :]
            nm = (c * ts[pl.ds(i, 1), :] * gain_t[u] + bias_t[u]).astype(BF16)
            change = dot(nm, ow[u], TN)
            now = cur[u, base + i].astype(F32) + gate[base + i] * change
            cur[1 - u, base + i] = now.astype(BF16)

    def loop(count, body):
        def step(i, carry):
            body(i)
            return carry

        lax.fori_loop(0, count, step, 0)

    def flight_of(flight):
        if flight < len(SIDES):
            u, first, rows = SIDES[flight]
            part = pl.ds(first, rows)
            dst = all_sides.at[u, col, row, part]
            return lambda r, c: sides.at[u, r * N_COL + c, part], dst, rows
        u, first, rows = MIXED[flight - len(SIDES)]
        part = pl.ds(first, rows)
        return lambda r, c: m_all.at[u, c, r, part], m_in.at[u, me, part], rows

    def spread(flight):
        src_at, dst, _ = flight_of(flight)
        pltpu.make_async_copy(src_at(row, col), dst, recv_sem.at[flight]).start()

        def send(r, c):
            pltpu.make_async_remote_copy(
                src_ref=src_at(r, c),
                dst_ref=dst,
                send_sem=send_sem.at[flight],
                recv_sem=recv_sem.at[flight],
                device_id=(r, c),
                device_id_type=pl.DeviceIdType.MESH,
            ).start()

        each_target(row, col, send)

    def arrived(flight):
        size = m_in.at[0, :, pl.ds(0, flight_of(flight)[2])]
        pltpu.make_async_copy(size, size, recv_sem.at[flight]).wait()

    def sent(flight):
        size = m_in.at[0, pl.ds(0, DEV - 1), pl.ds(0, flight_of(flight)[2])]
        pltpu.make_async_copy(size, size, send_sem.at[flight]).wait()

    def put_mixed(u, half, jb, out):
        out = out.astype(BF16)
        for k in range(2):
            m_all[u, 2 * jb + k, :, pl.ds(half * HALF, HALF), :] = out[
                :, k * COLS : (k + 1) * COLS
            ].reshape(N_ROW, HALF, COLS)

    def side_rows(u, c, k, half, part, rows=GROUP):
        first = PLACE[u][k, half, part]
        return all_sides[u, c, :, first : first + rows, :].reshape(N_ROW * rows, COLS)

    def mix_outgoing(half):
        a = jnp.concatenate(
            [
                side_rows(0, c, LEFT, half, 0, HALF)
                for c in range(N_COL)
            ],
            axis=1,
        )

        def block(jb):
            b = jnp.concatenate(
                [all_sides[0, c, pl.ds(4 * jb, 4), 0:64].reshape(256, COLS) for c in range(N_COL)],
                axis=1,
            )
            put_mixed(0, half, jb, dot(a, b, NT))

        loop(4, block)

    def turn(half, part):
        def block(c):
            t = side_rows(1, c, LEFT, half, part).T
            for r in range(2):
                lt[half, pl.ds(2 * c, 2), part * HALF : (part + 1) * HALF, r * 256 : r * 256 + 256] = (
                    t[r * 64 : (r + 1) * 64].reshape(2, HALF, 256)
                )

        loop(N_COL, block)

    def mix_incoming(half, k):
        a = lt[k, :, half * HALF : (half + 1) * HALF, :].reshape(512, 512)

        def block(jb):
            b = jnp.concatenate(
                [
                    jnp.concatenate(
                        [
                            side_rows(1, 2 * jb + c, RIGHT, k, r) for r in range(2)
                        ],
                        axis=0,
                    )
                    for c in range(2)
                ],
                axis=1,
            )
            if k == 0:
                acc[half, jb] = dot(a, b, NN)
            else:
                put_mixed(1, half, jb, acc[half, jb] + dot(a, b, NN))

        loop(4, block)

    load(0).wait()
    front_group(0, RIGHT, 0, 0)
    pl.semaphore_wait(barrier, DEV - 1)
    spread(0)
    load(1).wait()
    front_group(0, RIGHT, 0, 1)
    spread(1)
    load(2).wait()
    load(3).wait()
    loop(2, lambda g: front_group(0, RIGHT, 1, g))
    spread(2)
    for k in range(2):
        wt[0, k * CH : (k + 1) * CH] = pw[0, k].T
    for half in range(2):
        loop(2, lambda g: front_group(0, LEFT, half, g, False))
        spread(3 + half)
    for k in range(4):
        wt[1, k * CH : (k + 1) * CH] = pw[1, k].T
    for u in range(2):
        gain_t[u] = jnp.broadcast_to(og[u : u + 1], (CH, CH)).T
        bias_t[u] = jnp.broadcast_to(ob[u : u + 1], (CH, CH)).T
    loop(ROWS // 4, lambda s: gate_rows(0, s))
    for flight in range(3):
        arrived(flight)
    for half in range(2):
        arrived(3 + half)
        mix_outgoing(half)
        spread(9 + half)
    for half in range(2):
        arrived(9 + half)

        def turnover(g):
            back_group(0, 2 * half + g)
            front_group(1, RIGHT, half, g)

        loop(2, turnover)
        if half == 0:
            spread(5)
        left_by_parts(half)
        spread(6 + half)
    spread(8)
    loop(ROWS // 4, lambda s: gate_rows(1, s))
    arrived(5)
    arrived(6)
    turn(0, 0)
    mix_incoming(0, 0)
    arrived(7)
    turn(1, 0)
    mix_incoming(0, 1)
    spread(11)
    arrived(8)
    for k in range(2):
        turn(k, 1)
        mix_incoming(1, k)
    spread(12)
    spread(13)

    def store(k, first, count):
        rows = pl.ds(first, count)
        return pltpu.make_async_copy(cur.at[0, rows], out_h.at[rows], out_sem.at[k])

    stores = [store(0, 0, HALF), store(1, HALF, GROUP), store(2, HALF + GROUP, GROUP)]
    arrived(11)
    loop(2, lambda g: back_group(1, g))
    stores[0].start()
    for quarter in range(2):
        arrived(12 + quarter)
        loop(1, lambda g: back_group(1, 2 + quarter))
        stores[1 + quarter].start()
    for flight in range(FLIGHTS):
        sent(flight)
    for copy in stores:
        copy.wait()


def shards(*args):
    pieces = (2, DEV, ROWS, COLS)
    planes = (2, N_COL, N_ROW, ROWS, COLS)
    vmem = pltpu.VMEM
    scratch = [
        vmem((2, ROWS, COLS, CH), BF16),
        vmem((ROWS, COLS, CH), BF16),
        vmem((ROWS, COLS, CH), F32),
        vmem((2, DEV, 2 * ROWS, COLS), BF16),
        vmem((2, N_COL, N_ROW, 2 * ROWS, COLS), BF16),
        vmem((2, N_ROW, ROWS, 512), BF16),
        vmem((2, 4, 512, 256), F32),
        vmem(planes, BF16),
        vmem(pieces, BF16),
    ]
    scratch += [vmem(a.shape, a.dtype) for a in args[1:]]
    scratch += [
        vmem((2, 4 * CH, CH), BF16),
        vmem((2, CH, CH), F32),
        vmem((2, CH, CH), F32),
        vmem((CH * GROUP, COLS), F32),
        vmem((CH * GROUP, COLS), F32),
        vmem((GROUP, COLS), F32),
        pltpu.SemaphoreType.DMA((ROWS // GROUP,)),
        pltpu.SemaphoreType.DMA((7,)),
        pltpu.SemaphoreType.DMA((FLIGHTS,)),
        pltpu.SemaphoreType.DMA((FLIGHTS,)),
        pltpu.SemaphoreType.DMA((3,)),
    ]
    return pl.pallas_call(
        kernel,
        out_shape=jax.ShapeDtypeStruct((ROWS, COLS, CH), BF16),
        in_specs=[pl.BlockSpec(memory_space=pl.ANY)] * 8,
        out_specs=pl.BlockSpec(memory_space=pl.ANY),
        scratch_shapes=scratch,
        compiler_params=pltpu.CompilerParams(
            collective_id=0, has_side_effects=True, vmem_limit_bytes=60 * MIB
        ),
        name="triangle",
    )(*args)


def solution(mesh):
    placed = (P("row", "col", None), P(), P(), P(), P(), P(), P(), P())
    return jax.shard_map(
        shards, mesh=mesh, in_specs=placed, out_specs=P("row", "col", None), check_vma=False
    )
```

```python
import jax
import jax.numpy as jnp
from jax import lax
from jax.experimental import pallas as pl
from jax.experimental.pallas import tpu as pltpu
from jax.sharding import PartitionSpec as P

F32, BF16 = jnp.float32, jnp.bfloat16
ROWS, COLS, N_ROW, N_COL, CH = 64, 128, 16, 8, 128
DEV = N_ROW * N_COL
GROUP, HALF = 16, 32
MIB = 1 << 20
NT = (((1,), (1,)), ((), ()))
TN = (((0,), (0,)), ((), ()))
NN = (((1,), (0,)), ((), ()))
RIGHT, LEFT = 0, 1
PLACE = (
    {(k, half, g): 64 * k + 32 * half + 16 * g for k in range(2) for half in range(2) for g in range(2)},
    {
        (RIGHT, 0, 0): 0,
        (RIGHT, 0, 1): 16,
        (LEFT, 0, 0): 32,
        (RIGHT, 1, 0): 48,
        (RIGHT, 1, 1): 64,
        (LEFT, 1, 0): 80,
        (LEFT, 0, 1): 96,
        (LEFT, 1, 1): 112,
    },
)
SIDES = (
    (0, 0, 16), (0, 16, 16), (0, 32, 32), (0, 64, 32), (0, 96, 32),
    (1, 0, 32), (1, 32, 16), (1, 48, 48), (1, 96, 32),
)
ORDER = (
    (3, 3), (3, 1), (0, 1), (2, 3), (0, 0), (2, 2), (2, 0), (0, 2),
    (1, 2), (1, 0), (1, 1), (1, 3), (3, 2), (3, 0), (0, 3), (2, 1),
)
MIXED = ((0, 0, 32), (0, 32, 32), (1, 0, 32), (1, 32, 16), (1, 48, 16))
FLIGHTS = len(SIDES) + len(MIXED)


def sigmoid(v):
    return 0.5 * jnp.tanh(0.5 * v) + 0.5


def layer_norm(v, gain, bias):
    mean = jnp.mean(v, axis=-1, keepdims=True)
    centred = v - mean
    var = jnp.mean(centred * centred, axis=-1, keepdims=True)
    return centred * lax.rsqrt(var + 1e-5) * gain + bias


def dot(a, b, dims):
    return lax.dot_general(a, b, dims, preferred_element_type=F32)


def each_target(row, col, body):
    y, zh, k = row // 4, lax.rem(row // 2, 2), lax.rem(row, 2)
    x, zl = col // 2, lax.rem(col, 2)
    sign = 1 - 2 * k
    turns = [sign * a + 4 for a in range(4)]
    xs = [lax.rem(x + turn, 4) * 2 for turn in turns]
    ys = [lax.rem(y + turn, 4) * 4 for turn in turns]

    def sixteen(core, c, skip):
        core_at = lax.rem(k + core, 2)
        z = [lax.rem(zh * 2 + zl + sign * c + 4 + turn, 4) for turn in turns]
        z_rows = [(at // 2) * 2 + core_at for at in z]
        z_cols = [lax.rem(at, 2) for at in z]
        for dx, dyz in ORDER:
            if not (skip and dx == 0 and dyz == 0):
                body(ys[dyz] + z_rows[dyz], xs[dx] + z_cols[dyz])

    def step(p, carry):
        sixteen(p // 4, lax.rem(p, 4), False)
        return carry

    sixteen(0, 0, True)
    lax.fori_loop(1, 8, step, 0)


def kernel(
    pair_h, ng_h, nb_h, pw_h, gw_h, og_h, ob_h, ow_h, out_h,
    cur, normed, gate, sides, all_sides, lt, acc, m_all, m_in,
    ng, nb, pw, gw, og, ob, ow, wt, gain_t, bias_t, tl, tr, ts,
    load_sem, param_sem, send_sem, recv_sem, out_sem,
):
    row, col = lax.axis_index("row"), lax.axis_index("col")
    me = row * N_COL + col

    def load(g):
        rows = pl.ds(g * GROUP, GROUP)
        return pltpu.make_async_copy(pair_h.at[rows], cur.at[0, rows], load_sem.at[g])

    params = [
        pltpu.make_async_copy(src, dst, param_sem.at[k])
        for k, (src, dst) in enumerate(
            ((pw_h, pw), (ng_h, ng), (nb_h, nb), (gw_h, gw), (og_h, og), (ob_h, ob), (ow_h, ow))
        )
    ]
    load(0).start()
    for copy in params:
        copy.start()
    for g in range(1, ROWS // GROUP):
        load(g).start()

    barrier = pltpu.get_barrier_semaphore()

    def greet(r, c):
        pl.semaphore_signal(
            barrier, inc=1, device_id=(r, c), device_id_type=pl.DeviceIdType.MESH
        )

    each_target(row, col, greet)
    for copy in params:
        copy.wait()
    for k in range(2, 4):
        wt[0, k * CH : (k + 1) * CH] = pw[0, k].T

    def norm_rows(u, base):
        x = cur[u, pl.ds(base, 2)].reshape(2 * COLS, CH).astype(F32)
        n = layer_norm(x, ng[u : u + 1], nb[u : u + 1]).astype(BF16)
        normed[pl.ds(base, 2)] = n.reshape(2, COLS, CH)
        return n

    def project(u, k, n):
        first = 256 * (1 - k)
        p = dot(wt[u, first : first + 256], n, NT)
        return sigmoid(p[0:128]) * p[128:256]

    def keep(u, k, half, g, wide):
        first = PLACE[u][k, half, 0] + g * GROUP
        if (u, k) == (1, LEFT):
            first = PLACE[u][k, half, g]
        rows = pl.ds(pl.multiple_of(first, GROUP), GROUP)
        sides[u, :, rows, :] = wide[...].reshape(CH, GROUP, COLS).astype(BF16)

    def front_group(u, k, half, g, fresh=True):
        base = half * HALF + g * GROUP
        for i in range(0, GROUP, 2):
            if fresh:
                n = norm_rows(u, base + i)
            else:
                n = normed[pl.ds(base + i, 2)].reshape(2 * COLS, CH)
            side = project(u, k, n)
            for r in range(2):
                (tr, tl)[k][pl.ds(i + r, CH, stride=GROUP), :] = side[:, r * COLS : (r + 1) * COLS]
        keep(u, k, half, g, (tr, tl)[k])

    def left_by_parts(half):
        def eight(p):
            for q in range(8):
                rows = [half * HALF + p * 8 + q + r * GROUP for r in range(2)]
                order = [(r, c) for part in range(2) for r in rows for c in (part, part + 2)]
                n = jnp.concatenate([normed[r, c * 32 : (c + 1) * 32] for r, c in order], axis=0)
                side = project(1, LEFT, n)
                for part, wide in enumerate((tl, tr)):
                    wide[pl.ds(p * 8 + q, CH, stride=GROUP), :] = side[
                        :, part * COLS : (part + 1) * COLS
                    ]

        loop(2, eight)
        keep(1, LEFT, half, 0, tl)
        keep(1, LEFT, half, 1, tr)

    def gate_rows(u, step):
        n = normed[pl.ds(step * 4, 4)].reshape(4 * COLS, CH)
        gate[pl.ds(step * 4, 4)] = sigmoid(dot(n, gw[u], NN)).reshape(4, COLS, CH)

    def back_group(u, g):
        base = g * GROUP
        m = m_in[u, :, pl.ds(pl.multiple_of(base, GROUP), GROUP), :].astype(F32)
        mean = jnp.mean(m, axis=0)
        centred = m - mean[None]
        var = jnp.mean(centred * centred, axis=0)
        ts[...] = lax.rsqrt(var + 1e-5)
        tl[...] = centred.reshape(CH * GROUP, COLS)
        for i in range(GROUP):
            c = tl[pl.ds(i, CH, stride=GROUP), :]
            nm = (c * ts[pl.ds(i, 1), :] * gain_t[u] + bias_t[u]).astype(BF16)
            change = dot(nm, ow[u], TN)
            now = cur[u, base + i].astype(F32) + gate[base + i] * change
            cur[1 - u, base + i] = now.astype(BF16)

    def loop(count, body):
        def step(i, carry):
            body(i)
            return carry

        lax.fori_loop(0, count, step, 0)

    def flight_of(flight):
        if flight < len(SIDES):
            u, first, rows = SIDES[flight]
            part = pl.ds(first, rows)
            dst = all_sides.at[u, col, row, part]
            return lambda r, c: sides.at[u, r * N_COL + c, part], dst, rows
        u, first, rows = MIXED[flight - len(SIDES)]
        part = pl.ds(first, rows)
        return lambda r, c: m_all.at[u, c, r, part], m_in.at[u, me, part], rows

    def spread(flight):
        src_at, dst, _ = flight_of(flight)
        pltpu.make_async_copy(src_at(row, col), dst, recv_sem.at[flight]).start()

        def send(r, c):
            pltpu.make_async_remote_copy(
                src_ref=src_at(r, c),
                dst_ref=dst,
                send_sem=send_sem.at[flight],
                recv_sem=recv_sem.at[flight],
                device_id=(r, c),
                device_id_type=pl.DeviceIdType.MESH,
            ).start()

        each_target(row, col, send)

    def arrived(flight):
        size = m_in.at[0, :, pl.ds(0, flight_of(flight)[2])]
        pltpu.make_async_copy(size, size, recv_sem.at[flight]).wait()

    def sent(flight):
        size = m_in.at[0, pl.ds(0, DEV - 1), pl.ds(0, flight_of(flight)[2])]
        pltpu.make_async_copy(size, size, send_sem.at[flight]).wait()

    def put_mixed(u, half, jb, out):
        out = out.astype(BF16)
        for k in range(2):
            m_all[u, 2 * jb + k, :, pl.ds(half * HALF, HALF), :] = out[
                :, k * COLS : (k + 1) * COLS
            ].reshape(N_ROW, HALF, COLS)

    def side_rows(u, c, k, half, part, rows=GROUP):
        first = PLACE[u][k, half, part]
        return all_sides[u, c, :, first : first + rows, :].reshape(N_ROW * rows, COLS)

    def mix_outgoing(half):
        a = jnp.concatenate(
            [
                side_rows(0, c, LEFT, half, 0, HALF)
                for c in range(N_COL)
            ],
            axis=1,
        )

        def block(jb):
            b = jnp.concatenate(
                [all_sides[0, c, pl.ds(4 * jb, 4), 0:64].reshape(256, COLS) for c in range(N_COL)],
                axis=1,
            )
            put_mixed(0, half, jb, dot(a, b, NT))

        loop(4, block)

    def turn(half, part):
        def block(c):
            t = side_rows(1, c, LEFT, half, part).T
            for r in range(2):
                lt[half, pl.ds(2 * c, 2), part * HALF : (part + 1) * HALF, r * 256 : r * 256 + 256] = (
                    t[r * 64 : (r + 1) * 64].reshape(2, HALF, 256)
                )

        loop(N_COL, block)

    def mix_incoming(half, k):
        a = lt[k, :, half * HALF : (half + 1) * HALF, :].reshape(512, 512)

        def block(jb):
            b = jnp.concatenate(
                [
                    jnp.concatenate(
                        [
                            side_rows(1, 2 * jb + c, RIGHT, k, r) for r in range(2)
                        ],
                        axis=0,
                    )
                    for c in range(2)
                ],
                axis=1,
            )
            if k == 0:
                acc[half, jb] = dot(a, b, NN)
            else:
                put_mixed(1, half, jb, acc[half, jb] + dot(a, b, NN))

        loop(4, block)

    load(0).wait()
    front_group(0, RIGHT, 0, 0)
    pl.semaphore_wait(barrier, DEV - 1)
    spread(0)
    load(1).wait()
    front_group(0, RIGHT, 0, 1)
    spread(1)
    load(2).wait()
    load(3).wait()
    loop(2, lambda g: front_group(0, RIGHT, 1, g))
    spread(2)
    for k in range(2):
        wt[0, k * CH : (k + 1) * CH] = pw[0, k].T
    for half in range(2):
        loop(2, lambda g: front_group(0, LEFT, half, g, False))
        spread(3 + half)
    for k in range(4):
        wt[1, k * CH : (k + 1) * CH] = pw[1, k].T
    for u in range(2):
        gain_t[u] = jnp.broadcast_to(og[u : u + 1], (CH, CH)).T
        bias_t[u] = jnp.broadcast_to(ob[u : u + 1], (CH, CH)).T
    loop(ROWS // 4, lambda s: gate_rows(0, s))
    for flight in range(3):
        arrived(flight)
    for half in range(2):
        arrived(3 + half)
        mix_outgoing(half)
        spread(9 + half)
    for half in range(2):
        arrived(9 + half)

        def turnover(g):
            back_group(0, 2 * half + g)
            front_group(1, RIGHT, half, g)

        loop(2, turnover)
        if half == 0:
            spread(5)
        left_by_parts(half)
        spread(6 + half)
    spread(8)
    loop(ROWS // 4, lambda s: gate_rows(1, s))
    arrived(5)
    arrived(6)
    turn(0, 0)
    mix_incoming(0, 0)
    arrived(7)
    turn(1, 0)
    mix_incoming(0, 1)
    spread(11)
    arrived(8)
    for k in range(2):
        turn(k, 1)
        mix_incoming(1, k)
    spread(12)
    spread(13)

    def store(k, first, count):
        rows = pl.ds(first, count)
        return pltpu.make_async_copy(cur.at[0, rows], out_h.at[rows], out_sem.at[k])

    stores = [store(0, 0, HALF), store(1, HALF, GROUP), store(2, HALF + GROUP, GROUP)]
    arrived(11)
    loop(2, lambda g: back_group(1, g))
    stores[0].start()
    for quarter in range(2):
        arrived(12 + quarter)
        loop(1, lambda g: back_group(1, 2 + quarter))
        stores[1 + quarter].start()
    for flight in range(FLIGHTS):
        sent(flight)
    for copy in stores:
        copy.wait()


def shards(*args):
    pieces = (2, DEV, ROWS, COLS)
    planes = (2, N_COL, N_ROW, ROWS, COLS)
    vmem = pltpu.VMEM
    scratch = [
        vmem((2, ROWS, COLS, CH), BF16),
        vmem((ROWS, COLS, CH), BF16),
        vmem((ROWS, COLS, CH), F32),
        vmem((2, DEV, 2 * ROWS, COLS), BF16),
        vmem((2, N_COL, N_ROW, 2 * ROWS, COLS), BF16),
        vmem((2, N_ROW, ROWS, 512), BF16),
        vmem((2, 4, 512, 256), F32),
        vmem(planes, BF16),
        vmem(pieces, BF16),
    ]
    scratch += [vmem(a.shape, a.dtype) for a in args[1:]]
    scratch += [
        vmem((2, 4 * CH, CH), BF16),
        vmem((2, CH, CH), F32),
        vmem((2, CH, CH), F32),
        vmem((CH * GROUP, COLS), F32),
        vmem((CH * GROUP, COLS), F32),
        vmem((GROUP, COLS), F32),
        pltpu.SemaphoreType.DMA((ROWS // GROUP,)),
        pltpu.SemaphoreType.DMA((7,)),
        pltpu.SemaphoreType.DMA((FLIGHTS,)),
        pltpu.SemaphoreType.DMA((FLIGHTS,)),
        pltpu.SemaphoreType.DMA((3,)),
    ]
    return pl.pallas_call(
        kernel,
        out_shape=jax.ShapeDtypeStruct((ROWS, COLS, CH), BF16),
        in_specs=[pl.BlockSpec(memory_space=pl.ANY)] * 8,
        out_specs=pl.BlockSpec(memory_space=pl.ANY),
        scratch_shapes=scratch,
        compiler_params=pltpu.CompilerParams(
            collective_id=0, has_side_effects=True, vmem_limit_bytes=60 * MIB
        ),
        name="triangle",
    )(*args)


def solution(mesh):
    placed = (P("row", "col", None), P(), P(), P(), P(), P(), P(), P())
    return jax.shard_map(
        shards, mesh=mesh, in_specs=placed, out_specs=P("row", "col", None), check_vma=False
    )
```

```python
import jax
import jax.numpy as jnp
from jax import lax
from jax.experimental import pallas as pl
from jax.experimental.pallas import tpu as pltpu
from jax.sharding import PartitionSpec as P

F32, BF16 = jnp.float32, jnp.bfloat16
ROWS, COLS, N_ROW, N_COL, CH = 64, 128, 16, 8, 128
DEV = N_ROW * N_COL
GROUP, HALF = 16, 32
MIB = 1 << 20
NT = (((1,), (1,)), ((), ()))
TN = (((0,), (0,)), ((), ()))
NN = (((1,), (0,)), ((), ()))
RIGHT, LEFT = 0, 1
PLACE = (
    {(k, half, g): 64 * k + 32 * half + 16 * g for k in range(2) for half in range(2) for g in range(2)},
    {
        (RIGHT, 0, 0): 0,
        (RIGHT, 0, 1): 16,
        (LEFT, 0, 0): 32,
        (RIGHT, 1, 0): 48,
        (RIGHT, 1, 1): 64,
        (LEFT, 1, 0): 80,
        (LEFT, 0, 1): 96,
        (LEFT, 1, 1): 112,
    },
)
SIDES = (
    (0, 0, 16), (0, 16, 16), (0, 32, 32), (0, 64, 32), (0, 96, 32),
    (1, 0, 32), (1, 32, 16), (1, 48, 48), (1, 96, 32),
)
MIXED = ((0, 0, 32), (0, 32, 32), (1, 0, 32), (1, 32, 16), (1, 48, 16))
FLIGHTS = len(SIDES) + len(MIXED)


def sigmoid(v):
    return 0.5 * jnp.tanh(0.5 * v) + 0.5


def layer_norm(v, gain, bias):
    mean = jnp.mean(v, axis=-1, keepdims=True)
    centred = v - mean
    var = jnp.mean(centred * centred, axis=-1, keepdims=True)
    return centred * lax.rsqrt(var + 1e-5) * gain + bias


def dot(a, b, dims):
    return lax.dot_general(a, b, dims, preferred_element_type=F32)


def each_target(row, col, body):
    y, zh, k = row // 4, lax.rem(row // 2, 2), lax.rem(row, 2)
    x, zl = col // 2, lax.rem(col, 2)
    sign = 1 - 2 * k
    turns = [sign * a + 4 for a in range(4)]
    xs = [lax.rem(x + turn, 4) * 2 for turn in turns]
    ys = [lax.rem(y + turn, 4) * 4 for turn in turns]

    def sixteen(core, c, skip):
        core_at = lax.rem(k + core, 2)
        z = [lax.rem(zh * 2 + zl + sign * c + 4 + turn, 4) for turn in turns]
        z_rows = [(at // 2) * 2 + core_at for at in z]
        z_cols = [lax.rem(at, 2) for at in z]
        for b in range(4):
            for a in range(4):
                if not (skip and a == 0 and b == 0):
                    ab = (a + b) % 4
                    body(ys[ab] + z_rows[ab], xs[a] + z_cols[ab])

    def step(p, carry):
        sixteen(p // 4, lax.rem(p, 4), False)
        return carry

    sixteen(0, 0, True)
    lax.fori_loop(1, 8, step, 0)


def back_rows(mixed, cur, gate, new, gain_t, bias_t, weight, tl, ts):
    m = mixed.astype(F32)
    mean = jnp.mean(m, axis=0)
    centred = m - mean[None]
    var = jnp.mean(centred * centred, axis=0)
    ts[...] = lax.rsqrt(var + 1e-5)
    tl[...] = centred.reshape(CH * GROUP, COLS)
    for i in range(GROUP):
        c = tl[pl.ds(i, CH, stride=GROUP), :]
        nm = (c * ts[pl.ds(i, 1), :] * gain_t[...] + bias_t[...]).astype(BF16)
        change = dot(nm, weight[...], TN)
        new[i] = (cur[i].astype(F32) + gate[i] * change).astype(BF16)


def kernel(
    pair_h, ng_h, nb_h, pw_h, gw_h, og_h, ob_h, ow_h, out_h, last_mixed, last_gate, last_cur,
    cur, normed, gate, sides, all_sides, lt, acc, m_all, m_in,
    ng, nb, pw, gw, og, ob, ow, wt, gain_t, bias_t, tl, tr, ts,
    load_sem, param_sem, send_sem, recv_sem, out_sem, ahead_sem,
):
    row, col = lax.axis_index("row"), lax.axis_index("col")
    me = row * N_COL + col

    def load(g):
        rows = pl.ds(g * GROUP, GROUP)
        return pltpu.make_async_copy(pair_h.at[rows], cur.at[0, rows], load_sem.at[g])

    first = pl.ds(2, 2)
    params = [
        pltpu.make_async_copy(src, dst, param_sem.at[k])
        for k, (src, dst) in enumerate(
            (
                (pw_h.at[0, first], pw.at[0, first]),
                (ng_h, ng),
                (nb_h, nb),
                (pw_h.at[0, pl.ds(0, 2)], pw.at[0, pl.ds(0, 2)]),
                (pw_h.at[1], pw.at[1]),
                (gw_h, gw),
                (og_h, og),
                (ob_h, ob),
                (ow_h, ow),
            )
        )
    ]
    load(0).start()
    for copy in params[:3]:
        copy.start()
    for g in range(1, ROWS // GROUP):
        load(g).start()
    for copy in params[3:]:
        copy.start()

    barrier = pltpu.get_barrier_semaphore()

    def greet(r, c):
        pl.semaphore_signal(
            barrier, inc=1, device_id=(r, c), device_id_type=pl.DeviceIdType.MESH
        )

    each_target(row, col, greet)
    for copy in params[:3]:
        copy.wait()
    for k in range(2, 4):
        wt[0, k * CH : (k + 1) * CH] = pw[0, k].T

    def norm_rows(u, base):
        x = cur[u, pl.ds(base, 2)].reshape(2 * COLS, CH).astype(F32)
        n = layer_norm(x, ng[u : u + 1], nb[u : u + 1]).astype(BF16)
        normed[pl.ds(base, 2)] = n.reshape(2, COLS, CH)
        return n

    def project(u, k, n):
        first = 256 * (1 - k)
        p = dot(wt[u, first : first + 256], n, NT)
        return sigmoid(p[0:128]) * p[128:256]

    def keep(u, k, half, g, wide):
        first = PLACE[u][k, half, 0] + g * GROUP
        if (u, k) == (1, LEFT):
            first = PLACE[u][k, half, g]
        rows = pl.ds(pl.multiple_of(first, GROUP), GROUP)
        sides[u, :, rows, :] = wide[...].reshape(CH, GROUP, COLS).astype(BF16)

    def front_group(u, k, half, g, fresh=True):
        base = half * HALF + g * GROUP
        for i in range(0, GROUP, 2):
            if fresh:
                n = norm_rows(u, base + i)
            else:
                n = normed[pl.ds(base + i, 2)].reshape(2 * COLS, CH)
            side = project(u, k, n)
            for r in range(2):
                (tr, tl)[k][pl.ds(i + r, CH, stride=GROUP), :] = side[:, r * COLS : (r + 1) * COLS]
        keep(u, k, half, g, (tr, tl)[k])

    def left_by_parts(half):
        def eight(p):
            for q in range(8):
                rows = [half * HALF + p * 8 + q + r * GROUP for r in range(2)]
                order = [(r, c) for part in range(2) for r in rows for c in (part, part + 2)]
                n = jnp.concatenate([normed[r, c * 32 : (c + 1) * 32] for r, c in order], axis=0)
                side = project(1, LEFT, n)
                for part, wide in enumerate((tl, tr)):
                    wide[pl.ds(p * 8 + q, CH, stride=GROUP), :] = side[
                        :, part * COLS : (part + 1) * COLS
                    ]

        loop(2, eight)
        keep(1, LEFT, half, 0, tl)
        keep(1, LEFT, half, 1, tr)

    def gate_rows(u, step):
        n = normed[pl.ds(step * 4, 4)].reshape(4 * COLS, CH)
        gate[pl.ds(step * 4, 4)] = sigmoid(dot(n, gw[u], NN)).reshape(4, COLS, CH)

    def back_group(u, g):
        base = g * GROUP
        back_rows(
            m_in[u, :, pl.ds(pl.multiple_of(base, GROUP), GROUP), :],
            cur.at[u, pl.ds(base, GROUP)],
            gate.at[pl.ds(base, GROUP)],
            cur.at[1 - u, pl.ds(base, GROUP)],
            gain_t.at[u], bias_t.at[u], ow.at[u], tl, ts,
        )

    def loop(count, body):
        def step(i, carry):
            body(i)
            return carry

        lax.fori_loop(0, count, step, 0)

    def flight_of(flight):
        if flight < len(SIDES):
            u, first, rows = SIDES[flight]
            part = pl.ds(first, rows)
            dst = all_sides.at[u, col, row, part]
            return lambda r, c: sides.at[u, r * N_COL + c, part], dst, rows
        u, first, rows = MIXED[flight - len(SIDES)]
        part = pl.ds(first, rows)
        dst = last_mixed.at[me] if flight == FLIGHTS - 1 else m_in.at[u, me, part]
        return lambda r, c: m_all.at[u, c, r, part], dst, rows

    def spread(flight):
        src_at, dst, _ = flight_of(flight)
        pltpu.make_async_copy(src_at(row, col), dst, recv_sem.at[flight]).start()

        def send(r, c):
            pltpu.make_async_remote_copy(
                src_ref=src_at(r, c),
                dst_ref=dst,
                send_sem=send_sem.at[flight],
                recv_sem=recv_sem.at[flight],
                device_id=(r, c),
                device_id_type=pl.DeviceIdType.MESH,
            ).start()

        each_target(row, col, send)

    def arrived(flight):
        size = m_in.at[0, :, pl.ds(0, flight_of(flight)[2])]
        pltpu.make_async_copy(size, size, recv_sem.at[flight]).wait()

    def sent(flight):
        size = m_in.at[0, pl.ds(0, DEV - 1), pl.ds(0, flight_of(flight)[2])]
        pltpu.make_async_copy(size, size, send_sem.at[flight]).wait()

    def put_mixed(u, half, jb, out):
        out = out.astype(BF16)
        for k in range(2):
            m_all[u, 2 * jb + k, :, pl.ds(half * HALF, HALF), :] = out[
                :, k * COLS : (k + 1) * COLS
            ].reshape(N_ROW, HALF, COLS)

    def side_rows(u, c, k, half, part, rows=GROUP):
        first = PLACE[u][k, half, part]
        return all_sides[u, c, :, first : first + rows, :].reshape(N_ROW * rows, COLS)

    def mix_outgoing(half):
        a = jnp.concatenate(
            [
                side_rows(0, c, LEFT, half, 0, HALF)
                for c in range(N_COL)
            ],
            axis=1,
        )

        def block(jb):
            b = jnp.concatenate(
                [all_sides[0, c, pl.ds(4 * jb, 4), 0:64].reshape(256, COLS) for c in range(N_COL)],
                axis=1,
            )
            put_mixed(0, half, jb, dot(a, b, NT))

        loop(4, block)

    def turn(half, part):
        def block(c):
            t = side_rows(1, c, LEFT, half, part).T
            for r in range(2):
                lt[half, pl.ds(2 * c, 2), part * HALF : (part + 1) * HALF, r * 256 : r * 256 + 256] = (
                    t[r * 64 : (r + 1) * 64].reshape(2, HALF, 256)
                )

        loop(N_COL, block)

    def mix_incoming(half, k):
        a = lt[k, :, half * HALF : (half + 1) * HALF, :].reshape(512, 512)

        def block(jb):
            b = jnp.concatenate(
                [
                    jnp.concatenate(
                        [
                            side_rows(1, 2 * jb + c, RIGHT, k, r) for r in range(2)
                        ],
                        axis=0,
                    )
                    for c in range(2)
                ],
                axis=1,
            )
            if k == 0:
                acc[half, jb] = dot(a, b, NN)
            else:
                put_mixed(1, half, jb, acc[half, jb] + dot(a, b, NN))

        loop(4, block)

    load(0).wait()
    front_group(0, RIGHT, 0, 0)
    pl.semaphore_wait(barrier, DEV - 1)
    spread(0)
    for copy in params[3:]:
        copy.wait()
    load(1).wait()
    front_group(0, RIGHT, 0, 1)
    spread(1)
    load(2).wait()
    load(3).wait()
    loop(2, lambda g: front_group(0, RIGHT, 1, g))
    spread(2)
    for k in range(2):
        wt[0, k * CH : (k + 1) * CH] = pw[0, k].T
    for half in range(2):
        loop(2, lambda g: front_group(0, LEFT, half, g, False))
        spread(3 + half)
    for k in range(4):
        wt[1, k * CH : (k + 1) * CH] = pw[1, k].T
    for u in range(2):
        gain_t[u] = jnp.broadcast_to(og[u : u + 1], (CH, CH)).T
        bias_t[u] = jnp.broadcast_to(ob[u : u + 1], (CH, CH)).T
    loop(ROWS // 4, lambda s: gate_rows(0, s))
    for flight in range(3):
        arrived(flight)
    for half in range(2):
        arrived(3 + half)
        mix_outgoing(half)
        spread(9 + half)
    for half in range(2):
        arrived(9 + half)

        def turnover(g):
            back_group(0, 2 * half + g)
            front_group(1, RIGHT, half, g)

        loop(2, turnover)
        if half == 0:
            spread(5)
        left_by_parts(half)
        spread(6 + half)
    spread(8)
    loop(ROWS // 4, lambda s: gate_rows(1, s))
    last = pl.ds(HALF + GROUP, GROUP)
    ahead = [
        pltpu.make_async_copy(src, dst, ahead_sem.at[k])
        for k, (src, dst) in enumerate(((gate.at[last], last_gate), (cur.at[1, last], last_cur)))
    ]
    for copy in ahead:
        copy.start()
    arrived(5)
    arrived(6)
    turn(0, 0)
    mix_incoming(0, 0)
    arrived(7)
    turn(1, 0)
    mix_incoming(0, 1)
    spread(11)
    arrived(8)
    for k in range(2):
        turn(k, 1)
        mix_incoming(1, k)
    spread(12)
    spread(13)

    def store(k, first, count):
        rows = pl.ds(first, count)
        return pltpu.make_async_copy(cur.at[0, rows], out_h.at[rows], out_sem.at[k])

    stores = [store(0, 0, HALF), store(1, HALF, GROUP)]
    arrived(11)
    loop(2, lambda g: back_group(1, g))
    stores[0].start()
    arrived(12)
    loop(1, lambda g: back_group(1, 2))
    stores[1].start()
    for flight in range(FLIGHTS):
        sent(flight)
    for copy in ahead + stores:
        copy.wait()
    arrived(13)


def finish(
    done_h, mixed_h, gate_h, cur_h, og_h, ob_h, ow_h, out_h,
    done, mixed, gate, cur, og, ob, ow, new, gain_t, bias_t, tl, ts, sem, out_sem,
):
    loads = [
        pltpu.make_async_copy(src, dst, sem.at[k])
        for k, (src, dst) in enumerate(
            (
                (mixed_h, mixed), (og_h, og), (ob_h, ob), (ow_h, ow), (cur_h, cur), (gate_h, gate),
                *((done_h.at[pl.ds(g * 16, 16)], done.at[pl.ds(g * 16, 16)]) for g in range(3)),
            )
        )
    ]
    for copy in loads:
        copy.start()
    for copy in loads[1:4]:
        copy.wait()
    gain_t[...] = jnp.broadcast_to(og[1:2], (CH, CH)).T
    bias_t[...] = jnp.broadcast_to(ob[1:2], (CH, CH)).T
    carried = [
        pltpu.make_async_copy(
            done.at[pl.ds(g * 16, 16)], out_h.at[pl.ds(g * 16, 16)], out_sem.at[g]
        )
        for g in range(3)
    ]
    for copy in (loads[0], loads[4], loads[5]):
        copy.wait()
    for g in range(3):
        loads[6 + g].wait()
        carried[g].start()
    back_rows(mixed[...], cur, gate, new, gain_t, bias_t, ow.at[1], tl, ts)
    end = pltpu.make_async_copy(new, out_h.at[pl.ds(48, 16)], out_sem.at[3])
    end.start()
    for copy in (*carried, end):
        copy.wait()


def shards(*args):
    pieces = (2, DEV, ROWS, COLS)
    planes = (2, N_COL, N_ROW, ROWS, COLS)
    vmem = pltpu.VMEM
    scratch = [
        vmem((2, ROWS, COLS, CH), BF16),
        vmem((ROWS, COLS, CH), BF16),
        vmem((ROWS, COLS, CH), F32),
        vmem((2, DEV, 2 * ROWS, COLS), BF16),
        vmem((2, N_COL, N_ROW, 2 * ROWS, COLS), BF16),
        vmem((2, N_ROW, ROWS, 512), BF16),
        vmem((2, 4, 512, 256), F32),
        vmem(planes, BF16),
        vmem(pieces, BF16),
    ]
    scratch += [vmem(a.shape, a.dtype) for a in args[1:]]
    scratch += [
        vmem((2, 4 * CH, CH), BF16),
        vmem((2, CH, CH), F32),
        vmem((2, CH, CH), F32),
        vmem((CH * GROUP, COLS), F32),
        vmem((CH * GROUP, COLS), F32),
        vmem((GROUP, COLS), F32),
        pltpu.SemaphoreType.DMA((ROWS // GROUP,)),
        pltpu.SemaphoreType.DMA((9,)),
        pltpu.SemaphoreType.DMA((FLIGHTS,)),
        pltpu.SemaphoreType.DMA((FLIGHTS,)),
        pltpu.SemaphoreType.DMA((2,)),
        pltpu.SemaphoreType.DMA((2,)),
    ]
    quarter = (GROUP, COLS, CH)
    of_kernel = [
        jax.ShapeDtypeStruct((ROWS - GROUP, COLS, CH), BF16),
        jax.ShapeDtypeStruct((DEV, GROUP, COLS), BF16),
        jax.ShapeDtypeStruct(quarter, F32),
        jax.ShapeDtypeStruct(quarter, BF16),
    ]
    parts = pl.pallas_call(
        kernel,
        out_shape=of_kernel,
        in_specs=[pl.BlockSpec(memory_space=pl.ANY)] * 8,
        out_specs=[pl.BlockSpec(memory_space=pl.ANY)] * 4,
        scratch_shapes=scratch,
        compiler_params=pltpu.CompilerParams(
            collective_id=0, has_side_effects=True, vmem_limit_bytes=60 * MIB
        ),
        name="triangle",
    )(*args)
    ends = args[5:]
    return pl.pallas_call(
        finish,
        out_shape=jax.ShapeDtypeStruct((ROWS, COLS, CH), BF16),
        in_specs=[pl.BlockSpec(memory_space=pl.ANY)] * 7,
        out_specs=pl.BlockSpec(memory_space=pl.ANY),
        scratch_shapes=[vmem(a.shape, a.dtype) for a in (*of_kernel, *ends)]
        + [
            vmem(quarter, BF16),
            vmem((CH, CH), F32),
            vmem((CH, CH), F32),
            vmem((CH * GROUP, COLS), F32),
            vmem((GROUP, COLS), F32),
            pltpu.SemaphoreType.DMA((9,)),
            pltpu.SemaphoreType.DMA((4,)),
        ],
        compiler_params=pltpu.CompilerParams(vmem_limit_bytes=60 * MIB),
        name="finish",
    )(*parts, *ends)


def solution(mesh):
    placed = (P("row", "col", None), P(), P(), P(), P(), P(), P(), P())
    return jax.shard_map(
        shards, mesh=mesh, in_specs=placed, out_specs=P("row", "col", None), check_vma=False
    )
```

```python
import jax
import jax.numpy as jnp
from jax import lax
from jax.experimental import pallas as pl
from jax.experimental.pallas import tpu as pltpu
from jax.sharding import PartitionSpec as P

F32, BF16 = jnp.float32, jnp.bfloat16
ROWS, COLS, N_ROW, N_COL, CH = 64, 128, 16, 8, 128
DEV = N_ROW * N_COL
GROUP, HALF = 16, 32
MIB = 1 << 20
NT = (((1,), (1,)), ((), ()))
TN = (((0,), (0,)), ((), ()))
NN = (((1,), (0,)), ((), ()))
RIGHT, LEFT = 0, 1
PLACE = (
    {(k, half, g): 64 * k + 32 * half + 16 * g for k in range(2) for half in range(2) for g in range(2)},
    {
        (RIGHT, 0, 0): 0,
        (RIGHT, 0, 1): 16,
        (LEFT, 0, 0): 32,
        (RIGHT, 1, 0): 48,
        (RIGHT, 1, 1): 64,
        (LEFT, 1, 0): 80,
        (LEFT, 0, 1): 96,
        (LEFT, 1, 1): 112,
    },
)
SIDES = (
    (0, 0, 16), (0, 16, 16), (0, 32, 32), (0, 64, 32), (0, 96, 32),
    (1, 0, 16), (1, 16, 16), (1, 32, 16), (1, 48, 32), (1, 80, 16), (1, 96, 16), (1, 112, 16),
)
MIXED = ((0, 0, 16), (0, 16, 16), (0, 32, 16), (0, 48, 16), (1, 0, 32), (1, 32, 16), (1, 48, 16))
FLIGHTS = len(SIDES) + len(MIXED)


def sigmoid(v):
    return 0.5 * jnp.tanh(0.5 * v) + 0.5


def layer_norm(v, gain, bias):
    mean = jnp.mean(v, axis=-1, keepdims=True)
    centred = v - mean
    var = jnp.mean(centred * centred, axis=-1, keepdims=True)
    return centred * lax.rsqrt(var + 1e-5) * gain + bias


def dot(a, b, dims):
    return lax.dot_general(a, b, dims, preferred_element_type=F32)


def each_target(row, col, body):
    y, zh, k = row // 4, lax.rem(row // 2, 2), lax.rem(row, 2)
    x, zl = col // 2, lax.rem(col, 2)
    sign = 1 - 2 * k
    turns = [sign * a + 4 for a in range(4)]
    xs = [lax.rem(x + turn, 4) * 2 for turn in turns]
    ys = [lax.rem(y + turn, 4) * 4 for turn in turns]

    def sixteen(core, c, skip):
        core_at = lax.rem(k + core, 2)
        z = [lax.rem(zh * 2 + zl + sign * c + 4 + turn, 4) for turn in turns]
        z_rows = [(at // 2) * 2 + core_at for at in z]
        z_cols = [lax.rem(at, 2) for at in z]
        for b in range(4):
            for a in range(4):
                if not (skip and a == 0 and b == 0):
                    ab = (a + b) % 4
                    body(ys[ab] + z_rows[ab], xs[a] + z_cols[ab])

    def step(p, carry):
        sixteen(p // 4, lax.rem(p, 4), False)
        return carry

    sixteen(0, 0, True)
    lax.fori_loop(1, 8, step, 0)


def back_rows(mixed, cur, gate, new, gain_t, bias_t, weight, tl, ts):
    m = mixed.astype(F32)
    mean = jnp.mean(m, axis=0)
    centred = m - mean[None]
    var = jnp.mean(centred * centred, axis=0)
    ts[...] = lax.rsqrt(var + 1e-5)
    tl[...] = centred.reshape(CH * GROUP, COLS)
    for i in range(GROUP):
        c = tl[pl.ds(i, CH, stride=GROUP), :]
        nm = (c * ts[pl.ds(i, 1), :] * gain_t[...] + bias_t[...]).astype(BF16)
        change = dot(nm, weight[...], TN)
        new[i] = (cur[i].astype(F32) + gate[i] * change).astype(BF16)


def kernel(
    pair_h, ng_h, nb_h, pw_h, gw_h, og_h, ob_h, ow_h, out_h, last_mixed, last_gate, last_cur,
    cur, normed, gate, sides, all_sides, lt, acc, m_all, m_in,
    ng, nb, pw, gw, og, ob, ow, wt, gain_t, bias_t, tl, tr, ts,
    load_sem, param_sem, send_sem, recv_sem, out_sem, ahead_sem,
):
    row, col = lax.axis_index("row"), lax.axis_index("col")
    me = row * N_COL + col

    def load(g):
        rows = pl.ds(g * GROUP, GROUP)
        return pltpu.make_async_copy(pair_h.at[rows], cur.at[0, rows], load_sem.at[g])

    first = pl.ds(2, 2)
    params = [
        pltpu.make_async_copy(src, dst, param_sem.at[k])
        for k, (src, dst) in enumerate(
            (
                (pw_h.at[0, first], pw.at[0, first]),
                (ng_h, ng),
                (nb_h, nb),
                (pw_h.at[0, pl.ds(0, 2)], pw.at[0, pl.ds(0, 2)]),
                (pw_h.at[1], pw.at[1]),
                (gw_h, gw),
                (og_h, og),
                (ob_h, ob),
                (ow_h, ow),
            )
        )
    ]
    load(0).start()
    for copy in params[:3]:
        copy.start()
    for g in range(1, ROWS // GROUP):
        load(g).start()
    for copy in params[3:]:
        copy.start()

    barrier = pltpu.get_barrier_semaphore()

    def greet(r, c):
        pl.semaphore_signal(
            barrier, inc=1, device_id=(r, c), device_id_type=pl.DeviceIdType.MESH
        )

    each_target(row, col, greet)
    for copy in params[:3]:
        copy.wait()
    for k in range(2, 4):
        wt[0, k * CH : (k + 1) * CH] = pw[0, k].T

    def norm_rows(u, base):
        x = cur[u, pl.ds(base, 2)].reshape(2 * COLS, CH).astype(F32)
        n = layer_norm(x, ng[u : u + 1], nb[u : u + 1]).astype(BF16)
        normed[pl.ds(base, 2)] = n.reshape(2, COLS, CH)
        return n

    def project(u, k, n):
        first = 256 * (1 - k)
        p = dot(wt[u, first : first + 256], n, NT)
        return sigmoid(p[0:128]) * p[128:256]

    def keep(u, k, half, g, wide):
        first = PLACE[u][k, half, 0] + g * GROUP
        if (u, k) == (1, LEFT):
            first = PLACE[u][k, half, g]
        rows = pl.ds(pl.multiple_of(first, GROUP), GROUP)
        sides[u, :, rows, :] = wide[...].reshape(CH, GROUP, COLS).astype(BF16)

    def front_group(u, k, half, g, fresh=True):
        base = half * HALF + g * GROUP
        for i in range(0, GROUP, 2):
            if fresh:
                n = norm_rows(u, base + i)
            else:
                n = normed[pl.ds(base + i, 2)].reshape(2 * COLS, CH)
            side = project(u, k, n)
            for r in range(2):
                (tr, tl)[k][pl.ds(i + r, CH, stride=GROUP), :] = side[:, r * COLS : (r + 1) * COLS]
        keep(u, k, half, g, (tr, tl)[k])

    def left_by_parts(half):
        def eight(p):
            for q in range(8):
                rows = [half * HALF + p * 8 + q + r * GROUP for r in range(2)]
                order = [(r, c) for part in range(2) for r in rows for c in (part, part + 2)]
                n = jnp.concatenate([normed[r, c * 32 : (c + 1) * 32] for r, c in order], axis=0)
                side = project(1, LEFT, n)
                for part, wide in enumerate((tl, tr)):
                    wide[pl.ds(p * 8 + q, CH, stride=GROUP), :] = side[
                        :, part * COLS : (part + 1) * COLS
                    ]

        loop(2, eight)
        keep(1, LEFT, half, 0, tl)
        keep(1, LEFT, half, 1, tr)

    def gate_rows(u, step):
        n = normed[pl.ds(step * 4, 4)].reshape(4 * COLS, CH)
        gate[pl.ds(step * 4, 4)] = sigmoid(dot(n, gw[u], NN)).reshape(4, COLS, CH)

    def back_group(u, g):
        base = g * GROUP
        back_rows(
            m_in[u, :, pl.ds(pl.multiple_of(base, GROUP), GROUP), :],
            cur.at[u, pl.ds(base, GROUP)],
            gate.at[pl.ds(base, GROUP)],
            cur.at[1 - u, pl.ds(base, GROUP)],
            gain_t.at[u], bias_t.at[u], ow.at[u], tl, ts,
        )

    def loop(count, body):
        def step(i, carry):
            body(i)
            return carry

        lax.fori_loop(0, count, step, 0)

    def rows_of(flight):
        return (*SIDES, *MIXED)[flight][2]

    def spread(flight, g=0):
        if flight < len(SIDES):
            u, first, rows = SIDES[flight]
            part = pl.ds(first + g * rows, rows)
            src_at = lambda r, c: sides.at[u, r * N_COL + c, part]
            dst = all_sides.at[u, col, row, part]
        else:
            u, first, rows = MIXED[flight - len(SIDES)]
            part = pl.ds(first, rows)
            src_at = lambda r, c: m_all.at[u, c, r, part]
            dst = last_mixed.at[me] if flight == FLIGHTS - 1 else m_in.at[u, me, part]
        flight = flight + g
        pltpu.make_async_copy(src_at(row, col), dst, recv_sem.at[flight]).start()

        def send(r, c):
            pltpu.make_async_remote_copy(
                src_ref=src_at(r, c),
                dst_ref=dst,
                send_sem=send_sem.at[flight],
                recv_sem=recv_sem.at[flight],
                device_id=(r, c),
                device_id_type=pl.DeviceIdType.MESH,
            ).start()

        each_target(row, col, send)

    def arrived(flight, g=0):
        size = m_in.at[0, :, pl.ds(0, rows_of(flight))]
        pltpu.make_async_copy(size, size, recv_sem.at[flight + g]).wait()

    def sent(flight):
        size = m_in.at[0, pl.ds(0, DEV - 1), pl.ds(0, rows_of(flight))]
        pltpu.make_async_copy(size, size, send_sem.at[flight]).wait()

    def put_mixed(u, half, jb, out):
        out = out.astype(BF16)
        for k in range(2):
            m_all[u, 2 * jb + k, :, pl.ds(half * HALF, HALF), :] = out[
                :, k * COLS : (k + 1) * COLS
            ].reshape(N_ROW, HALF, COLS)

    def side_rows(u, c, k, half, part, rows=GROUP):
        first = PLACE[u][k, half, part]
        return all_sides[u, c, :, first : first + rows, :].reshape(N_ROW * rows, COLS)

    def mix_outgoing(half):
        a = jnp.concatenate(
            [
                side_rows(0, c, LEFT, half, 0, HALF)
                for c in range(N_COL)
            ],
            axis=1,
        )

        def block(jb):
            b = jnp.concatenate(
                [all_sides[0, c, pl.ds(4 * jb, 4), 0:64].reshape(256, COLS) for c in range(N_COL)],
                axis=1,
            )
            put_mixed(0, half, jb, dot(a, b, NT))

        loop(4, block)

    def turn(half, part):
        def block(c):
            t = side_rows(1, c, LEFT, half, part).T
            for r in range(2):
                lt[half, pl.ds(2 * c, 2), part * HALF : (part + 1) * HALF, r * 256 : r * 256 + 256] = (
                    t[r * 64 : (r + 1) * 64].reshape(2, HALF, 256)
                )

        loop(N_COL, block)

    def mix_incoming(half, k):
        a = lt[k, :, half * HALF : (half + 1) * HALF, :].reshape(512, 512)

        def block(jb):
            b = jnp.concatenate(
                [
                    jnp.concatenate(
                        [
                            side_rows(1, 2 * jb + c, RIGHT, k, r) for r in range(2)
                        ],
                        axis=0,
                    )
                    for c in range(2)
                ],
                axis=1,
            )
            if k == 0:
                acc[half, jb] = dot(a, b, NN)
            else:
                put_mixed(1, half, jb, acc[half, jb] + dot(a, b, NN))

        loop(4, block)

    load(0).wait()
    front_group(0, RIGHT, 0, 0)
    pl.semaphore_wait(barrier, DEV - 1)
    spread(0)
    for copy in params[3:]:
        copy.wait()
    load(1).wait()
    front_group(0, RIGHT, 0, 1)
    spread(1)
    load(2).wait()
    load(3).wait()
    loop(2, lambda g: front_group(0, RIGHT, 1, g))
    spread(2)
    for k in range(2):
        wt[0, k * CH : (k + 1) * CH] = pw[0, k].T
    for half in range(2):
        loop(2, lambda g: front_group(0, LEFT, half, g, False))
        spread(3 + half)
    for k in range(4):
        wt[1, k * CH : (k + 1) * CH] = pw[1, k].T
    for u in range(2):
        gain_t[u] = jnp.broadcast_to(og[u : u + 1], (CH, CH)).T
        bias_t[u] = jnp.broadcast_to(ob[u : u + 1], (CH, CH)).T
    loop(ROWS // 4, lambda s: gate_rows(0, s))
    for flight in range(3):
        arrived(flight)
    for half in range(2):
        arrived(3 + half)
        mix_outgoing(half)
        spread(12 + 2 * half)
        spread(13 + 2 * half)
    for half in range(2):

        def turnover(g):
            arrived(12 + 2 * half, g)
            back_group(0, 2 * half + g)
            front_group(1, RIGHT, half, g)
            if half == 0:
                spread(5, g)

        loop(2, turnover)
        if half == 1:
            spread(8)
        left_by_parts(half)
        spread(7 if half == 0 else 9)
    spread(10)
    spread(11)
    loop(ROWS // 4, lambda s: gate_rows(1, s))
    last = pl.ds(HALF + GROUP, GROUP)
    ahead = [
        pltpu.make_async_copy(src, dst, ahead_sem.at[k])
        for k, (src, dst) in enumerate(((gate.at[last], last_gate), (cur.at[1, last], last_cur)))
    ]
    for copy in ahead:
        copy.start()
    for flight in range(5, 8):
        arrived(flight)
    turn(0, 0)
    mix_incoming(0, 0)
    arrived(8)
    arrived(9)
    turn(1, 0)
    mix_incoming(0, 1)
    spread(16)
    for k in range(2):
        arrived(10 + k)
        turn(k, 1)
        mix_incoming(1, k)
    spread(17)
    spread(18)

    def store(k, first, count):
        rows = pl.ds(first, count)
        return pltpu.make_async_copy(cur.at[0, rows], out_h.at[rows], out_sem.at[k])

    stores = [store(0, 0, HALF), store(1, HALF, GROUP)]
    arrived(16)
    loop(2, lambda g: back_group(1, g))
    stores[0].start()
    arrived(17)
    loop(1, lambda g: back_group(1, 2))
    stores[1].start()
    for flight in range(FLIGHTS):
        sent(flight)
    for copy in ahead + stores:
        copy.wait()
    arrived(18)


def finish(
    done_h, mixed_h, gate_h, cur_h, og_h, ob_h, ow_h, out_h,
    done, mixed, gate, cur, og, ob, ow, new, gain_t, bias_t, tl, ts, sem, out_sem,
):
    loads = [
        pltpu.make_async_copy(src, dst, sem.at[k])
        for k, (src, dst) in enumerate(
            (
                (mixed_h, mixed), (og_h, og), (ob_h, ob), (ow_h, ow), (cur_h, cur), (gate_h, gate),
                *((done_h.at[pl.ds(g * 16, 16)], done.at[pl.ds(g * 16, 16)]) for g in range(3)),
            )
        )
    ]
    for copy in loads[:6]:
        copy.start()
    for copy in loads[1:4]:
        copy.wait()
    gain_t[...] = jnp.broadcast_to(og[1:2], (CH, CH)).T
    bias_t[...] = jnp.broadcast_to(ob[1:2], (CH, CH)).T
    carried = [
        pltpu.make_async_copy(
            done.at[pl.ds(g * 16, 16)], out_h.at[pl.ds(g * 16, 16)], out_sem.at[g]
        )
        for g in range(3)
    ]
    loads[0].wait()
    for copy in loads[6:]:
        copy.start()
    for copy in loads[4:6]:
        copy.wait()
    back_rows(mixed[...], cur, gate, new, gain_t, bias_t, ow.at[1], tl, ts)
    for g in range(3):
        loads[6 + g].wait()
        carried[g].start()
    end = pltpu.make_async_copy(new, out_h.at[pl.ds(48, 16)], out_sem.at[3])
    end.start()
    for copy in (*carried, end):
        copy.wait()


def shards(*args):
    pieces = (2, DEV, ROWS, COLS)
    planes = (2, N_COL, N_ROW, ROWS, COLS)
    vmem = pltpu.VMEM
    scratch = [
        vmem((2, ROWS, COLS, CH), BF16),
        vmem((ROWS, COLS, CH), BF16),
        vmem((ROWS, COLS, CH), F32),
        vmem((2, DEV, 2 * ROWS, COLS), BF16),
        vmem((2, N_COL, N_ROW, 2 * ROWS, COLS), BF16),
        vmem((2, N_ROW, ROWS, 512), BF16),
        vmem((2, 4, 512, 256), F32),
        vmem(planes, BF16),
        vmem(pieces, BF16),
    ]
    scratch += [vmem(a.shape, a.dtype) for a in args[1:]]
    scratch += [
        vmem((2, 4 * CH, CH), BF16),
        vmem((2, CH, CH), F32),
        vmem((2, CH, CH), F32),
        vmem((CH * GROUP, COLS), F32),
        vmem((CH * GROUP, COLS), F32),
        vmem((GROUP, COLS), F32),
        pltpu.SemaphoreType.DMA((ROWS // GROUP,)),
        pltpu.SemaphoreType.DMA((9,)),
        pltpu.SemaphoreType.DMA((FLIGHTS,)),
        pltpu.SemaphoreType.DMA((FLIGHTS,)),
        pltpu.SemaphoreType.DMA((2,)),
        pltpu.SemaphoreType.DMA((2,)),
    ]
    quarter = (GROUP, COLS, CH)
    of_kernel = [
        jax.ShapeDtypeStruct((ROWS - GROUP, COLS, CH), BF16),
        jax.ShapeDtypeStruct((DEV, GROUP, COLS), BF16),
        jax.ShapeDtypeStruct(quarter, F32),
        jax.ShapeDtypeStruct(quarter, BF16),
    ]
    parts = pl.pallas_call(
        kernel,
        out_shape=of_kernel,
        in_specs=[pl.BlockSpec(memory_space=pl.ANY)] * 8,
        out_specs=[pl.BlockSpec(memory_space=pl.ANY)] * 4,
        scratch_shapes=scratch,
        compiler_params=pltpu.CompilerParams(
            collective_id=0, has_side_effects=True, vmem_limit_bytes=60 * MIB
        ),
        name="triangle",
    )(*args)
    ends = args[5:]
    return pl.pallas_call(
        finish,
        out_shape=jax.ShapeDtypeStruct((ROWS, COLS, CH), BF16),
        in_specs=[pl.BlockSpec(memory_space=pl.ANY)] * 7,
        out_specs=pl.BlockSpec(memory_space=pl.ANY),
        scratch_shapes=[vmem(a.shape, a.dtype) for a in (*of_kernel, *ends)]
        + [
            vmem(quarter, BF16),
            vmem((CH, CH), F32),
            vmem((CH, CH), F32),
            vmem((CH * GROUP, COLS), F32),
            vmem((GROUP, COLS), F32),
            pltpu.SemaphoreType.DMA((9,)),
            pltpu.SemaphoreType.DMA((4,)),
        ],
        compiler_params=pltpu.CompilerParams(vmem_limit_bytes=60 * MIB),
        name="finish",
    )(*parts, *ends)


def solution(mesh):
    placed = (P("row", "col", None), P(), P(), P(), P(), P(), P(), P())
    return jax.shard_map(
        shards, mesh=mesh, in_specs=placed, out_specs=P("row", "col", None), check_vma=False
    )
```

```python
import jax
import jax.numpy as jnp
from jax import lax
from jax.experimental import pallas as pl
from jax.experimental.pallas import tpu as pltpu
from jax.sharding import PartitionSpec as P

F32, BF16 = jnp.float32, jnp.bfloat16
ROWS, COLS, N_ROW, N_COL, CH = 64, 128, 16, 8, 128
DEV = N_ROW * N_COL
GROUP, HALF = 16, 32
MIB = 1 << 20
NT = (((1,), (1,)), ((), ()))
TN = (((0,), (0,)), ((), ()))
NN = (((1,), (0,)), ((), ()))
RIGHT, LEFT = 0, 1
SIDES = (
    (0, 0, 16), (0, 16, 16), (0, 32, 16), (0, 48, 16), (0, 64, 32), (0, 96, 32),
    (1, 0, 32), (1, 48, 32), (1, 32, 16), (1, 80, 16), (1, 96, 32),
)
MIXED = ((0, 0, 32), (0, 32, 32), (1, 0, 32), (1, 32, 16), (1, 48, 16))
FLIGHTS = len(SIDES) + len(MIXED)
FIRST_RIGHT, FIRST_LEFT, NEXT_RIGHT, NEXT_LEFT, LAST_LEFT, FIRST_MIXED, NEXT_MIXED = 0, 4, 6, 8, 10, 11, 13


def sigmoid(v):
    return 0.5 * jnp.tanh(0.5 * v) + 0.5


def layer_norm(v, gain, bias):
    mean = jnp.mean(v, axis=-1, keepdims=True)
    centred = v - mean
    var = jnp.mean(centred * centred, axis=-1, keepdims=True)
    return centred * lax.rsqrt(var + 1e-5) * gain + bias


def dot(a, b, dims):
    return lax.dot_general(a, b, dims, preferred_element_type=F32)


def each_target(row, col, body):
    y, zh, k = row // 4, lax.rem(row // 2, 2), lax.rem(row, 2)
    x, zl = col // 2, lax.rem(col, 2)
    sign = 1 - 2 * k
    turns = [sign * a + 4 for a in range(4)]
    xs = [lax.rem(x + turn, 4) * 2 for turn in turns]
    ys = [lax.rem(y + turn, 4) * 4 for turn in turns]

    def sixteen(core, c, skip):
        core_at = lax.rem(k + core, 2)
        z = [lax.rem(zh * 2 + zl + sign * c + 4 + turn, 4) for turn in turns]
        z_rows = [(at // 2) * 2 + core_at for at in z]
        z_cols = [lax.rem(at, 2) for at in z]
        for b in range(4):
            for a in range(4):
                if not (skip and a == 0 and b == 0):
                    ab = (a + b) % 4
                    body(ys[ab] + z_rows[ab], xs[a] + z_cols[ab])

    def step(p, carry):
        sixteen(p // 4, lax.rem(p, 4), False)
        return carry

    sixteen(0, 0, True)
    lax.fori_loop(1, 8, step, 0)


def back_rows(mixed, cur, gate, new, gain_t, bias_t, weight, tl, ts, ready=None):
    m = mixed.astype(F32)
    mean = jnp.mean(m, axis=0)
    centred = m - mean[None]
    var = jnp.mean(centred * centred, axis=0)
    ts[...] = lax.rsqrt(var + 1e-5)
    tl[...] = centred.reshape(CH * GROUP, COLS)
    if ready is not None:
        ready()
    for i in range(GROUP):
        c = tl[pl.ds(i, CH, stride=GROUP), :]
        nm = (c * ts[pl.ds(i, 1), :] * gain_t[...] + bias_t[...]).astype(BF16)
        change = dot(nm, weight[...], TN)
        new[i] = (cur[i].astype(F32) + gate[i] * change).astype(BF16)


def kernel(
    pair_h, ng_h, nb_h, pw_h, gw_h, og_h, ob_h, ow_h, out_h, last_mixed, last_gate, last_cur,
    cur, normed, gate, sides, all_sides, lt, acc, m_all, m_in,
    ng, nb, pw, gw, og, ob, ow, wt, gain_t, bias_t, tl, tr, ts,
    load_sem, param_sem, send_sem, recv_sem, out_sem, ahead_sem,
):
    row, col = lax.axis_index("row"), lax.axis_index("col")
    me = row * N_COL + col

    def load(g):
        rows = pl.ds(g * GROUP, GROUP)
        return pltpu.make_async_copy(pair_h.at[rows], cur.at[0, rows], load_sem.at[g])

    first = pl.ds(2, 2)
    params = [
        pltpu.make_async_copy(src, dst, param_sem.at[k])
        for k, (src, dst) in enumerate(
            (
                (pw_h.at[0, first], pw.at[0, first]),
                (ng_h, ng),
                (nb_h, nb),
                (pw_h.at[0, pl.ds(0, 2)], pw.at[0, pl.ds(0, 2)]),
                (pw_h.at[1], pw.at[1]),
                (gw_h, gw),
                (og_h, og),
                (ob_h, ob),
                (ow_h, ow),
            )
        )
    ]
    load(0).start()
    for copy in params[:3]:
        copy.start()
    for g in range(1, ROWS // GROUP):
        load(g).start()
    for copy in params[3:]:
        copy.start()

    barrier = pltpu.get_barrier_semaphore()

    def greet(r, c):
        pl.semaphore_signal(
            barrier, inc=1, device_id=(r, c), device_id_type=pl.DeviceIdType.MESH
        )

    each_target(row, col, greet)
    for copy in params[:3]:
        copy.wait()
    for k in range(2, 4):
        wt[0, k * CH : (k + 1) * CH] = pw[0, k].T

    def norm_rows(u, base):
        x = cur[u, pl.ds(base, 2)].reshape(2 * COLS, CH).astype(F32)
        n = layer_norm(x, ng[u : u + 1], nb[u : u + 1]).astype(BF16)
        normed[pl.ds(base, 2)] = n.reshape(2, COLS, CH)
        return n

    def project(u, k, n):
        first = 256 * (1 - k)
        p = dot(wt[u, first : first + 256], n, NT)
        return sigmoid(p[0:128]) * p[128:256]

    def keep(u, first, wide):
        rows = pl.ds(pl.multiple_of(first, GROUP), GROUP)
        sides[u, :, rows, :] = wide[...].reshape(CH, GROUP, COLS).astype(BF16)

    def front_group(u, k, base, first, fresh=True):
        for i in range(0, GROUP, 2):
            if fresh:
                n = norm_rows(u, base + i)
            else:
                n = normed[pl.ds(base + i, 2)].reshape(2 * COLS, CH)
            side = project(u, k, n)
            for r in range(2):
                (tr, tl)[k][pl.ds(i + r, CH, stride=GROUP), :] = side[:, r * COLS : (r + 1) * COLS]
        keep(u, first, (tr, tl)[k])

    def left_by_parts(half):
        def eight(p):
            for q in range(8):
                rows = [half * HALF + p * 8 + q + r * GROUP for r in range(2)]
                order = [(r, c) for part in range(2) for r in rows for c in (part, part + 2)]
                n = jnp.concatenate([normed[r, c * 32 : (c + 1) * 32] for r, c in order], axis=0)
                side = project(1, LEFT, n)
                for part, wide in enumerate((tl, tr)):
                    wide[pl.ds(p * 8 + q, CH, stride=GROUP), :] = side[
                        :, part * COLS : (part + 1) * COLS
                    ]

        loop(2, eight)
        keep(1, half * 48 + 32, tl)
        keep(1, half * 16 + 96, tr)

    def gate_rows(u, step):
        n = normed[pl.ds(step * 4, 4)].reshape(4 * COLS, CH)
        gate[pl.ds(step * 4, 4)] = sigmoid(dot(n, gw[u], NN)).reshape(4, COLS, CH)

    def back_group(u, g):
        base = g * GROUP
        back_rows(
            m_in[u, :, pl.ds(pl.multiple_of(base, GROUP), GROUP), :],
            cur.at[u, pl.ds(base, GROUP)],
            gate.at[pl.ds(base, GROUP)],
            cur.at[1 - u, pl.ds(base, GROUP)],
            gain_t.at[u], bias_t.at[u], ow.at[u], tl, ts,
        )

    def loop(count, body):
        def step(i, carry):
            body(i)
            return carry

        lax.fori_loop(0, count, step, 0)

    def rows_of(flight):
        return (*SIDES, *MIXED)[flight][2]

    def spread(flight, g=0):
        u, first, rows = (*SIDES, *MIXED)[flight]
        if isinstance(g, int) and g == 0:
            start = first
        else:
            start = pl.multiple_of(first + g * ((*SIDES, *MIXED)[flight + 1][1] - first), GROUP)
        part = pl.ds(start, rows)
        if flight < len(SIDES):
            src_at = lambda r, c: sides.at[u, r * N_COL + c, part]
            dst = all_sides.at[u, col, row, part]
        else:
            src_at = lambda r, c: m_all.at[u, c, r, part]
            dst = last_mixed.at[me] if flight == FLIGHTS - 1 else m_in.at[u, me, part]
        index = flight + g
        pltpu.make_async_copy(src_at(row, col), dst, recv_sem.at[index]).start()

        def send(r, c):
            pltpu.make_async_remote_copy(
                src_ref=src_at(r, c),
                dst_ref=dst,
                send_sem=send_sem.at[index],
                recv_sem=recv_sem.at[index],
                device_id=(r, c),
                device_id_type=pl.DeviceIdType.MESH,
            ).start()

        each_target(row, col, send)

    def arrived(flight, g=0):
        size = m_in.at[0, :, pl.ds(0, rows_of(flight))]
        pltpu.make_async_copy(size, size, recv_sem.at[flight + g]).wait()

    def sent(flight):
        size = m_in.at[0, pl.ds(0, DEV - 1), pl.ds(0, rows_of(flight))]
        pltpu.make_async_copy(size, size, send_sem.at[flight]).wait()

    def put_mixed(u, half, jb, out):
        out = out.astype(BF16)
        rows = pl.ds(half * HALF, HALF)
        for k in range(2):
            m_all[u, 2 * jb + k, :, rows, :] = out[:, k * COLS : (k + 1) * COLS].reshape(
                N_ROW, HALF, COLS
            )

    def side_rows(u, c, first, rows=GROUP):
        return all_sides[u, c, :, pl.ds(first, rows), :].reshape(N_ROW * rows, COLS)

    def mix_outgoing(half):
        first = pl.multiple_of(64 + half * HALF, HALF)
        a = jnp.concatenate([side_rows(0, c, first, HALF) for c in range(N_COL)], axis=1)

        def block(jb):
            b = jnp.concatenate(
                [all_sides[0, c, pl.ds(4 * jb, 4), 0:64].reshape(256, COLS) for c in range(N_COL)],
                axis=1,
            )
            put_mixed(0, half, jb, dot(a, b, NT))

        loop(4, block)

    def turn(half, part):
        def block(c):
            t = side_rows(1, c, half * 48 + 32 if part == 0 else half * 16 + 96).T
            for r in range(2):
                lt[half, pl.ds(2 * c, 2), part * HALF : (part + 1) * HALF, r * 256 : r * 256 + 256] = (
                    t[r * 64 : (r + 1) * 64].reshape(2, HALF, 256)
                )

        loop(N_COL, block)

    def mix_incoming(half, k):
        a = lt[k, :, half * HALF : (half + 1) * HALF, :].reshape(512, 512)

        def block(jb):
            b = jnp.concatenate(
                [
                    jnp.concatenate(
                        [
                            side_rows(1, 2 * jb + c, k * 48 + r * GROUP) for r in range(2)
                        ],
                        axis=0,
                    )
                    for c in range(2)
                ],
                axis=1,
            )
            if k == 0:
                acc[half, jb] = dot(a, b, NN)
            else:
                put_mixed(1, half, jb, acc[half, jb] + dot(a, b, NN))

        loop(4, block)


    def open_right(g):
        load(g).wait()
        front_group(0, RIGHT, g * GROUP, g * GROUP)

        @pl.when(g == 0)
        def _():
            pl.semaphore_wait(barrier, DEV - 1)

        spread(FIRST_RIGHT, g)

    loop(ROWS // GROUP, open_right)
    for copy in params[3:]:
        copy.wait()
    for k in range(2):
        wt[0, k * CH : (k + 1) * CH] = pw[0, k].T

    def open_left(half):
        def group(g):
            base = half * HALF + g * GROUP
            front_group(0, LEFT, base, 64 + base, False)

        loop(2, group)
        spread(FIRST_LEFT, half)

    loop(2, open_left)
    for k in range(4):
        wt[1, k * CH : (k + 1) * CH] = pw[1, k].T
    for u in range(2):
        gain_t[u] = jnp.broadcast_to(og[u : u + 1], (CH, CH)).T
        bias_t[u] = jnp.broadcast_to(ob[u : u + 1], (CH, CH)).T
    loop(ROWS // 4, lambda s: gate_rows(0, s))
    for g in range(ROWS // GROUP):
        arrived(FIRST_RIGHT, g)

    def outgoing(half):
        arrived(FIRST_LEFT, half)
        mix_outgoing(half)
        spread(FIRST_MIXED, half)

    loop(2, outgoing)

    def turnover(half):
        arrived(FIRST_MIXED, half)

        def group(g):
            back_group(0, 2 * half + g)
            front_group(1, RIGHT, half * HALF + g * GROUP, half * 48 + g * GROUP)

        loop(2, group)
        spread(NEXT_RIGHT, half)
        left_by_parts(half)
        spread(NEXT_LEFT, half)

    loop(2, turnover)
    spread(LAST_LEFT)
    loop(ROWS // 4, lambda s: gate_rows(1, s))
    last = pl.ds(HALF + GROUP, GROUP)
    ahead = [
        pltpu.make_async_copy(src, dst, ahead_sem.at[k])
        for k, (src, dst) in enumerate(((gate.at[last], last_gate), (cur.at[1, last], last_cur)))
    ]
    for copy in ahead:
        copy.start()
    for half in range(2):
        arrived(NEXT_RIGHT, half)
        arrived(NEXT_LEFT, half)
        turn(half, 0)
        mix_incoming(0, half)
    spread(NEXT_MIXED)
    arrived(LAST_LEFT)
    for half in range(2):
        turn(half, 1)
        mix_incoming(1, half)
    spread(NEXT_MIXED + 1)
    spread(NEXT_MIXED + 2)

    def store(g):
        rows = pl.ds(g * GROUP, GROUP)
        return pltpu.make_async_copy(cur.at[0, rows], out_h.at[rows], out_sem.at[g])

    def close(g):
        @pl.when(g == 0)
        def _():
            arrived(NEXT_MIXED)

        @pl.when(g == 2)
        def _():
            arrived(NEXT_MIXED + 1)

        back_group(1, g)
        store(g).start()

    loop(3, close)
    for flight in range(FLIGHTS):
        sent(flight)
    for copy in (*ahead, store(0), store(1), store(2)):
        copy.wait()
    arrived(NEXT_MIXED + 2)


def finish(
    done_h, mixed_h, gate_h, cur_h, og_h, ob_h, ow_h, out_h,
    done, mixed, gate, cur, og, ob, ow, new, gain_t, bias_t, tl, ts, sem, out_sem,
):
    loads = [
        pltpu.make_async_copy(src, dst, sem.at[k])
        for k, (src, dst) in enumerate(
            (
                (mixed_h, mixed), (og_h, og), (ob_h, ob), (ow_h, ow), (cur_h, cur), (gate_h, gate),
                *((done_h.at[pl.ds(g * 16, 16)], done.at[pl.ds(g * 16, 16)]) for g in range(3)),
            )
        )
    ]
    for copy in loads:
        copy.start()
    for copy in loads[1:4]:
        copy.wait()
    gain_t[...] = jnp.broadcast_to(og[1:2], (CH, CH)).T
    bias_t[...] = jnp.broadcast_to(ob[1:2], (CH, CH)).T
    carried = [
        pltpu.make_async_copy(
            done.at[pl.ds(g * 16, 16)], out_h.at[pl.ds(g * 16, 16)], out_sem.at[g]
        )
        for g in range(3)
    ]
    loads[0].wait()

    def ready():
        for copy in loads[4:6]:
            copy.wait()
        for g in range(3):
            loads[6 + g].wait()
            carried[g].start()

    back_rows(mixed[...], cur, gate, new, gain_t, bias_t, ow.at[1], tl, ts, ready)
    end = pltpu.make_async_copy(new, out_h.at[pl.ds(48, 16)], out_sem.at[3])
    end.start()
    for copy in (*carried, end):
        copy.wait()


def shards(*args):
    pieces = (2, DEV, ROWS, COLS)
    planes = (2, N_COL, N_ROW, ROWS, COLS)
    vmem = pltpu.VMEM
    scratch = [
        vmem((2, ROWS, COLS, CH), BF16),
        vmem((ROWS, COLS, CH), BF16),
        vmem((ROWS, COLS, CH), F32),
        vmem((2, DEV, 2 * ROWS, COLS), BF16),
        vmem((2, N_COL, N_ROW, 2 * ROWS, COLS), BF16),
        vmem((2, N_ROW, ROWS, 512), BF16),
        vmem((2, 4, 512, 256), F32),
        vmem(planes, BF16),
        vmem(pieces, BF16),
    ]
    scratch += [vmem(a.shape, a.dtype) for a in args[1:]]
    scratch += [
        vmem((2, 4 * CH, CH), BF16),
        vmem((2, CH, CH), F32),
        vmem((2, CH, CH), F32),
        vmem((CH * GROUP, COLS), F32),
        vmem((CH * GROUP, COLS), F32),
        vmem((GROUP, COLS), F32),
        pltpu.SemaphoreType.DMA((ROWS // GROUP,)),
        pltpu.SemaphoreType.DMA((9,)),
        pltpu.SemaphoreType.DMA((FLIGHTS,)),
        pltpu.SemaphoreType.DMA((FLIGHTS,)),
        pltpu.SemaphoreType.DMA((3,)),
        pltpu.SemaphoreType.DMA((2,)),
    ]
    quarter = (GROUP, COLS, CH)
    of_kernel = [
        jax.ShapeDtypeStruct((ROWS - GROUP, COLS, CH), BF16),
        jax.ShapeDtypeStruct((DEV, GROUP, COLS), BF16),
        jax.ShapeDtypeStruct(quarter, F32),
        jax.ShapeDtypeStruct(quarter, BF16),
    ]
    parts = pl.pallas_call(
        kernel,
        out_shape=of_kernel,
        in_specs=[pl.BlockSpec(memory_space=pl.ANY)] * 8,
        out_specs=[pl.BlockSpec(memory_space=pl.ANY)] * 4,
        scratch_shapes=scratch,
        compiler_params=pltpu.CompilerParams(
            collective_id=0, has_side_effects=True, vmem_limit_bytes=60 * MIB
        ),
        name="triangle",
    )(*args)
    ends = args[5:]
    return pl.pallas_call(
        finish,
        out_shape=jax.ShapeDtypeStruct((ROWS, COLS, CH), BF16),
        in_specs=[pl.BlockSpec(memory_space=pl.ANY)] * 7,
        out_specs=pl.BlockSpec(memory_space=pl.ANY),
        scratch_shapes=[vmem(a.shape, a.dtype) for a in (*of_kernel, *ends)]
        + [
            vmem(quarter, BF16),
            vmem((CH, CH), F32),
            vmem((CH, CH), F32),
            vmem((CH * GROUP, COLS), F32),
            vmem((GROUP, COLS), F32),
            pltpu.SemaphoreType.DMA((9,)),
            pltpu.SemaphoreType.DMA((4,)),
        ],
        compiler_params=pltpu.CompilerParams(vmem_limit_bytes=60 * MIB),
        name="finish",
    )(*parts, *ends)


def solution(mesh):
    placed = (P("row", "col", None), P(), P(), P(), P(), P(), P(), P())
    return jax.shard_map(
        shards, mesh=mesh, in_specs=placed, out_specs=P("row", "col", None), check_vma=False
    )
```

```python
import jax
import jax.numpy as jnp
from jax import lax
from jax.experimental import pallas as pl
from jax.experimental.pallas import tpu as pltpu
from jax.sharding import PartitionSpec as P

F32, BF16 = jnp.float32, jnp.bfloat16
ROWS, COLS, N_ROW, N_COL, CH = 64, 128, 16, 8, 128
DEV = N_ROW * N_COL
GROUP, HALF = 16, 32
MIB = 1 << 20
NT = (((1,), (1,)), ((), ()))
TN = (((0,), (0,)), ((), ()))
NN = (((1,), (0,)), ((), ()))
RIGHT, LEFT = 0, 1
SIDES = (
    (0, 0, 16), (0, 16, 16), (0, 32, 16), (0, 48, 16), (0, 64, 32), (0, 96, 32),
    (1, 0, 32), (1, 48, 32), (1, 32, 16), (1, 80, 16), (1, 96, 32),
)
MIXED = ((0, 0, 32), (0, 32, 32), (1, 0, 32), (1, 32, 16), (1, 48, 16))
FLIGHTS = len(SIDES) + len(MIXED)
FIRST_RIGHT, FIRST_LEFT, NEXT_RIGHT, NEXT_LEFT, LAST_LEFT, FIRST_MIXED, NEXT_MIXED = 0, 4, 6, 8, 10, 11, 13


def sigmoid(v):
    return 0.5 * jnp.tanh(0.5 * v) + 0.5


def layer_norm(v, gain, bias):
    mean = jnp.mean(v, axis=-1, keepdims=True)
    centred = v - mean
    var = jnp.mean(centred * centred, axis=-1, keepdims=True)
    return centred * lax.rsqrt(var + 1e-5) * gain + bias


def dot(a, b, dims):
    return lax.dot_general(a, b, dims, preferred_element_type=F32)


def each_target(row, col, body):
    y, zh, k = row // 4, lax.rem(row // 2, 2), lax.rem(row, 2)
    x, zl = col // 2, lax.rem(col, 2)
    sign = 1 - 2 * k
    turns = [sign * a + 4 for a in range(4)]
    xs = [lax.rem(x + turn, 4) * 2 for turn in turns]
    ys = [lax.rem(y + turn, 4) * 4 for turn in turns]

    def sixteen(core, c, skip):
        core_at = lax.rem(k + core, 2)
        z = [lax.rem(zh * 2 + zl + sign * c + 4 + turn, 4) for turn in turns]
        z_rows = [(at // 2) * 2 + core_at for at in z]
        z_cols = [lax.rem(at, 2) for at in z]
        for b in range(4):
            for a in range(4):
                if not (skip and a == 0 and b == 0):
                    ab = (a + b) % 4
                    body(ys[ab] + z_rows[ab], xs[a] + z_cols[ab])

    def step(p, carry):
        sixteen(p // 4, lax.rem(p, 4), False)
        return carry

    sixteen(0, 0, True)
    lax.fori_loop(1, 8, step, 0)


def back_rows(mixed, cur, gate, new, gain_t, bias_t, weight, tl, ts, ready=None, after=None):
    m = mixed.astype(F32)
    mean = jnp.mean(m, axis=0)
    centred = m - mean[None]
    var = jnp.mean(centred * centred, axis=0)
    ts[...] = lax.rsqrt(var + 1e-5)
    tl[0 : CH * GROUP] = centred.reshape(CH * GROUP, COLS)
    if ready is not None:
        ready()
    for i in range(GROUP):
        c = tl[pl.ds(i, CH, stride=GROUP), :]
        nm = (c * ts[pl.ds(i, 1), :] * gain_t[...] + bias_t[...]).astype(BF16)
        change = dot(nm, weight[...], TN)
        new[i] = (cur[i].astype(F32) + gate[i] * change).astype(BF16)
        if after is not None:
            after(i)


def kernel(
    pair_h, ng_h, nb_h, pw_h, gw_h, og_h, ob_h, ow_h, out_h, last_mixed, last_gate, last_cur,
    cur, normed, gate, sides, all_sides, lt, acc, m_all, m_in,
    ng, nb, pw, gw, og, ob, ow, wt, gain_t, bias_t, tl, tr, ts,
    load_sem, param_sem, send_sem, recv_sem, out_sem, ahead_sem,
):
    row, col = lax.axis_index("row"), lax.axis_index("col")
    me = row * N_COL + col

    def load(g):
        rows = pl.ds(g * GROUP, GROUP)
        return pltpu.make_async_copy(pair_h.at[rows], cur.at[0, rows], load_sem.at[g])

    first = pl.ds(2, 2)
    params = [
        pltpu.make_async_copy(src, dst, param_sem.at[k])
        for k, (src, dst) in enumerate(
            (
                (pw_h.at[0, first], pw.at[0, first]),
                (ng_h, ng),
                (nb_h, nb),
                (pw_h.at[0, pl.ds(0, 2)], pw.at[0, pl.ds(0, 2)]),
                (pw_h.at[1], pw.at[1]),
                (gw_h, gw),
                (og_h, og),
                (ob_h, ob),
                (ow_h, ow),
            )
        )
    ]
    load(0).start()
    for copy in params[:3]:
        copy.start()

    barrier = pltpu.get_barrier_semaphore()

    def greet(r, c):
        pl.semaphore_signal(
            barrier, inc=1, device_id=(r, c), device_id_type=pl.DeviceIdType.MESH
        )

    each_target(row, col, greet)
    for g in range(1, ROWS // GROUP):
        load(g).start()
    for copy in params[3:]:
        copy.start()
    for copy in params[:3]:
        copy.wait()
    for k in range(2, 4):
        wt[0, k * CH : (k + 1) * CH] = pw[0, k].T

    def norm_rows(u, base):
        x = cur[u, pl.ds(base, 2)].reshape(2 * COLS, CH).astype(F32)
        n = layer_norm(x, ng[u : u + 1], nb[u : u + 1]).astype(BF16)
        normed[pl.ds(base, 2)] = n.reshape(2, COLS, CH)
        return n

    def project(u, k, n):
        first = 256 * (1 - k)
        p = dot(wt[u, first : first + 256], n, NT)
        return sigmoid(p[0:128]) * p[128:256]

    def keep(u, first, wide):
        rows = pl.ds(pl.multiple_of(first, GROUP), GROUP)
        sides[u, :, rows, :] = wide[0 : CH * GROUP].reshape(CH, GROUP, COLS).astype(BF16)

    def front_group(u, k, base, first, fresh=True):
        for i in range(0, GROUP, 2):
            if fresh:
                n = norm_rows(u, base + i)
            else:
                n = normed[pl.ds(base + i, 2)].reshape(2 * COLS, CH)
            side = project(u, k, n)
            for r in range(2):
                (tr, tl)[k][pl.ds(i + r, CH, stride=GROUP), :] = side[:, r * COLS : (r + 1) * COLS]
        keep(u, first, (tr, tl)[k])

    def left_by_parts(half):
        def eight(p):
            for q in range(8):
                rows = [half * HALF + p * 8 + q + r * GROUP for r in range(2)]
                order = [(r, c) for part in range(2) for r in rows for c in (part, part + 2)]
                n = jnp.concatenate([normed[r, c * 32 : (c + 1) * 32] for r, c in order], axis=0)
                side = project(1, LEFT, n)
                for part, wide in enumerate((tl, tr)):
                    wide[pl.ds(p * 8 + q, CH, stride=GROUP), :] = side[
                        :, part * COLS : (part + 1) * COLS
                    ]

        loop(2, eight)
        keep(1, half * 48 + 32, tl)
        keep(1, half * 16 + 96, tr)

    def gate_rows(u, step):
        n = normed[pl.ds(step * 4, 4)].reshape(4 * COLS, CH)
        gate[pl.ds(step * 4, 4)] = sigmoid(dot(n, gw[u], NN)).reshape(4, COLS, CH)

    def back_group(u, g):
        base = g * GROUP
        back_rows(
            m_in[u, :, pl.ds(pl.multiple_of(base, GROUP), GROUP), :],
            cur.at[u, pl.ds(base, GROUP)],
            gate.at[pl.ds(base, GROUP)],
            cur.at[1 - u, pl.ds(base, GROUP)],
            gain_t.at[u], bias_t.at[u], ow.at[u], tl, ts,
        )

    def loop(count, body):
        def step(i, carry):
            body(i)
            return carry

        lax.fori_loop(0, count, step, 0)

    def rows_of(flight):
        return (*SIDES, *MIXED)[flight][2]

    def spread(flight, g=0):
        u, first, rows = (*SIDES, *MIXED)[flight]
        if isinstance(g, int) and g == 0:
            start = first
        else:
            start = pl.multiple_of(first + g * ((*SIDES, *MIXED)[flight + 1][1] - first), GROUP)
        part = pl.ds(start, rows)
        if flight < len(SIDES):
            src_at = lambda r, c: sides.at[u, r * N_COL + c, part]
            dst = all_sides.at[u, col, row, part]
        else:
            src_at = lambda r, c: m_all.at[u, c, r, part]
            dst = last_mixed.at[me] if flight == FLIGHTS - 1 else m_in.at[u, me, part]
        index = flight + g
        pltpu.make_async_copy(src_at(row, col), dst, recv_sem.at[index]).start()

        def send(r, c):
            pltpu.make_async_remote_copy(
                src_ref=src_at(r, c),
                dst_ref=dst,
                send_sem=send_sem.at[index],
                recv_sem=recv_sem.at[index],
                device_id=(r, c),
                device_id_type=pl.DeviceIdType.MESH,
            ).start()

        each_target(row, col, send)

    def arrived(flight, g=0):
        size = m_in.at[0, :, pl.ds(0, rows_of(flight))]
        pltpu.make_async_copy(size, size, recv_sem.at[flight + g]).wait()

    def sent(flight):
        size = m_in.at[0, pl.ds(0, DEV - 1), pl.ds(0, rows_of(flight))]
        pltpu.make_async_copy(size, size, send_sem.at[flight]).wait()

    def put_mixed(u, half, jb, out):
        out = out.astype(BF16)
        rows = pl.ds(half * HALF, HALF)
        for k in range(2):
            m_all[u, 2 * jb + k, :, rows, :] = out[:, k * COLS : (k + 1) * COLS].reshape(
                N_ROW, HALF, COLS
            )

    def side_rows(u, c, first, rows=GROUP):
        return all_sides[u, c, :, pl.ds(first, rows), :].reshape(N_ROW * rows, COLS)

    def mix_outgoing(half):
        first = pl.multiple_of(64 + half * HALF, HALF)
        a = jnp.concatenate([side_rows(0, c, first, HALF) for c in range(N_COL)], axis=1)

        def block(jb):
            b = jnp.concatenate(
                [all_sides[0, c, pl.ds(4 * jb, 4), 0:64].reshape(256, COLS) for c in range(N_COL)],
                axis=1,
            )
            put_mixed(0, half, jb, dot(a, b, NT))

        loop(4, block)

    def turn(half, part):
        def block(c):
            t = side_rows(1, c, half * 48 + 32 if part == 0 else half * 16 + 96).T
            for r in range(2):
                lt[half, pl.ds(2 * c, 2), part * HALF : (part + 1) * HALF, r * 256 : r * 256 + 256] = (
                    t[r * 64 : (r + 1) * 64].reshape(2, HALF, 256)
                )

        loop(N_COL, block)

    def mix_incoming(half, k):
        a = lt[k, :, half * HALF : (half + 1) * HALF, :].reshape(512, 512)

        def block(jb):
            b = jnp.concatenate(
                [
                    jnp.concatenate(
                        [
                            side_rows(1, 2 * jb + c, k * 48 + r * GROUP) for r in range(2)
                        ],
                        axis=0,
                    )
                    for c in range(2)
                ],
                axis=1,
            )
            if k == 0:
                acc[half, jb] = dot(a, b, NN)
            else:
                put_mixed(1, half, jb, acc[half, jb] + dot(a, b, NN))

        loop(4, block)


    def open_right(g):
        load(g).wait()
        front_group(0, RIGHT, g * GROUP, g * GROUP)

        @pl.when(g == 0)
        def _():
            pl.semaphore_wait(barrier, DEV - 1)

        spread(FIRST_RIGHT, g)

    loop(ROWS // GROUP, open_right)
    for copy in params[3:]:
        copy.wait()
    for k in range(2):
        wt[0, k * CH : (k + 1) * CH] = pw[0, k].T

    def open_left(half):
        def group(g):
            base = half * HALF + g * GROUP
            front_group(0, LEFT, base, 64 + base, False)

        loop(2, group)
        spread(FIRST_LEFT, half)

    loop(2, open_left)
    for k in range(4):
        wt[1, k * CH : (k + 1) * CH] = pw[1, k].T
    for u in range(2):
        gain_t[u] = jnp.broadcast_to(og[u : u + 1], (CH, CH)).T
        bias_t[u] = jnp.broadcast_to(ob[u : u + 1], (CH, CH)).T
    loop(ROWS // 4, lambda s: gate_rows(0, s))
    for g in range(ROWS // GROUP):
        arrived(FIRST_RIGHT, g)

    def outgoing(half):
        arrived(FIRST_LEFT, half)
        mix_outgoing(half)
        spread(FIRST_MIXED, half)

    loop(2, outgoing)

    def turnover(half):
        arrived(FIRST_MIXED, half)

        def group(g):
            back_group(0, 2 * half + g)
            front_group(1, RIGHT, half * HALF + g * GROUP, half * 48 + g * GROUP)

        loop(2, group)
        spread(NEXT_RIGHT, half)
        left_by_parts(half)
        spread(NEXT_LEFT, half)

    loop(2, turnover)
    spread(LAST_LEFT)
    loop(ROWS // 4, lambda s: gate_rows(1, s))
    last = pl.ds(HALF + GROUP, GROUP)
    ahead = [
        pltpu.make_async_copy(src, dst, ahead_sem.at[k])
        for k, (src, dst) in enumerate(((gate.at[last], last_gate), (cur.at[1, last], last_cur)))
    ]
    for copy in ahead:
        copy.start()
    for half in range(2):
        arrived(NEXT_RIGHT, half)
        arrived(NEXT_LEFT, half)
        turn(half, 0)
        mix_incoming(0, half)
    spread(NEXT_MIXED)
    arrived(LAST_LEFT)
    for half in range(2):
        turn(half, 1)
        mix_incoming(1, half)
    spread(NEXT_MIXED + 1)
    spread(NEXT_MIXED + 2)

    def store(g):
        rows = pl.ds(g * GROUP, GROUP)
        return pltpu.make_async_copy(cur.at[0, rows], out_h.at[rows], out_sem.at[g])

    def close(g):
        @pl.when(g == 0)
        def _():
            arrived(NEXT_MIXED)

        @pl.when(g == 2)
        def _():
            arrived(NEXT_MIXED + 1)

        back_group(1, g)
        store(g).start()

    loop(3, close)
    for flight in range(FLIGHTS):
        sent(flight)
    for copy in (*ahead, store(0), store(1), store(2)):
        copy.wait()
    arrived(NEXT_MIXED + 2)


def finish(
    done_h, mixed_h, gate_h, cur_h, og_h, ob_h, ow_h, out_h,
    done, mixed, gate, cur, og, ob, ow, new, gain_t, bias_t, tl, ts, sem, out_sem,
):
    loads = [
        pltpu.make_async_copy(src, dst, sem.at[k])
        for k, (src, dst) in enumerate(
            (
                (mixed_h, mixed), (og_h, og), (ob_h, ob), (ow_h, ow), (cur_h, cur), (gate_h, gate),
                *((done_h.at[pl.ds(g * 16, 16)], done.at[pl.ds(g * 16, 16)]) for g in range(3)),
            )
        )
    ]
    for copy in loads:
        copy.start()
    for copy in loads[1:4]:
        copy.wait()
    gain_t[...] = jnp.broadcast_to(og[1:2], (CH, CH)).T
    bias_t[...] = jnp.broadcast_to(ob[1:2], (CH, CH)).T
    carried = [
        pltpu.make_async_copy(
            done.at[pl.ds(g * 16, 16)], out_h.at[pl.ds(g * 16, 16)], out_sem.at[g]
        )
        for g in range(3)
    ]
    loads[0].wait()

    def ready():
        for copy in loads[4:6]:
            copy.wait()
        for g in range(3):
            loads[6 + g].wait()
            carried[g].start()

    ends = [
        pltpu.make_async_copy(
            new.at[pl.ds(g * 4, 4)], out_h.at[pl.ds(48 + g * 4, 4)], out_sem.at[3 + g]
        )
        for g in range(4)
    ]

    def after(i):
        if i % 4 == 3:
            ends[i // 4].start()

    back_rows(mixed[...], cur, gate, new, gain_t, bias_t, ow.at[1], tl, ts, ready, after)
    for copy in (*carried, *ends):
        copy.wait()


def shards(*args):
    pieces = (2, DEV, ROWS, COLS)
    planes = (2, N_COL, N_ROW, ROWS, COLS)
    vmem = pltpu.VMEM
    scratch = [
        vmem((2, ROWS, COLS, CH), BF16),
        vmem((ROWS, COLS, CH), BF16),
        vmem((ROWS, COLS, CH), F32),
        vmem((2, DEV, 2 * ROWS, COLS), BF16),
        vmem((2, N_COL, N_ROW, 2 * ROWS, COLS), BF16),
        vmem((2, N_ROW, ROWS, 512), BF16),
        vmem((2, 4, 512, 256), F32),
        vmem(planes, BF16),
        vmem(pieces, BF16),
    ]
    scratch += [vmem(a.shape, a.dtype) for a in args[1:]]
    scratch += [
        vmem((2, 4 * CH, CH), BF16),
        vmem((2, CH, CH), F32),
        vmem((2, CH, CH), F32),
        vmem((CH * GROUP + GROUP, COLS), F32),
        vmem((CH * GROUP + GROUP, COLS), F32),
        vmem((GROUP, COLS), F32),
        pltpu.SemaphoreType.DMA((ROWS // GROUP,)),
        pltpu.SemaphoreType.DMA((9,)),
        pltpu.SemaphoreType.DMA((FLIGHTS,)),
        pltpu.SemaphoreType.DMA((FLIGHTS,)),
        pltpu.SemaphoreType.DMA((3,)),
        pltpu.SemaphoreType.DMA((2,)),
    ]
    quarter = (GROUP, COLS, CH)
    of_kernel = [
        jax.ShapeDtypeStruct((ROWS - GROUP, COLS, CH), BF16),
        jax.ShapeDtypeStruct((DEV, GROUP, COLS), BF16),
        jax.ShapeDtypeStruct(quarter, F32),
        jax.ShapeDtypeStruct(quarter, BF16),
    ]
    parts = pl.pallas_call(
        kernel,
        out_shape=of_kernel,
        in_specs=[pl.BlockSpec(memory_space=pl.ANY)] * 8,
        out_specs=[pl.BlockSpec(memory_space=pl.ANY)] * 4,
        scratch_shapes=scratch,
        compiler_params=pltpu.CompilerParams(
            collective_id=0, has_side_effects=True, vmem_limit_bytes=60 * MIB
        ),
        name="triangle",
    )(*args)
    ends = args[5:]
    return pl.pallas_call(
        finish,
        out_shape=jax.ShapeDtypeStruct((ROWS, COLS, CH), BF16),
        in_specs=[pl.BlockSpec(memory_space=pl.ANY)] * 7,
        out_specs=pl.BlockSpec(memory_space=pl.ANY),
        scratch_shapes=[vmem(a.shape, a.dtype) for a in (*of_kernel, *ends)]
        + [
            vmem(quarter, BF16),
            vmem((CH, CH), F32),
            vmem((CH, CH), F32),
            vmem((CH * GROUP + GROUP, COLS), F32),
            vmem((GROUP, COLS), F32),
            pltpu.SemaphoreType.DMA((9,)),
            pltpu.SemaphoreType.DMA((7,)),
        ],
        compiler_params=pltpu.CompilerParams(vmem_limit_bytes=60 * MIB),
        name="finish",
    )(*parts, *ends)


def solution(mesh):
    placed = (P("row", "col", None), P(), P(), P(), P(), P(), P(), P())
    return jax.shard_map(
        shards, mesh=mesh, in_specs=placed, out_specs=P("row", "col", None), check_vma=False
    )
```

```python
import jax
import jax.numpy as jnp
from jax import lax
from jax.experimental import pallas as pl
from jax.experimental.pallas import tpu as pltpu
from jax.sharding import PartitionSpec as P

F32, BF16 = jnp.float32, jnp.bfloat16
ROWS, COLS, N_ROW, N_COL, CH = 64, 128, 16, 8, 128
DEV = N_ROW * N_COL
GROUP, HALF = 16, 32
MIB = 1 << 20
NT = (((1,), (1,)), ((), ()))
TN = (((0,), (0,)), ((), ()))
NN = (((1,), (0,)), ((), ()))
RIGHT, LEFT = 0, 1
SIDES = (
    (0, 0, 16), (0, 16, 16), (0, 32, 16), (0, 48, 16), (0, 64, 32), (0, 96, 32),
    (1, 0, 32), (1, 48, 32), (1, 32, 16), (1, 80, 16), (1, 96, 32),
)
MIXED = ((0, 0, 32), (0, 32, 32), (1, 0, 32), (1, 32, 16), (1, 48, 16))
FLIGHTS = len(SIDES) + len(MIXED)
FIRST_RIGHT, FIRST_LEFT, NEXT_RIGHT, NEXT_LEFT, LAST_LEFT, FIRST_MIXED, NEXT_MIXED = 0, 4, 6, 8, 10, 11, 13


def sigmoid(v):
    return 0.5 * jnp.tanh(0.5 * v) + 0.5


def layer_norm(v, gain, bias):
    mean = jnp.mean(v, axis=-1, keepdims=True)
    centred = v - mean
    var = jnp.mean(centred * centred, axis=-1, keepdims=True)
    return centred * lax.rsqrt(var + 1e-5) * gain + bias


def dot(a, b, dims):
    return lax.dot_general(a, b, dims, preferred_element_type=F32)


def each_target(row, col, body):
    y, zh, k = row // 4, lax.rem(row // 2, 2), lax.rem(row, 2)
    x, zl = col // 2, lax.rem(col, 2)
    sign = 1 - 2 * k
    turns = [sign * a + 4 for a in range(4)]
    xs = [lax.rem(x + turn, 4) * 2 for turn in turns]
    ys = [lax.rem(y + turn, 4) * 4 for turn in turns]

    def sixteen(core, c, skip):
        core_at = lax.rem(k + core, 2)
        z = [lax.rem(zh * 2 + zl + sign * c + 4 + turn, 4) for turn in turns]
        z_rows = [(at // 2) * 2 + core_at for at in z]
        z_cols = [lax.rem(at, 2) for at in z]
        for b in range(4):
            for a in range(4):
                if not (skip and a == 0 and b == 0):
                    ab = (a + b) % 4
                    body(ys[ab] + z_rows[ab], xs[a] + z_cols[ab])

    def step(p, carry):
        sixteen(p // 4, lax.rem(p, 4), False)
        return carry

    sixteen(0, 0, True)
    lax.fori_loop(1, 8, step, 0)


def back_rows(mixed, cur, gate, new, gain_t, bias_t, weight, tl, ts, ready=None, after=None):
    m = mixed.astype(F32)
    mean = jnp.mean(m, axis=0)
    centred = m - mean[None]
    var = jnp.mean(centred * centred, axis=0)
    ts[...] = lax.rsqrt(var + 1e-5)
    tl[0 : CH * GROUP] = centred.reshape(CH * GROUP, COLS)
    if ready is not None:
        ready()
    for i in range(GROUP):
        c = tl[pl.ds(i, CH, stride=GROUP), :]
        nm = (c * ts[pl.ds(i, 1), :] * gain_t[...] + bias_t[...]).astype(BF16)
        change = dot(nm, weight[...], TN)
        new[i] = (cur[i].astype(F32) + gate[i] * change).astype(BF16)
        if after is not None:
            after(i)


def kernel(
    pair_h, ng_h, nb_h, pw_h, gw_h, og_h, ob_h, ow_h, out_h, last_mixed, last_gate, last_cur,
    cur, normed, gate, sides, all_sides, lt, acc, m_all, m_in,
    ng, nb, pw, gw, og, ob, ow, wt, gain_t, bias_t, tl, tr, ts,
    load_sem, param_sem, send_sem, recv_sem, out_sem, ahead_sem,
):
    row, col = lax.axis_index("row"), lax.axis_index("col")
    me = row * N_COL + col

    def load(g):
        rows = pl.ds(g * GROUP, GROUP)
        return pltpu.make_async_copy(pair_h.at[rows], cur.at[0, rows], load_sem.at[g])

    first = pl.ds(2, 2)
    params = [
        pltpu.make_async_copy(src, dst, param_sem.at[k])
        for k, (src, dst) in enumerate(
            (
                (pw_h.at[0, first], pw.at[0, first]),
                (ng_h, ng),
                (nb_h, nb),
                (pw_h.at[0, pl.ds(0, 2)], pw.at[0, pl.ds(0, 2)]),
                (pw_h.at[1], pw.at[1]),
                (gw_h, gw),
                (og_h, og),
                (ob_h, ob),
                (ow_h, ow),
            )
        )
    ]
    for k in range(4):
        rows = pl.ds(4 * k, 4)
        pltpu.make_async_copy(pair_h.at[rows], cur.at[0, rows], load_sem.at[0]).start()
    for copy in params[:3]:
        copy.start()

    barrier = pltpu.get_barrier_semaphore()

    def greet(r, c):
        pl.semaphore_signal(
            barrier, inc=1, device_id=(r, c), device_id_type=pl.DeviceIdType.MESH
        )

    each_target(row, col, greet)
    for g in range(1, ROWS // GROUP):
        load(g).start()
    for copy in params[3:]:
        copy.start()
    for copy in params[:3]:
        copy.wait()
    for k in range(2, 4):
        wt[0, k * CH : (k + 1) * CH] = pw[0, k].T

    def norm_rows(u, base):
        x = cur[u, pl.ds(base, 2)].reshape(2 * COLS, CH).astype(F32)
        n = layer_norm(x, ng[u : u + 1], nb[u : u + 1]).astype(BF16)
        normed[pl.ds(base, 2)] = n.reshape(2, COLS, CH)
        return n

    def project(u, k, n):
        first = 256 * (1 - k)
        p = dot(wt[u, first : first + 256], n, NT)
        return sigmoid(p[0:128]) * p[128:256]

    def keep(u, first, wide):
        rows = pl.ds(pl.multiple_of(first, GROUP), GROUP)
        sides[u, :, rows, :] = wide[0 : CH * GROUP].reshape(CH, GROUP, COLS).astype(BF16)

    def front_group(u, k, base, first, fresh=True):
        for i in range(0, GROUP, 2):
            if fresh:
                n = norm_rows(u, base + i)
            else:
                n = normed[pl.ds(base + i, 2)].reshape(2 * COLS, CH)
            side = project(u, k, n)
            for r in range(2):
                (tr, tl)[k][pl.ds(i + r, CH, stride=GROUP), :] = side[:, r * COLS : (r + 1) * COLS]
        keep(u, first, (tr, tl)[k])

    def left_by_parts(half):
        def eight(p):
            for q in range(8):
                rows = [half * HALF + p * 8 + q + r * GROUP for r in range(2)]
                order = [(r, c) for part in range(2) for r in rows for c in (part, part + 2)]
                n = jnp.concatenate([normed[r, c * 32 : (c + 1) * 32] for r, c in order], axis=0)
                side = project(1, LEFT, n)
                for part, wide in enumerate((tl, tr)):
                    wide[pl.ds(p * 8 + q, CH, stride=GROUP), :] = side[
                        :, part * COLS : (part + 1) * COLS
                    ]

        loop(2, eight)
        keep(1, half * 48 + 32, tl)
        keep(1, half * 16 + 96, tr)

    def gate_rows(u, step):
        n = normed[pl.ds(step * 4, 4)].reshape(4 * COLS, CH)
        gate[pl.ds(step * 4, 4)] = sigmoid(dot(n, gw[u], NN)).reshape(4, COLS, CH)

    def back_group(u, g):
        base = g * GROUP
        back_rows(
            m_in[u, :, pl.ds(pl.multiple_of(base, GROUP), GROUP), :],
            cur.at[u, pl.ds(base, GROUP)],
            gate.at[pl.ds(base, GROUP)],
            cur.at[1 - u, pl.ds(base, GROUP)],
            gain_t.at[u], bias_t.at[u], ow.at[u], tl, ts,
        )

    def loop(count, body):
        def step(i, carry):
            body(i)
            return carry

        lax.fori_loop(0, count, step, 0)

    def rows_of(flight):
        return (*SIDES, *MIXED)[flight][2]

    def spread(flight, g=0):
        u, first, rows = (*SIDES, *MIXED)[flight]
        if isinstance(g, int) and g == 0:
            start = first
        else:
            start = pl.multiple_of(first + g * ((*SIDES, *MIXED)[flight + 1][1] - first), GROUP)
        part = pl.ds(start, rows)
        if flight < len(SIDES):
            src_at = lambda r, c: sides.at[u, r * N_COL + c, part]
            dst = all_sides.at[u, col, row, part]
        else:
            src_at = lambda r, c: m_all.at[u, c, r, part]
            dst = last_mixed.at[me] if flight == FLIGHTS - 1 else m_in.at[u, me, part]
        index = flight + g
        pltpu.make_async_copy(src_at(row, col), dst, recv_sem.at[index]).start()

        def send(r, c):
            pltpu.make_async_remote_copy(
                src_ref=src_at(r, c),
                dst_ref=dst,
                send_sem=send_sem.at[index],
                recv_sem=recv_sem.at[index],
                device_id=(r, c),
                device_id_type=pl.DeviceIdType.MESH,
            ).start()

        each_target(row, col, send)

    def arrived(flight, g=0):
        size = m_in.at[0, :, pl.ds(0, rows_of(flight))]
        pltpu.make_async_copy(size, size, recv_sem.at[flight + g]).wait()

    def sent(flight):
        size = m_in.at[0, pl.ds(0, DEV - 1), pl.ds(0, rows_of(flight))]
        pltpu.make_async_copy(size, size, send_sem.at[flight]).wait()

    def put_mixed(u, half, jb, out):
        out = out.astype(BF16)
        rows = pl.ds(half * HALF, HALF)
        for k in range(2):
            m_all[u, 2 * jb + k, :, rows, :] = out[:, k * COLS : (k + 1) * COLS].reshape(
                N_ROW, HALF, COLS
            )

    def side_rows(u, c, first, rows=GROUP):
        return all_sides[u, c, :, pl.ds(first, rows), :].reshape(N_ROW * rows, COLS)

    def mix_outgoing(half):
        first = pl.multiple_of(64 + half * HALF, HALF)
        a = jnp.concatenate([side_rows(0, c, first, HALF) for c in range(N_COL)], axis=1)

        def block(jb):
            b = jnp.concatenate(
                [all_sides[0, c, pl.ds(4 * jb, 4), 0:64].reshape(256, COLS) for c in range(N_COL)],
                axis=1,
            )
            put_mixed(0, half, jb, dot(a, b, NT))

        loop(4, block)

    def turn(half, part):
        def block(c):
            t = side_rows(1, c, half * 48 + 32 if part == 0 else half * 16 + 96).T
            for r in range(2):
                lt[half, pl.ds(2 * c, 2), part * HALF : (part + 1) * HALF, r * 256 : r * 256 + 256] = (
                    t[r * 64 : (r + 1) * 64].reshape(2, HALF, 256)
                )

        loop(N_COL, block)

    def mix_incoming(half, k):
        a = lt[k, :, half * HALF : (half + 1) * HALF, :].reshape(512, 512)

        def block(jb):
            b = jnp.concatenate(
                [
                    jnp.concatenate(
                        [
                            side_rows(1, 2 * jb + c, k * 48 + r * GROUP) for r in range(2)
                        ],
                        axis=0,
                    )
                    for c in range(2)
                ],
                axis=1,
            )
            if k == 0:
                acc[half, jb] = dot(a, b, NN)
            else:
                put_mixed(1, half, jb, acc[half, jb] + dot(a, b, NN))

        loop(4, block)


    def open_right(g):
        load(g).wait()
        front_group(0, RIGHT, g * GROUP, g * GROUP)

        @pl.when(g == 0)
        def _():
            pl.semaphore_wait(barrier, DEV - 1)

        spread(FIRST_RIGHT, g)

    loop(ROWS // GROUP, open_right)
    for copy in params[3:]:
        copy.wait()
    for k in range(2):
        wt[0, k * CH : (k + 1) * CH] = pw[0, k].T

    def open_left(half):
        def group(g):
            base = half * HALF + g * GROUP
            front_group(0, LEFT, base, 64 + base, False)

        loop(2, group)
        spread(FIRST_LEFT, half)

    loop(2, open_left)
    for k in range(4):
        wt[1, k * CH : (k + 1) * CH] = pw[1, k].T
    for u in range(2):
        gain_t[u] = jnp.broadcast_to(og[u : u + 1], (CH, CH)).T
        bias_t[u] = jnp.broadcast_to(ob[u : u + 1], (CH, CH)).T
    loop(ROWS // 4, lambda s: gate_rows(0, s))
    for g in range(ROWS // GROUP):
        arrived(FIRST_RIGHT, g)

    def outgoing(half):
        arrived(FIRST_LEFT, half)
        mix_outgoing(half)
        spread(FIRST_MIXED, half)

    loop(2, outgoing)

    def turnover(half):
        arrived(FIRST_MIXED, half)

        def group(g):
            back_group(0, 2 * half + g)
            front_group(1, RIGHT, half * HALF + g * GROUP, half * 48 + g * GROUP)

        loop(2, group)
        spread(NEXT_RIGHT, half)
        left_by_parts(half)
        spread(NEXT_LEFT, half)

    loop(2, turnover)
    spread(LAST_LEFT)
    loop(ROWS // 4, lambda s: gate_rows(1, s))
    last = pl.ds(HALF + GROUP, GROUP)
    ahead = [
        pltpu.make_async_copy(src, dst, ahead_sem.at[k])
        for k, (src, dst) in enumerate(((gate.at[last], last_gate), (cur.at[1, last], last_cur)))
    ]
    for copy in ahead:
        copy.start()
    for half in range(2):
        arrived(NEXT_RIGHT, half)
        arrived(NEXT_LEFT, half)
        turn(half, 0)
        mix_incoming(0, half)
    spread(NEXT_MIXED)
    arrived(LAST_LEFT)
    for half in range(2):
        turn(half, 1)
        mix_incoming(1, half)
    spread(NEXT_MIXED + 1)
    spread(NEXT_MIXED + 2)

    def store(g):
        rows = pl.ds(g * GROUP, GROUP)
        return pltpu.make_async_copy(cur.at[0, rows], out_h.at[rows], out_sem.at[g])

    def close(g):
        @pl.when(g == 0)
        def _():
            arrived(NEXT_MIXED)

        @pl.when(g == 2)
        def _():
            arrived(NEXT_MIXED + 1)

        back_group(1, g)
        store(g).start()

    loop(3, close)
    for flight in range(FLIGHTS):
        sent(flight)
    for copy in (*ahead, store(0), store(1), store(2)):
        copy.wait()
    arrived(NEXT_MIXED + 2)


def finish(
    done_h, mixed_h, gate_h, cur_h, og_h, ob_h, ow_h, out_h,
    done, mixed, gate, cur, og, ob, ow, new, gain_t, bias_t, tl, ts, sem, out_sem,
):
    def in_fours(src, dst, k):
        count = src.shape[0] // 4
        for part in range(4):
            rows = pl.ds(part * count, count)
            pltpu.make_async_copy(src.at[rows], dst.at[rows], sem.at[k]).start()
        return pltpu.make_async_copy(src, dst, sem.at[k])

    own_mixed = in_fours(mixed_h, mixed, 0)
    small = [
        pltpu.make_async_copy(src, dst, sem.at[1 + k])
        for k, (src, dst) in enumerate(((og_h, og), (ob_h, ob), (ow_h, ow)))
    ]
    for copy in small:
        copy.start()
    own_cur, own_gate = in_fours(cur_h, cur, 4), in_fours(gate_h, gate, 5)
    for copy in small:
        copy.wait()
    gain_t[...] = jnp.broadcast_to(og[1:2], (CH, CH)).T
    bias_t[...] = jnp.broadcast_to(ob[1:2], (CH, CH)).T
    blocks = [pl.ds(g * 16, 16) for g in range(3)]
    brought = [
        pltpu.make_async_copy(done_h.at[rows], done.at[rows], sem.at[6 + g])
        for g, rows in enumerate(blocks)
    ]
    carried = [
        pltpu.make_async_copy(done.at[rows], out_h.at[rows], out_sem.at[g])
        for g, rows in enumerate(blocks)
    ]
    own_mixed.wait()
    for copy in brought:
        copy.start()

    def ready():
        own_cur.wait()
        own_gate.wait()

    ends = [
        pltpu.make_async_copy(
            new.at[pl.ds(g * 4, 4)], out_h.at[pl.ds(48 + g * 4, 4)], out_sem.at[3 + g]
        )
        for g in range(4)
    ]

    def after(i):
        if i % 4 == 3:
            ends[i // 4].start()
            if i < 12:
                brought[i // 4].wait()
                carried[i // 4].start()

    back_rows(mixed[...], cur, gate, new, gain_t, bias_t, ow.at[1], tl, ts, ready, after)
    for copy in (*carried, *ends):
        copy.wait()


def shards(*args):
    pieces = (2, DEV, ROWS, COLS)
    planes = (2, N_COL, N_ROW, ROWS, COLS)
    vmem = pltpu.VMEM
    scratch = [
        vmem((2, ROWS, COLS, CH), BF16),
        vmem((ROWS, COLS, CH), BF16),
        vmem((ROWS, COLS, CH), F32),
        vmem((2, DEV, 2 * ROWS, COLS), BF16),
        vmem((2, N_COL, N_ROW, 2 * ROWS, COLS), BF16),
        vmem((2, N_ROW, ROWS, 512), BF16),
        vmem((2, 4, 512, 256), F32),
        vmem(planes, BF16),
        vmem(pieces, BF16),
    ]
    scratch += [vmem(a.shape, a.dtype) for a in args[1:]]
    scratch += [
        vmem((2, 4 * CH, CH), BF16),
        vmem((2, CH, CH), F32),
        vmem((2, CH, CH), F32),
        vmem((CH * GROUP + GROUP, COLS), F32),
        vmem((CH * GROUP + GROUP, COLS), F32),
        vmem((GROUP, COLS), F32),
        pltpu.SemaphoreType.DMA((ROWS // GROUP,)),
        pltpu.SemaphoreType.DMA((9,)),
        pltpu.SemaphoreType.DMA((FLIGHTS,)),
        pltpu.SemaphoreType.DMA((FLIGHTS,)),
        pltpu.SemaphoreType.DMA((3,)),
        pltpu.SemaphoreType.DMA((2,)),
    ]
    quarter = (GROUP, COLS, CH)
    of_kernel = [
        jax.ShapeDtypeStruct((ROWS - GROUP, COLS, CH), BF16),
        jax.ShapeDtypeStruct((DEV, GROUP, COLS), BF16),
        jax.ShapeDtypeStruct(quarter, F32),
        jax.ShapeDtypeStruct(quarter, BF16),
    ]
    parts = pl.pallas_call(
        kernel,
        out_shape=of_kernel,
        in_specs=[pl.BlockSpec(memory_space=pl.ANY)] * 8,
        out_specs=[pl.BlockSpec(memory_space=pl.ANY)] * 4,
        scratch_shapes=scratch,
        compiler_params=pltpu.CompilerParams(
            collective_id=0, has_side_effects=True, vmem_limit_bytes=60 * MIB
        ),
        name="triangle",
    )(*args)
    ends = args[5:]
    return pl.pallas_call(
        finish,
        out_shape=jax.ShapeDtypeStruct((ROWS, COLS, CH), BF16),
        in_specs=[pl.BlockSpec(memory_space=pl.ANY)] * 7,
        out_specs=pl.BlockSpec(memory_space=pl.ANY),
        scratch_shapes=[vmem(a.shape, a.dtype) for a in (*of_kernel, *ends)]
        + [
            vmem(quarter, BF16),
            vmem((CH, CH), F32),
            vmem((CH, CH), F32),
            vmem((CH * GROUP + GROUP, COLS), F32),
            vmem((GROUP, COLS), F32),
            pltpu.SemaphoreType.DMA((9,)),
            pltpu.SemaphoreType.DMA((7,)),
        ],
        compiler_params=pltpu.CompilerParams(vmem_limit_bytes=60 * MIB),
        name="finish",
    )(*parts, *ends)


def solution(mesh):
    placed = (P("row", "col", None), P(), P(), P(), P(), P(), P(), P())
    return jax.shard_map(
        shards, mesh=mesh, in_specs=placed, out_specs=P("row", "col", None), check_vma=False
    )
```

```python
import jax
import jax.numpy as jnp
from jax import lax
from jax.experimental import pallas as pl
from jax.experimental.pallas import tpu as pltpu
from jax.sharding import PartitionSpec as P

F32, BF16 = jnp.float32, jnp.bfloat16
ROWS, COLS, N_ROW, N_COL, CH = 64, 128, 16, 8, 128
DEV = N_ROW * N_COL
GROUP, HALF = 16, 32
MIB = 1 << 20
NT = (((1,), (1,)), ((), ()))
TN = (((0,), (0,)), ((), ()))
NN = (((1,), (0,)), ((), ()))
RIGHT, LEFT = 0, 1
SIDES = (
    (0, 0, 16), (0, 16, 16), (0, 32, 16), (0, 48, 16), (0, 64, 32), (0, 96, 32),
    (1, 0, 32), (1, 48, 32), (1, 32, 16), (1, 80, 16), (1, 96, 32),
)
MIXED = ((0, 0, 32), (0, 32, 32), (1, 0, 32), (1, 32, 16), (1, 48, 16))
FLIGHTS = len(SIDES) + len(MIXED)
FIRST_RIGHT, FIRST_LEFT, NEXT_RIGHT, NEXT_LEFT, LAST_LEFT, FIRST_MIXED, NEXT_MIXED = 0, 4, 6, 8, 10, 11, 13


def sigmoid(v):
    return 0.5 * jnp.tanh(0.5 * v) + 0.5


def layer_norm(v, gain, bias):
    mean = jnp.mean(v, axis=-1, keepdims=True)
    centred = v - mean
    var = jnp.mean(centred * centred, axis=-1, keepdims=True)
    return centred * lax.rsqrt(var + 1e-5) * gain + bias


def dot(a, b, dims):
    return lax.dot_general(a, b, dims, preferred_element_type=F32)


def each_target(row, col, body):
    y, zh, k = row // 4, lax.rem(row // 2, 2), lax.rem(row, 2)
    x, zl = col // 2, lax.rem(col, 2)
    sign = 1 - 2 * k
    turns = [sign * a + 4 for a in range(4)]
    xs = [lax.rem(x + turn, 4) * 2 for turn in turns]
    ys = [lax.rem(y + turn, 4) * 4 for turn in turns]

    def sixteen(core, c, skip):
        core_at = lax.rem(k + core, 2)
        z = [lax.rem(zh * 2 + zl + sign * c + 4 + turn, 4) for turn in turns]
        z_rows = [(at // 2) * 2 + core_at for at in z]
        z_cols = [lax.rem(at, 2) for at in z]
        for b in range(4):
            for a in range(4):
                if not (skip and a == 0 and b == 0):
                    ab = (a + b) % 4
                    body(ys[ab] + z_rows[ab], xs[a] + z_cols[ab])

    def step(p, carry):
        sixteen(p // 4, lax.rem(p, 4), False)
        return carry

    sixteen(0, 0, True)
    lax.fori_loop(1, 8, step, 0)


def back_rows(mixed, cur, gate, new, gain_t, bias_t, weight, tl, ts, ready=None, after=None):
    m = mixed.astype(F32)
    mean = jnp.mean(m, axis=0)
    centred = m - mean[None]
    var = jnp.mean(centred * centred, axis=0)
    ts[...] = lax.rsqrt(var + 1e-5)
    tl[0 : CH * GROUP] = centred.reshape(CH * GROUP, COLS)
    if ready is not None:
        ready()
    for i in range(GROUP):
        c = tl[pl.ds(i, CH, stride=GROUP), :]
        nm = (c * ts[pl.ds(i, 1), :] * gain_t[...] + bias_t[...]).astype(BF16)
        change = dot(nm, weight[...], TN)
        new[i] = (cur[i].astype(F32) + gate[i] * change).astype(BF16)
        if after is not None:
            after(i)


def kernel(
    pair_h, ng_h, nb_h, pw_h, gw_h, og_h, ob_h, ow_h, out_h, last_mixed, last_gate, last_cur,
    cur, normed, gate, sides, all_sides, lt, acc, m_all, m_in,
    ng, nb, pw, gw, og, ob, ow, wt, gain_t, bias_t, tl, tr, ts,
    load_sem, param_sem, send_sem, recv_sem, out_sem, ahead_sem,
):
    row, col = lax.axis_index("row"), lax.axis_index("col")
    me = row * N_COL + col

    def load(g):
        rows = pl.ds(g * GROUP, GROUP)
        return pltpu.make_async_copy(pair_h.at[rows], cur.at[0, rows], load_sem.at[g])

    first = pl.ds(2, 2)
    params = [
        pltpu.make_async_copy(src, dst, param_sem.at[k])
        for k, (src, dst) in enumerate(
            (
                (pw_h.at[0, first], pw.at[0, first]),
                (ng_h, ng),
                (nb_h, nb),
                (pw_h.at[0, pl.ds(0, 2)], pw.at[0, pl.ds(0, 2)]),
                (pw_h.at[1], pw.at[1]),
                (gw_h, gw),
                (og_h, og),
                (ob_h, ob),
                (ow_h, ow),
            )
        )
    ]
    for k in range(4):
        rows = pl.ds(4 * k, 4)
        pltpu.make_async_copy(pair_h.at[rows], cur.at[0, rows], load_sem.at[0]).start()
    for copy in params[:3]:
        copy.start()

    barrier = pltpu.get_barrier_semaphore()

    def greet(r, c):
        pl.semaphore_signal(
            barrier, inc=1, device_id=(r, c), device_id_type=pl.DeviceIdType.MESH
        )

    each_target(row, col, greet)
    for g in range(1, ROWS // GROUP):
        load(g).start()
    for copy in params[3:]:
        copy.start()
    for copy in params[:3]:
        copy.wait()
    for k in range(2, 4):
        wt[0, k * CH : (k + 1) * CH] = pw[0, k].T

    def norm_rows(u, base):
        x = cur[u, pl.ds(base, 2)].reshape(2 * COLS, CH).astype(F32)
        n = layer_norm(x, ng[u : u + 1], nb[u : u + 1]).astype(BF16)
        normed[pl.ds(base, 2)] = n.reshape(2, COLS, CH)
        return n

    def project(u, k, n):
        first = 256 * (1 - k)
        p = dot(wt[u, first : first + 256], n, NT)
        return sigmoid(p[0:128]) * p[128:256]

    def keep(u, first, wide):
        rows = pl.ds(pl.multiple_of(first, GROUP), GROUP)
        sides[u, :, rows, :] = wide[0 : CH * GROUP].reshape(CH, GROUP, COLS).astype(BF16)

    def front_group(u, k, base, first, fresh=True):
        for i in range(0, GROUP, 2):
            if fresh:
                n = norm_rows(u, base + i)
            else:
                n = normed[pl.ds(base + i, 2)].reshape(2 * COLS, CH)
            side = project(u, k, n)
            for r in range(2):
                (tr, tl)[k][pl.ds(i + r, CH, stride=GROUP), :] = side[:, r * COLS : (r + 1) * COLS]
        keep(u, first, (tr, tl)[k])

    def left_by_parts(half):
        def eight(p):
            for q in range(8):
                rows = [half * HALF + p * 8 + q + r * GROUP for r in range(2)]
                order = [(r, c) for part in range(2) for r in rows for c in (part, part + 2)]
                n = jnp.concatenate([normed[r, c * 32 : (c + 1) * 32] for r, c in order], axis=0)
                side = project(1, LEFT, n)
                for part, wide in enumerate((tl, tr)):
                    wide[pl.ds(p * 8 + q, CH, stride=GROUP), :] = side[
                        :, part * COLS : (part + 1) * COLS
                    ]

        loop(2, eight)
        keep(1, half * 48 + 32, tl)
        keep(1, half * 16 + 96, tr)

    def gate_rows(u, step):
        n = normed[pl.ds(step * 4, 4)].reshape(4 * COLS, CH)
        gate[pl.ds(step * 4, 4)] = sigmoid(dot(n, gw[u], NN)).reshape(4, COLS, CH)

    def back_group(u, g):
        base = g * GROUP
        back_rows(
            m_in[u, :, pl.ds(pl.multiple_of(base, GROUP), GROUP), :],
            cur.at[u, pl.ds(base, GROUP)],
            gate.at[pl.ds(base, GROUP)],
            cur.at[1 - u, pl.ds(base, GROUP)],
            gain_t.at[u], bias_t.at[u], ow.at[u], tl, ts,
        )

    def loop(count, body):
        def step(i, carry):
            body(i)
            return carry

        lax.fori_loop(0, count, step, 0)

    def rows_of(flight):
        return (*SIDES, *MIXED)[flight][2]

    def spread(flight, g=0):
        u, first, rows = (*SIDES, *MIXED)[flight]
        if isinstance(g, int) and g == 0:
            start = first
        else:
            start = pl.multiple_of(first + g * ((*SIDES, *MIXED)[flight + 1][1] - first), GROUP)
        part = pl.ds(start, rows)
        if flight < len(SIDES):
            src_at = lambda r, c: sides.at[u, r * N_COL + c, part]
            dst = all_sides.at[u, col, row, part]
        else:
            src_at = lambda r, c: m_all.at[u, c, r, part]
            dst = last_mixed.at[me] if flight == FLIGHTS - 1 else m_in.at[u, me, part]
        index = flight + g
        pltpu.make_async_copy(src_at(row, col), dst, recv_sem.at[index]).start()

        def send(r, c):
            pltpu.make_async_remote_copy(
                src_ref=src_at(r, c),
                dst_ref=dst,
                send_sem=send_sem.at[index],
                recv_sem=recv_sem.at[index],
                device_id=(r, c),
                device_id_type=pl.DeviceIdType.MESH,
            ).start()

        each_target(row, col, send)

    def arrived(flight, g=0):
        size = m_in.at[0, :, pl.ds(0, rows_of(flight))]
        pltpu.make_async_copy(size, size, recv_sem.at[flight + g]).wait()

    def sent(flight):
        size = m_in.at[0, pl.ds(0, DEV - 1), pl.ds(0, rows_of(flight))]
        pltpu.make_async_copy(size, size, send_sem.at[flight]).wait()

    def put_mixed(u, half, jb, out):
        out = out.astype(BF16)
        rows = pl.ds(half * HALF, HALF)
        for k in range(2):
            m_all[u, 2 * jb + k, :, rows, :] = out[:, k * COLS : (k + 1) * COLS].reshape(
                N_ROW, HALF, COLS
            )

    def side_rows(u, c, first, rows=GROUP):
        return all_sides[u, c, :, pl.ds(first, rows), :].reshape(N_ROW * rows, COLS)

    def mix_outgoing(half):
        first = pl.multiple_of(64 + half * HALF, HALF)
        a = jnp.concatenate([side_rows(0, c, first, HALF) for c in range(N_COL)], axis=1)

        def block(jb):
            b = jnp.concatenate(
                [all_sides[0, c, pl.ds(4 * jb, 4), 0:64].reshape(256, COLS) for c in range(N_COL)],
                axis=1,
            )
            put_mixed(0, half, jb, dot(a, b, NT))

        loop(4, block)

    def turn(half, part):
        def block(c):
            t = side_rows(1, c, half * 48 + 32 if part == 0 else half * 16 + 96).T
            for r in range(2):
                lt[half, pl.ds(2 * c, 2), part * HALF : (part + 1) * HALF, r * 256 : r * 256 + 256] = (
                    t[r * 64 : (r + 1) * 64].reshape(2, HALF, 256)
                )

        loop(N_COL, block)

    def mix_incoming(half, k):
        a = lt[k, :, half * HALF : (half + 1) * HALF, :].reshape(512, 512)

        def block(jb):
            b = jnp.concatenate(
                [
                    jnp.concatenate(
                        [
                            side_rows(1, 2 * jb + c, k * 48 + r * GROUP) for r in range(2)
                        ],
                        axis=0,
                    )
                    for c in range(2)
                ],
                axis=1,
            )
            if k == 0:
                acc[half, jb] = dot(a, b, NN)
            else:
                put_mixed(1, half, jb, acc[half, jb] + dot(a, b, NN))

        loop(4, block)


    def open_right(g):
        load(g).wait()
        front_group(0, RIGHT, g * GROUP, g * GROUP)

        @pl.when(g == 0)
        def _():
            pl.semaphore_wait(barrier, DEV - 1)

        spread(FIRST_RIGHT, g)

    loop(ROWS // GROUP, open_right)
    for copy in params[3:]:
        copy.wait()
    for k in range(2):
        wt[0, k * CH : (k + 1) * CH] = pw[0, k].T

    def open_left(half):
        def group(g):
            base = half * HALF + g * GROUP
            front_group(0, LEFT, base, 64 + base, False)

        loop(2, group)
        spread(FIRST_LEFT, half)

    loop(2, open_left)
    for k in range(4):
        wt[1, k * CH : (k + 1) * CH] = pw[1, k].T
    for u in range(2):
        gain_t[u] = jnp.broadcast_to(og[u : u + 1], (CH, CH)).T
        bias_t[u] = jnp.broadcast_to(ob[u : u + 1], (CH, CH)).T
    loop(ROWS // 4, lambda s: gate_rows(0, s))
    for g in range(ROWS // GROUP):
        arrived(FIRST_RIGHT, g)

    def outgoing(half):
        arrived(FIRST_LEFT, half)
        mix_outgoing(half)
        spread(FIRST_MIXED, half)

    loop(2, outgoing)

    def turnover(half):
        arrived(FIRST_MIXED, half)

        def group(g):
            back_group(0, 2 * half + g)
            front_group(1, RIGHT, half * HALF + g * GROUP, half * 48 + g * GROUP)

        loop(2, group)
        spread(NEXT_RIGHT, half)
        left_by_parts(half)
        spread(NEXT_LEFT, half)

    loop(2, turnover)
    spread(LAST_LEFT)
    loop(ROWS // 4, lambda s: gate_rows(1, s))
    last = pl.ds(HALF + GROUP, GROUP)
    ahead = [
        pltpu.make_async_copy(src, dst, ahead_sem.at[k])
        for k, (src, dst) in enumerate(((gate.at[last], last_gate), (cur.at[1, last], last_cur)))
    ]
    for copy in ahead:
        copy.start()
    for half in range(2):
        arrived(NEXT_RIGHT, half)
        arrived(NEXT_LEFT, half)
        turn(half, 0)
        mix_incoming(0, half)
    spread(NEXT_MIXED)
    arrived(LAST_LEFT)
    for half in range(2):
        turn(half, 1)
        mix_incoming(1, half)
    spread(NEXT_MIXED + 1)
    spread(NEXT_MIXED + 2)

    def store(g):
        rows = pl.ds(g * GROUP, GROUP)
        return pltpu.make_async_copy(cur.at[0, rows], out_h.at[rows], out_sem.at[g])

    def close(g):
        @pl.when(g == 0)
        def _():
            arrived(NEXT_MIXED)

        @pl.when(g == 2)
        def _():
            arrived(NEXT_MIXED + 1)

        back_group(1, g)
        store(g).start()

    loop(3, close)
    for flight in range(FLIGHTS):
        sent(flight)
    for copy in (*ahead, store(0), store(1), store(2)):
        copy.wait()
    arrived(NEXT_MIXED + 2)


def finish(
    done_h, mixed_h, gate_h, cur_h, og_h, ob_h, ow_h, out_h,
    done, mixed, gate, cur, og, ob, ow, new, gain_t, bias_t, tl, ts, sem, out_sem,
):
    def in_fours(src, dst, k):
        count = src.shape[0] // 4
        for part in range(4):
            rows = pl.ds(part * count, count)
            pltpu.make_async_copy(src.at[rows], dst.at[rows], sem.at[k]).start()
        return pltpu.make_async_copy(src, dst, sem.at[k])

    own_mixed = in_fours(mixed_h, mixed, 0)
    small = [
        pltpu.make_async_copy(src, dst, sem.at[1 + k])
        for k, (src, dst) in enumerate(((og_h, og), (ob_h, ob), (ow_h, ow)))
    ]
    for copy in small:
        copy.start()
    own_cur, own_gate = in_fours(cur_h, cur, 4), in_fours(gate_h, gate, 5)
    for copy in small:
        copy.wait()
    gain_t[...] = jnp.broadcast_to(og[1:2], (CH, CH)).T
    bias_t[...] = jnp.broadcast_to(ob[1:2], (CH, CH)).T
    blocks = [pl.ds(g * 16, 16) for g in range(3)]
    brought = [
        pltpu.make_async_copy(done_h.at[rows], done.at[rows], sem.at[6 + g])
        for g, rows in enumerate(blocks)
    ]
    carried = [
        pltpu.make_async_copy(done.at[rows], out_h.at[rows], out_sem.at[g])
        for g, rows in enumerate(blocks)
    ]
    for copy in brought:
        copy.start()
    own_mixed.wait()

    def ready():
        own_cur.wait()
        own_gate.wait()
        for come, go in zip(brought, carried):
            come.wait()
            go.start()

    ends = [
        pltpu.make_async_copy(
            new.at[pl.ds(g * 4, 4)], out_h.at[pl.ds(48 + g * 4, 4)], out_sem.at[3 + g]
        )
        for g in range(4)
    ]

    def after(i):
        if i % 4 == 3:
            ends[i // 4].start()

    back_rows(mixed[...], cur, gate, new, gain_t, bias_t, ow.at[1], tl, ts, ready, after)
    for copy in (*carried, *ends):
        copy.wait()


def shards(*args):
    pieces = (2, DEV, ROWS, COLS)
    planes = (2, N_COL, N_ROW, ROWS, COLS)
    vmem = pltpu.VMEM
    scratch = [
        vmem((2, ROWS, COLS, CH), BF16),
        vmem((ROWS, COLS, CH), BF16),
        vmem((ROWS, COLS, CH), F32),
        vmem((2, DEV, 2 * ROWS, COLS), BF16),
        vmem((2, N_COL, N_ROW, 2 * ROWS, COLS), BF16),
        vmem((2, N_ROW, ROWS, 512), BF16),
        vmem((2, 4, 512, 256), F32),
        vmem(planes, BF16),
        vmem(pieces, BF16),
    ]
    scratch += [vmem(a.shape, a.dtype) for a in args[1:]]
    scratch += [
        vmem((2, 4 * CH, CH), BF16),
        vmem((2, CH, CH), F32),
        vmem((2, CH, CH), F32),
        vmem((CH * GROUP + GROUP, COLS), F32),
        vmem((CH * GROUP + GROUP, COLS), F32),
        vmem((GROUP, COLS), F32),
        pltpu.SemaphoreType.DMA((ROWS // GROUP,)),
        pltpu.SemaphoreType.DMA((9,)),
        pltpu.SemaphoreType.DMA((FLIGHTS,)),
        pltpu.SemaphoreType.DMA((FLIGHTS,)),
        pltpu.SemaphoreType.DMA((3,)),
        pltpu.SemaphoreType.DMA((2,)),
    ]
    quarter = (GROUP, COLS, CH)
    of_kernel = [
        jax.ShapeDtypeStruct((ROWS - GROUP, COLS, CH), BF16),
        jax.ShapeDtypeStruct((DEV, GROUP, COLS), BF16),
        jax.ShapeDtypeStruct(quarter, F32),
        jax.ShapeDtypeStruct(quarter, BF16),
    ]
    parts = pl.pallas_call(
        kernel,
        out_shape=of_kernel,
        in_specs=[pl.BlockSpec(memory_space=pl.ANY)] * 8,
        out_specs=[pl.BlockSpec(memory_space=pl.ANY)] * 4,
        scratch_shapes=scratch,
        compiler_params=pltpu.CompilerParams(
            collective_id=0, has_side_effects=True, vmem_limit_bytes=60 * MIB
        ),
        name="triangle",
    )(*args)
    ends = args[5:]
    return pl.pallas_call(
        finish,
        out_shape=jax.ShapeDtypeStruct((ROWS, COLS, CH), BF16),
        in_specs=[pl.BlockSpec(memory_space=pl.ANY)] * 7,
        out_specs=pl.BlockSpec(memory_space=pl.ANY),
        scratch_shapes=[vmem(a.shape, a.dtype) for a in (*of_kernel, *ends)]
        + [
            vmem(quarter, BF16),
            vmem((CH, CH), F32),
            vmem((CH, CH), F32),
            vmem((CH * GROUP + GROUP, COLS), F32),
            vmem((GROUP, COLS), F32),
            pltpu.SemaphoreType.DMA((9,)),
            pltpu.SemaphoreType.DMA((7,)),
        ],
        compiler_params=pltpu.CompilerParams(vmem_limit_bytes=60 * MIB),
        name="finish",
    )(*parts, *ends)


def solution(mesh):
    placed = (P("row", "col", None), P(), P(), P(), P(), P(), P(), P())
    return jax.shard_map(
        shards, mesh=mesh, in_specs=placed, out_specs=P("row", "col", None), check_vma=False
    )
```

```python
import jax
import jax.numpy as jnp
from jax import lax
from jax.experimental import pallas as pl
from jax.experimental.pallas import tpu as pltpu
from jax.sharding import PartitionSpec as P

F32, BF16 = jnp.float32, jnp.bfloat16
ROWS, COLS, N_ROW, N_COL, CH = 64, 128, 16, 8, 128
DEV = N_ROW * N_COL
GROUP, HALF = 16, 32
MIB = 1 << 20
NT = (((1,), (1,)), ((), ()))
TN = (((0,), (0,)), ((), ()))
NN = (((1,), (0,)), ((), ()))
RIGHT, LEFT = 0, 1
SIDES = (
    (0, 0, 16), (0, 16, 16), (0, 32, 16), (0, 48, 16), (0, 64, 32), (0, 96, 32),
    (1, 0, 32), (1, 48, 32), (1, 32, 16), (1, 80, 16), (1, 96, 32),
)
MIXED = ((0, 0, 32), (0, 32, 32), (1, 0, 32), (1, 32, 16), (1, 48, 16))
FLIGHTS = len(SIDES) + len(MIXED)
FIRST_RIGHT, FIRST_LEFT, NEXT_RIGHT, NEXT_LEFT, LAST_LEFT, FIRST_MIXED, NEXT_MIXED = 0, 4, 6, 8, 10, 11, 13


def sigmoid(v):
    return 0.5 * jnp.tanh(0.5 * v) + 0.5


def layer_norm(v, gain, bias):
    mean = jnp.mean(v, axis=-1, keepdims=True)
    centred = v - mean
    var = jnp.mean(centred * centred, axis=-1, keepdims=True)
    return centred * lax.rsqrt(var + 1e-5) * gain + bias


def dot(a, b, dims):
    return lax.dot_general(a, b, dims, preferred_element_type=F32)


def each_target(row, col, body):
    y, zh, k = row // 4, lax.rem(row // 2, 2), lax.rem(row, 2)
    x, zl = col // 2, lax.rem(col, 2)
    sign = 1 - 2 * k
    turns = [sign * a + 4 for a in range(4)]
    xs = [lax.rem(x + turn, 4) * 2 for turn in turns]
    ys = [lax.rem(y + turn, 4) * 4 for turn in turns]

    def sixteen(core, c, skip):
        core_at = lax.rem(k + core, 2)
        z = [lax.rem(zh * 2 + zl + sign * c + 4 + turn, 4) for turn in turns]
        z_rows = [(at // 2) * 2 + core_at for at in z]
        z_cols = [lax.rem(at, 2) for at in z]
        for b in range(4):
            for a in range(4):
                if not (skip and a == 0 and b == 0):
                    ab = (a + b) % 4
                    body(ys[ab] + z_rows[ab], xs[a] + z_cols[ab])

    def step(p, carry):
        sixteen(p // 4, lax.rem(p, 4), False)
        return carry

    sixteen(0, 0, True)
    lax.fori_loop(1, 8, step, 0)


def back_rows(mixed, cur, gate, new, gain_t, bias_t, weight, tl, ts, ready=None, after=None):
    m = mixed.astype(F32)
    mean = jnp.mean(m, axis=0)
    centred = m - mean[None]
    var = jnp.mean(centred * centred, axis=0)
    ts[...] = lax.rsqrt(var + 1e-5)
    tl[0 : CH * GROUP] = centred.reshape(CH * GROUP, COLS)
    if ready is not None:
        ready()
    for i in range(GROUP):
        c = tl[pl.ds(i, CH, stride=GROUP), :]
        nm = (c * ts[pl.ds(i, 1), :] * gain_t[...] + bias_t[...]).astype(BF16)
        change = dot(nm, weight[...], TN)
        new[i] = (cur[i].astype(F32) + gate[i] * change).astype(BF16)
        if after is not None:
            after(i)


def kernel(
    pair_h, ng_h, nb_h, pw_h, gw_h, og_h, ob_h, ow_h, out_h, last_mixed, last_gate, last_cur,
    cur, normed, gate, sides, all_sides, lt, acc, m_all, m_in,
    ng, nb, pw, gw, og, ob, ow, wt, gain_t, bias_t, tl, tr, ts,
    load_sem, param_sem, send_sem, recv_sem, out_sem, ahead_sem,
):
    row, col = lax.axis_index("row"), lax.axis_index("col")
    me = row * N_COL + col

    def load(g):
        rows = pl.ds(g * GROUP, GROUP)
        return pltpu.make_async_copy(pair_h.at[rows], cur.at[0, rows], load_sem.at[g])

    first = pl.ds(2, 2)
    params = [
        pltpu.make_async_copy(src, dst, param_sem.at[k])
        for k, (src, dst) in enumerate(
            (
                (pw_h.at[0, first], pw.at[0, first]),
                (ng_h, ng),
                (nb_h, nb),
                (pw_h.at[0, pl.ds(0, 2)], pw.at[0, pl.ds(0, 2)]),
                (pw_h.at[1], pw.at[1]),
                (gw_h, gw),
                (og_h, og),
                (ob_h, ob),
                (ow_h, ow),
            )
        )
    ]
    load(0).start()
    for copy in params[:3]:
        copy.start()

    barrier = pltpu.get_barrier_semaphore()

    def greet(r, c):
        pl.semaphore_signal(
            barrier, inc=1, device_id=(r, c), device_id_type=pl.DeviceIdType.MESH
        )

    each_target(row, col, greet)
    for g in range(1, ROWS // GROUP):
        load(g).start()
    for copy in params[3:]:
        copy.start()
    for copy in params[:3]:
        copy.wait()
    for k in range(2, 4):
        wt[0, k * CH : (k + 1) * CH] = pw[0, k].T

    def norm_rows(u, base):
        x = cur[u, pl.ds(base, 2)].reshape(2 * COLS, CH).astype(F32)
        n = layer_norm(x, ng[u : u + 1], nb[u : u + 1]).astype(BF16)
        normed[pl.ds(base, 2)] = n.reshape(2, COLS, CH)
        return n

    def project(u, k, n):
        first = 256 * (1 - k)
        p = dot(wt[u, first : first + 256], n, NT)
        return sigmoid(p[0:128]) * p[128:256]

    def keep(u, first, wide):
        rows = pl.ds(pl.multiple_of(first, GROUP), GROUP)
        sides[u, :, rows, :] = wide[0 : CH * GROUP].reshape(CH, GROUP, COLS).astype(BF16)

    def front_group(u, k, base, first, fresh=True):
        for i in range(0, GROUP, 2):
            if fresh:
                n = norm_rows(u, base + i)
            else:
                n = normed[pl.ds(base + i, 2)].reshape(2 * COLS, CH)
            side = project(u, k, n)
            for r in range(2):
                (tr, tl)[k][pl.ds(i + r, CH, stride=GROUP), :] = side[:, r * COLS : (r + 1) * COLS]
        keep(u, first, (tr, tl)[k])

    def left_by_parts(half):
        def eight(p):
            for q in range(8):
                rows = [half * HALF + p * 8 + q + r * GROUP for r in range(2)]
                order = [(r, c) for part in range(2) for r in rows for c in (part, part + 2)]
                n = jnp.concatenate([normed[r, c * 32 : (c + 1) * 32] for r, c in order], axis=0)
                side = project(1, LEFT, n)
                for part, wide in enumerate((tl, tr)):
                    wide[pl.ds(p * 8 + q, CH, stride=GROUP), :] = side[
                        :, part * COLS : (part + 1) * COLS
                    ]

        loop(2, eight)
        keep(1, half * 48 + 32, tl)
        keep(1, half * 16 + 96, tr)

    def gate_rows(u, step):
        n = normed[pl.ds(step * 4, 4)].reshape(4 * COLS, CH)
        gate[pl.ds(step * 4, 4)] = sigmoid(dot(n, gw[u], NN)).reshape(4, COLS, CH)

    def back_group(u, g):
        base = g * GROUP
        back_rows(
            m_in[u, :, pl.ds(pl.multiple_of(base, GROUP), GROUP), :],
            cur.at[u, pl.ds(base, GROUP)],
            gate.at[pl.ds(base, GROUP)],
            cur.at[1 - u, pl.ds(base, GROUP)],
            gain_t.at[u], bias_t.at[u], ow.at[u], tl, ts,
        )

    def loop(count, body):
        def step(i, carry):
            body(i)
            return carry

        lax.fori_loop(0, count, step, 0)

    def rows_of(flight):
        return (*SIDES, *MIXED)[flight][2]

    def spread(flight, g=0):
        u, first, rows = (*SIDES, *MIXED)[flight]
        if isinstance(g, int) and g == 0:
            start = first
        else:
            start = pl.multiple_of(first + g * ((*SIDES, *MIXED)[flight + 1][1] - first), GROUP)
        part = pl.ds(start, rows)
        if flight < len(SIDES):
            src_at = lambda r, c: sides.at[u, r * N_COL + c, part]
            dst = all_sides.at[u, col, row, part]
        else:
            src_at = lambda r, c: m_all.at[u, c, r, part]
            dst = last_mixed.at[me] if flight == FLIGHTS - 1 else m_in.at[u, me, part]
        index = flight + g
        pltpu.make_async_copy(src_at(row, col), dst, recv_sem.at[index]).start()

        def send(r, c):
            pltpu.make_async_remote_copy(
                src_ref=src_at(r, c),
                dst_ref=dst,
                send_sem=send_sem.at[index],
                recv_sem=recv_sem.at[index],
                device_id=(r, c),
                device_id_type=pl.DeviceIdType.MESH,
            ).start()

        each_target(row, col, send)

    def arrived(flight, g=0):
        size = m_in.at[0, :, pl.ds(0, rows_of(flight))]
        pltpu.make_async_copy(size, size, recv_sem.at[flight + g]).wait()

    def sent(flight):
        size = m_in.at[0, pl.ds(0, DEV - 1), pl.ds(0, rows_of(flight))]
        pltpu.make_async_copy(size, size, send_sem.at[flight]).wait()

    def put_mixed(u, half, jb, out):
        out = out.astype(BF16)
        rows = pl.ds(half * HALF, HALF)
        for k in range(2):
            m_all[u, 2 * jb + k, :, rows, :] = out[:, k * COLS : (k + 1) * COLS].reshape(
                N_ROW, HALF, COLS
            )

    def side_rows(u, c, first, rows=GROUP):
        return all_sides[u, c, :, pl.ds(first, rows), :].reshape(N_ROW * rows, COLS)

    def mix_outgoing(half):
        first = pl.multiple_of(64 + half * HALF, HALF)
        a = jnp.concatenate([side_rows(0, c, first, HALF) for c in range(N_COL)], axis=1)

        def block(jb):
            b = jnp.concatenate(
                [all_sides[0, c, pl.ds(4 * jb, 4), 0:64].reshape(256, COLS) for c in range(N_COL)],
                axis=1,
            )
            put_mixed(0, half, jb, dot(a, b, NT))

        loop(4, block)

    def turn(half, part):
        def block(c):
            t = side_rows(1, c, half * 48 + 32 if part == 0 else half * 16 + 96).T
            for r in range(2):
                lt[half, pl.ds(2 * c, 2), part * HALF : (part + 1) * HALF, r * 256 : r * 256 + 256] = (
                    t[r * 64 : (r + 1) * 64].reshape(2, HALF, 256)
                )

        loop(N_COL, block)

    def mix_incoming(half, k):
        a = lt[k, :, half * HALF : (half + 1) * HALF, :].reshape(512, 512)

        def block(jb):
            b = jnp.concatenate(
                [
                    jnp.concatenate(
                        [
                            side_rows(1, 2 * jb + c, k * 48 + r * GROUP) for r in range(2)
                        ],
                        axis=0,
                    )
                    for c in range(2)
                ],
                axis=1,
            )
            if k == 0:
                acc[half, jb] = dot(a, b, NN)
            else:
                put_mixed(1, half, jb, acc[half, jb] + dot(a, b, NN))

        loop(4, block)


    def open_right(g):
        load(g).wait()
        front_group(0, RIGHT, g * GROUP, g * GROUP)

        @pl.when(g == 0)
        def _():
            pl.semaphore_wait(barrier, DEV - 1)

        spread(FIRST_RIGHT, g)

    loop(ROWS // GROUP, open_right)
    for copy in params[3:]:
        copy.wait()
    for k in range(2):
        wt[0, k * CH : (k + 1) * CH] = pw[0, k].T

    def open_left(half):
        def group(g):
            base = half * HALF + g * GROUP
            front_group(0, LEFT, base, 64 + base, False)

        loop(2, group)
        spread(FIRST_LEFT, half)

    loop(2, open_left)
    for k in range(4):
        wt[1, k * CH : (k + 1) * CH] = pw[1, k].T
    for u in range(2):
        gain_t[u] = jnp.broadcast_to(og[u : u + 1], (CH, CH)).T
        bias_t[u] = jnp.broadcast_to(ob[u : u + 1], (CH, CH)).T
    loop(ROWS // 4, lambda s: gate_rows(0, s))
    for g in range(ROWS // GROUP):
        arrived(FIRST_RIGHT, g)

    def outgoing(half):
        arrived(FIRST_LEFT, half)
        mix_outgoing(half)
        spread(FIRST_MIXED, half)

    loop(2, outgoing)

    def turnover(half):
        arrived(FIRST_MIXED, half)

        def group(g):
            back_group(0, 2 * half + g)
            front_group(1, RIGHT, half * HALF + g * GROUP, half * 48 + g * GROUP)

        loop(2, group)
        spread(NEXT_RIGHT, half)
        left_by_parts(half)
        spread(NEXT_LEFT, half)

    loop(2, turnover)
    spread(LAST_LEFT)
    loop(ROWS // 4, lambda s: gate_rows(1, s))
    last = pl.ds(HALF + GROUP, GROUP)
    ahead = [
        pltpu.make_async_copy(src, dst, ahead_sem.at[k])
        for k, (src, dst) in enumerate(((gate.at[last], last_gate), (cur.at[1, last], last_cur)))
    ]
    for copy in ahead:
        copy.start()
    for half in range(2):
        arrived(NEXT_RIGHT, half)
        arrived(NEXT_LEFT, half)
        turn(half, 0)
        mix_incoming(0, half)
    spread(NEXT_MIXED)
    arrived(LAST_LEFT)
    for half in range(2):
        turn(half, 1)
        mix_incoming(1, half)
    spread(NEXT_MIXED + 1)
    spread(NEXT_MIXED + 2)

    def store(g):
        rows = pl.ds(g * GROUP, GROUP)
        return pltpu.make_async_copy(cur.at[0, rows], out_h.at[rows], out_sem.at[g])

    def close(g):
        @pl.when(g == 0)
        def _():
            arrived(NEXT_MIXED)

        @pl.when(g == 2)
        def _():
            arrived(NEXT_MIXED + 1)

        back_group(1, g)
        store(g).start()

    loop(3, close)
    for flight in range(FLIGHTS):
        sent(flight)
    for copy in (*ahead, store(0), store(1), store(2)):
        copy.wait()
    arrived(NEXT_MIXED + 2)


def finish(
    done_h, mixed_h, gate_h, cur_h, og_h, ob_h, ow_h, out_h,
    done, mixed, gate, cur, og, ob, ow, new, gain_t, bias_t, tl, ts, sem, out_sem,
):
    loads = [
        pltpu.make_async_copy(src, dst, sem.at[k])
        for k, (src, dst) in enumerate(
            (
                (mixed_h, mixed), (og_h, og), (ob_h, ob), (ow_h, ow), (cur_h, cur), (gate_h, gate),
                (done_h, done),
            )
        )
    ]
    for copy in loads:
        copy.start()
    for copy in loads[1:4]:
        copy.wait()
    gain_t[...] = jnp.broadcast_to(og[1:2], (CH, CH)).T
    bias_t[...] = jnp.broadcast_to(ob[1:2], (CH, CH)).T
    kept = pl.ds(0, ROWS - GROUP)
    carried = pltpu.make_async_copy(done, out_h.at[kept], out_sem.at[0])
    loads[0].wait()

    def ready():
        for copy in loads[4:]:
            copy.wait()
        carried.start()

    ends = [
        pltpu.make_async_copy(
            new.at[pl.ds(g * 8, 8)], out_h.at[pl.ds(48 + g * 8, 8)], out_sem.at[1 + g]
        )
        for g in range(2)
    ]

    def after(i):
        if i % 8 == 7:
            ends[i // 8].start()

    back_rows(mixed[...], cur, gate, new, gain_t, bias_t, ow.at[1], tl, ts, ready, after)
    for copy in (carried, *ends):
        copy.wait()


def shards(*args):
    pieces = (2, DEV, ROWS, COLS)
    planes = (2, N_COL, N_ROW, ROWS, COLS)
    vmem = pltpu.VMEM
    scratch = [
        vmem((2, ROWS, COLS, CH), BF16),
        vmem((ROWS, COLS, CH), BF16),
        vmem((ROWS, COLS, CH), F32),
        vmem((2, DEV, 2 * ROWS, COLS), BF16),
        vmem((2, N_COL, N_ROW, 2 * ROWS, COLS), BF16),
        vmem((2, N_ROW, ROWS, 512), BF16),
        vmem((2, 4, 512, 256), F32),
        vmem(planes, BF16),
        vmem(pieces, BF16),
    ]
    scratch += [vmem(a.shape, a.dtype) for a in args[1:]]
    scratch += [
        vmem((2, 4 * CH, CH), BF16),
        vmem((2, CH, CH), F32),
        vmem((2, CH, CH), F32),
        vmem((CH * GROUP + GROUP, COLS), F32),
        vmem((CH * GROUP + GROUP, COLS), F32),
        vmem((GROUP, COLS), F32),
        pltpu.SemaphoreType.DMA((ROWS // GROUP,)),
        pltpu.SemaphoreType.DMA((9,)),
        pltpu.SemaphoreType.DMA((FLIGHTS,)),
        pltpu.SemaphoreType.DMA((FLIGHTS,)),
        pltpu.SemaphoreType.DMA((3,)),
        pltpu.SemaphoreType.DMA((2,)),
    ]
    quarter = (GROUP, COLS, CH)
    of_kernel = [
        jax.ShapeDtypeStruct((ROWS - GROUP, COLS, CH), BF16),
        jax.ShapeDtypeStruct((DEV, GROUP, COLS), BF16),
        jax.ShapeDtypeStruct(quarter, F32),
        jax.ShapeDtypeStruct(quarter, BF16),
    ]
    parts = pl.pallas_call(
        kernel,
        out_shape=of_kernel,
        in_specs=[pl.BlockSpec(memory_space=pl.ANY)] * 8,
        out_specs=[pl.BlockSpec(memory_space=pl.ANY)] * 4,
        scratch_shapes=scratch,
        compiler_params=pltpu.CompilerParams(
            collective_id=0, has_side_effects=True, vmem_limit_bytes=60 * MIB
        ),
        name="triangle",
    )(*args)
    ends = args[5:]
    return pl.pallas_call(
        finish,
        out_shape=jax.ShapeDtypeStruct((ROWS, COLS, CH), BF16),
        in_specs=[pl.BlockSpec(memory_space=pl.ANY)] * 7,
        out_specs=pl.BlockSpec(memory_space=pl.ANY),
        scratch_shapes=[vmem(a.shape, a.dtype) for a in (*of_kernel, *ends)]
        + [
            vmem(quarter, BF16),
            vmem((CH, CH), F32),
            vmem((CH, CH), F32),
            vmem((CH * GROUP + GROUP, COLS), F32),
            vmem((GROUP, COLS), F32),
            pltpu.SemaphoreType.DMA((7,)),
            pltpu.SemaphoreType.DMA((3,)),
        ],
        compiler_params=pltpu.CompilerParams(vmem_limit_bytes=60 * MIB),
        name="finish",
    )(*parts, *ends)


def solution(mesh):
    placed = (P("row", "col", None), P(), P(), P(), P(), P(), P(), P())
    return jax.shard_map(
        shards, mesh=mesh, in_specs=placed, out_specs=P("row", "col", None), check_vma=False
    )
```

```python
import jax
import jax.numpy as jnp
from jax import lax
from jax.experimental import pallas as pl
from jax.experimental.pallas import tpu as pltpu
from jax.sharding import PartitionSpec as P

F32, BF16 = jnp.float32, jnp.bfloat16
ROWS, COLS, N_ROW, N_COL, CH = 64, 128, 16, 8, 128
DEV = N_ROW * N_COL
GROUP, HALF = 16, 32
MIB = 1 << 20
NT = (((1,), (1,)), ((), ()))
TN = (((0,), (0,)), ((), ()))
NN = (((1,), (0,)), ((), ()))
RIGHT, LEFT = 0, 1
SIDES = (
    (0, 0, 16), (0, 16, 16), (0, 32, 16), (0, 48, 16), (0, 64, 32), (0, 96, 32),
    (1, 0, 32), (1, 48, 32), (1, 32, 16), (1, 80, 16), (1, 96, 32),
)
MIXED = ((0, 0, 32), (0, 32, 32), (1, 0, 32), (1, 32, 16), (1, 48, 16))
FLIGHTS = len(SIDES) + len(MIXED)
FIRST_RIGHT, FIRST_LEFT, NEXT_RIGHT, NEXT_LEFT, LAST_LEFT, FIRST_MIXED, NEXT_MIXED = 0, 4, 6, 8, 10, 11, 13


def sigmoid(v):
    return 0.5 * jnp.tanh(0.5 * v) + 0.5


def layer_norm(v, gain, bias):
    mean = jnp.mean(v, axis=-1, keepdims=True)
    centred = v - mean
    var = jnp.mean(centred * centred, axis=-1, keepdims=True)
    return centred * lax.rsqrt(var + 1e-5) * gain + bias


def dot(a, b, dims):
    return lax.dot_general(a, b, dims, preferred_element_type=F32)


def each_target(row, col, body):
    y, zh, k = row // 4, lax.rem(row // 2, 2), lax.rem(row, 2)
    x, zl = col // 2, lax.rem(col, 2)
    sign = 1 - 2 * k
    turns = [sign * a + 4 for a in range(4)]
    xs = [lax.rem(x + turn, 4) * 2 for turn in turns]
    ys = [lax.rem(y + turn, 4) * 4 for turn in turns]
    x_of = {(a, d): xs[a] + k * (xs[d] - xs[a]) for a in range(4) for d in range(4)}
    y_of = {(a, d): ys[d] + k * (ys[a] - ys[d]) for a in range(4) for d in range(4)}

    def sixteen(core, c, skip):
        core_at = lax.rem(k + core, 2)
        z = [lax.rem(zh * 2 + zl + sign * c + 4 + turn, 4) for turn in turns]
        z_rows = [(at // 2) * 2 + core_at for at in z]
        z_cols = [lax.rem(at, 2) for at in z]
        for b in range(4):
            for a in range(4):
                if not (skip and a == 0 and b == 0):
                    ab = (a + b) % 4
                    body(y_of[a, ab] + z_rows[ab], x_of[a, ab] + z_cols[ab])

    def step(p, carry):
        sixteen(p // 4, lax.rem(p, 4), False)
        return carry

    sixteen(0, 0, True)
    lax.fori_loop(1, 8, step, 0)


def back_rows(mixed, cur, gate, new, gain_t, bias_t, weight, tl, ts, ready=None, after=None):
    m = mixed.astype(F32)
    mean = jnp.mean(m, axis=0)
    centred = m - mean[None]
    var = jnp.mean(centred * centred, axis=0)
    ts[...] = lax.rsqrt(var + 1e-5)
    tl[0 : CH * GROUP] = centred.reshape(CH * GROUP, COLS)
    if ready is not None:
        ready()
    for i in range(GROUP):
        c = tl[pl.ds(i, CH, stride=GROUP), :]
        nm = (c * ts[pl.ds(i, 1), :] * gain_t[...] + bias_t[...]).astype(BF16)
        change = dot(nm, weight[...], TN)
        new[i] = (cur[i].astype(F32) + gate[i] * change).astype(BF16)
        if after is not None:
            after(i)


def kernel(
    pair_h, ng_h, nb_h, pw_h, gw_h, og_h, ob_h, ow_h, out_h, last_mixed, last_gate, last_cur,
    cur, normed, gate, sides, all_sides, lt, acc, m_all, m_in,
    ng, nb, pw, gw, og, ob, ow, wt, gain_t, bias_t, tl, tr, ts,
    load_sem, param_sem, send_sem, recv_sem, out_sem, ahead_sem,
):
    row, col = lax.axis_index("row"), lax.axis_index("col")
    me = row * N_COL + col

    def load(g):
        rows = pl.ds(g * GROUP, GROUP)
        return pltpu.make_async_copy(pair_h.at[rows], cur.at[0, rows], load_sem.at[g])

    first = pl.ds(2, 2)
    params = [
        pltpu.make_async_copy(src, dst, param_sem.at[k])
        for k, (src, dst) in enumerate(
            (
                (pw_h.at[0, first], pw.at[0, first]),
                (ng_h, ng),
                (nb_h, nb),
                (pw_h.at[0, pl.ds(0, 2)], pw.at[0, pl.ds(0, 2)]),
                (pw_h.at[1], pw.at[1]),
                (gw_h, gw),
                (og_h, og),
                (ob_h, ob),
                (ow_h, ow),
            )
        )
    ]
    load(0).start()
    for copy in params[:3]:
        copy.start()

    barrier = pltpu.get_barrier_semaphore()

    def greet(r, c):
        pl.semaphore_signal(
            barrier, inc=1, device_id=(r, c), device_id_type=pl.DeviceIdType.MESH
        )

    each_target(row, col, greet)
    for g in range(1, ROWS // GROUP):
        load(g).start()
    for copy in params[3:]:
        copy.start()
    for copy in params[:3]:
        copy.wait()
    for k in range(2, 4):
        wt[0, k * CH : (k + 1) * CH] = pw[0, k].T

    def norm_rows(u, base):
        x = cur[u, pl.ds(base, 2)].reshape(2 * COLS, CH).astype(F32)
        n = layer_norm(x, ng[u : u + 1], nb[u : u + 1]).astype(BF16)
        normed[pl.ds(base, 2)] = n.reshape(2, COLS, CH)
        return n

    def project(u, k, n):
        first = 256 * (1 - k)
        p = dot(wt[u, first : first + 256], n, NT)
        return sigmoid(p[0:128]) * p[128:256]

    def keep(u, first, wide):
        rows = pl.ds(pl.multiple_of(first, GROUP), GROUP)
        sides[u, :, rows, :] = wide[0 : CH * GROUP].reshape(CH, GROUP, COLS).astype(BF16)

    def front_group(u, k, base, first, fresh=True):
        for i in range(0, GROUP, 2):
            if fresh:
                n = norm_rows(u, base + i)
            else:
                n = normed[pl.ds(base + i, 2)].reshape(2 * COLS, CH)
            side = project(u, k, n)
            for r in range(2):
                (tr, tl)[k][pl.ds(i + r, CH, stride=GROUP), :] = side[:, r * COLS : (r + 1) * COLS]
        keep(u, first, (tr, tl)[k])

    def left_by_parts(half):
        def eight(p):
            for q in range(8):
                rows = [half * HALF + p * 8 + q + r * GROUP for r in range(2)]
                order = [(r, c) for part in range(2) for r in rows for c in (part, part + 2)]
                n = jnp.concatenate([normed[r, c * 32 : (c + 1) * 32] for r, c in order], axis=0)
                side = project(1, LEFT, n)
                for part, wide in enumerate((tl, tr)):
                    wide[pl.ds(p * 8 + q, CH, stride=GROUP), :] = side[
                        :, part * COLS : (part + 1) * COLS
                    ]

        loop(2, eight)
        keep(1, half * 48 + 32, tl)
        keep(1, half * 16 + 96, tr)

    def gate_rows(u, step):
        n = normed[pl.ds(step * 4, 4)].reshape(4 * COLS, CH)
        gate[pl.ds(step * 4, 4)] = sigmoid(dot(n, gw[u], NN)).reshape(4, COLS, CH)

    def back_group(u, g):
        base = g * GROUP
        back_rows(
            m_in[u, :, pl.ds(pl.multiple_of(base, GROUP), GROUP), :],
            cur.at[u, pl.ds(base, GROUP)],
            gate.at[pl.ds(base, GROUP)],
            cur.at[1 - u, pl.ds(base, GROUP)],
            gain_t.at[u], bias_t.at[u], ow.at[u], tl, ts,
        )

    def loop(count, body):
        def step(i, carry):
            body(i)
            return carry

        lax.fori_loop(0, count, step, 0)

    def rows_of(flight):
        return (*SIDES, *MIXED)[flight][2]

    def spread(flight, g=0):
        u, first, rows = (*SIDES, *MIXED)[flight]
        if isinstance(g, int) and g == 0:
            start = first
        else:
            start = pl.multiple_of(first + g * ((*SIDES, *MIXED)[flight + 1][1] - first), GROUP)
        part = pl.ds(start, rows)
        if flight < len(SIDES):
            src_at = lambda r, c: sides.at[u, r * N_COL + c, part]
            dst = all_sides.at[u, col, row, part]
        else:
            src_at = lambda r, c: m_all.at[u, c, r, part]
            dst = last_mixed.at[me] if flight == FLIGHTS - 1 else m_in.at[u, me, part]
        index = flight + g
        pltpu.make_async_copy(src_at(row, col), dst, recv_sem.at[index]).start()

        def send(r, c):
            pltpu.make_async_remote_copy(
                src_ref=src_at(r, c),
                dst_ref=dst,
                send_sem=send_sem.at[index],
                recv_sem=recv_sem.at[index],
                device_id=(r, c),
                device_id_type=pl.DeviceIdType.MESH,
            ).start()

        each_target(row, col, send)

    def arrived(flight, g=0):
        size = m_in.at[0, :, pl.ds(0, rows_of(flight))]
        pltpu.make_async_copy(size, size, recv_sem.at[flight + g]).wait()

    def sent(flight):
        size = m_in.at[0, pl.ds(0, DEV - 1), pl.ds(0, rows_of(flight))]
        pltpu.make_async_copy(size, size, send_sem.at[flight]).wait()

    def put_mixed(u, half, jb, out):
        out = out.astype(BF16)
        rows = pl.ds(half * HALF, HALF)
        for k in range(2):
            m_all[u, 2 * jb + k, :, rows, :] = out[:, k * COLS : (k + 1) * COLS].reshape(
                N_ROW, HALF, COLS
            )

    def side_rows(u, c, first, rows=GROUP):
        return all_sides[u, c, :, pl.ds(first, rows), :].reshape(N_ROW * rows, COLS)

    def mix_outgoing(half):
        first = pl.multiple_of(64 + half * HALF, HALF)
        a = jnp.concatenate([side_rows(0, c, first, HALF) for c in range(N_COL)], axis=1)

        def block(jb):
            b = jnp.concatenate(
                [all_sides[0, c, pl.ds(4 * jb, 4), 0:64].reshape(256, COLS) for c in range(N_COL)],
                axis=1,
            )
            put_mixed(0, half, jb, dot(a, b, NT))

        loop(4, block)

    def turn(half, part):
        def block(c):
            t = side_rows(1, c, half * 48 + 32 if part == 0 else half * 16 + 96).T
            for r in range(2):
                lt[half, pl.ds(2 * c, 2), part * HALF : (part + 1) * HALF, r * 256 : r * 256 + 256] = (
                    t[r * 64 : (r + 1) * 64].reshape(2, HALF, 256)
                )

        loop(N_COL, block)

    def mix_incoming(half, k):
        a = lt[k, :, half * HALF : (half + 1) * HALF, :].reshape(512, 512)

        def block(jb):
            b = jnp.concatenate(
                [
                    jnp.concatenate(
                        [
                            side_rows(1, 2 * jb + c, k * 48 + r * GROUP) for r in range(2)
                        ],
                        axis=0,
                    )
                    for c in range(2)
                ],
                axis=1,
            )
            if k == 0:
                acc[half, jb] = dot(a, b, NN)
            else:
                put_mixed(1, half, jb, acc[half, jb] + dot(a, b, NN))

        loop(4, block)


    def open_right(g):
        load(g).wait()
        front_group(0, RIGHT, g * GROUP, g * GROUP)

        @pl.when(g == 0)
        def _():
            pl.semaphore_wait(barrier, DEV - 1)

        spread(FIRST_RIGHT, g)

    loop(ROWS // GROUP, open_right)
    for copy in params[3:]:
        copy.wait()
    for k in range(2):
        wt[0, k * CH : (k + 1) * CH] = pw[0, k].T

    def open_left(half):
        def group(g):
            base = half * HALF + g * GROUP
            front_group(0, LEFT, base, 64 + base, False)

        loop(2, group)
        spread(FIRST_LEFT, half)

    loop(2, open_left)
    for k in range(4):
        wt[1, k * CH : (k + 1) * CH] = pw[1, k].T
    for u in range(2):
        gain_t[u] = jnp.broadcast_to(og[u : u + 1], (CH, CH)).T
        bias_t[u] = jnp.broadcast_to(ob[u : u + 1], (CH, CH)).T
    loop(ROWS // 4, lambda s: gate_rows(0, s))
    for g in range(ROWS // GROUP):
        arrived(FIRST_RIGHT, g)

    def outgoing(half):
        arrived(FIRST_LEFT, half)
        mix_outgoing(half)
        spread(FIRST_MIXED, half)

    loop(2, outgoing)

    def turnover(half):
        arrived(FIRST_MIXED, half)

        def group(g):
            back_group(0, 2 * half + g)
            front_group(1, RIGHT, half * HALF + g * GROUP, half * 48 + g * GROUP)

        loop(2, group)
        spread(NEXT_RIGHT, half)
        left_by_parts(half)
        spread(NEXT_LEFT, half)

    loop(2, turnover)
    spread(LAST_LEFT)
    loop(ROWS // 4, lambda s: gate_rows(1, s))
    last = pl.ds(HALF + GROUP, GROUP)
    ahead = [
        pltpu.make_async_copy(src, dst, ahead_sem.at[k])
        for k, (src, dst) in enumerate(((gate.at[last], last_gate), (cur.at[1, last], last_cur)))
    ]
    for copy in ahead:
        copy.start()
    for half in range(2):
        arrived(NEXT_RIGHT, half)
        arrived(NEXT_LEFT, half)
        turn(half, 0)
        mix_incoming(0, half)
    spread(NEXT_MIXED)
    arrived(LAST_LEFT)
    for half in range(2):
        turn(half, 1)
        mix_incoming(1, half)
    spread(NEXT_MIXED + 1)
    spread(NEXT_MIXED + 2)

    def store(g):
        rows = pl.ds(g * GROUP, GROUP)
        return pltpu.make_async_copy(cur.at[0, rows], out_h.at[rows], out_sem.at[g])

    def close(g):
        @pl.when(g == 0)
        def _():
            arrived(NEXT_MIXED)

        @pl.when(g == 2)
        def _():
            arrived(NEXT_MIXED + 1)

        back_group(1, g)
        store(g).start()

    loop(3, close)
    for flight in range(FLIGHTS):
        sent(flight)
    for copy in (*ahead, store(0), store(1), store(2)):
        copy.wait()
    arrived(NEXT_MIXED + 2)


def finish(
    done_h, mixed_h, gate_h, cur_h, og_h, ob_h, ow_h, out_h,
    done, mixed, gate, cur, og, ob, ow, new, gain_t, bias_t, tl, ts, sem, out_sem,
):
    loads = [
        pltpu.make_async_copy(src, dst, sem.at[k])
        for k, (src, dst) in enumerate(
            (
                (mixed_h, mixed), (og_h, og), (ob_h, ob), (ow_h, ow), (cur_h, cur), (gate_h, gate),
                *((done_h.at[pl.ds(g * 16, 16)], done.at[pl.ds(g * 16, 16)]) for g in range(3)),
            )
        )
    ]
    for copy in loads:
        copy.start()
    for copy in loads[1:4]:
        copy.wait()
    gain_t[...] = jnp.broadcast_to(og[1:2], (CH, CH)).T
    bias_t[...] = jnp.broadcast_to(ob[1:2], (CH, CH)).T
    carried = [
        pltpu.make_async_copy(
            done.at[pl.ds(g * 16, 16)], out_h.at[pl.ds(g * 16, 16)], out_sem.at[g]
        )
        for g in range(3)
    ]
    loads[0].wait()

    def ready():
        for copy in loads[4:6]:
            copy.wait()
        for g in range(3):
            loads[6 + g].wait()
            carried[g].start()

    ends = [
        pltpu.make_async_copy(
            new.at[pl.ds(g * 4, 4)], out_h.at[pl.ds(48 + g * 4, 4)], out_sem.at[3 + g]
        )
        for g in range(4)
    ]

    def after(i):
        if i % 4 == 3:
            ends[i // 4].start()

    back_rows(mixed[...], cur, gate, new, gain_t, bias_t, ow.at[1], tl, ts, ready, after)
    for copy in (*carried, *ends):
        copy.wait()


def shards(*args):
    pieces = (2, DEV, ROWS, COLS)
    planes = (2, N_COL, N_ROW, ROWS, COLS)
    vmem = pltpu.VMEM
    scratch = [
        vmem((2, ROWS, COLS, CH), BF16),
        vmem((ROWS, COLS, CH), BF16),
        vmem((ROWS, COLS, CH), F32),
        vmem((2, DEV, 2 * ROWS, COLS), BF16),
        vmem((2, N_COL, N_ROW, 2 * ROWS, COLS), BF16),
        vmem((2, N_ROW, ROWS, 512), BF16),
        vmem((2, 4, 512, 256), F32),
        vmem(planes, BF16),
        vmem(pieces, BF16),
    ]
    scratch += [vmem(a.shape, a.dtype) for a in args[1:]]
    scratch += [
        vmem((2, 4 * CH, CH), BF16),
        vmem((2, CH, CH), F32),
        vmem((2, CH, CH), F32),
        vmem((CH * GROUP + GROUP, COLS), F32),
        vmem((CH * GROUP + GROUP, COLS), F32),
        vmem((GROUP, COLS), F32),
        pltpu.SemaphoreType.DMA((ROWS // GROUP,)),
        pltpu.SemaphoreType.DMA((9,)),
        pltpu.SemaphoreType.DMA((FLIGHTS,)),
        pltpu.SemaphoreType.DMA((FLIGHTS,)),
        pltpu.SemaphoreType.DMA((3,)),
        pltpu.SemaphoreType.DMA((2,)),
    ]
    quarter = (GROUP, COLS, CH)
    of_kernel = [
        jax.ShapeDtypeStruct((ROWS - GROUP, COLS, CH), BF16),
        jax.ShapeDtypeStruct((DEV, GROUP, COLS), BF16),
        jax.ShapeDtypeStruct(quarter, F32),
        jax.ShapeDtypeStruct(quarter, BF16),
    ]
    parts = pl.pallas_call(
        kernel,
        out_shape=of_kernel,
        in_specs=[pl.BlockSpec(memory_space=pl.ANY)] * 8,
        out_specs=[pl.BlockSpec(memory_space=pl.ANY)] * 4,
        scratch_shapes=scratch,
        compiler_params=pltpu.CompilerParams(
            collective_id=0, has_side_effects=True, vmem_limit_bytes=60 * MIB
        ),
        name="triangle",
    )(*args)
    ends = args[5:]
    return pl.pallas_call(
        finish,
        out_shape=jax.ShapeDtypeStruct((ROWS, COLS, CH), BF16),
        in_specs=[pl.BlockSpec(memory_space=pl.ANY)] * 7,
        out_specs=pl.BlockSpec(memory_space=pl.ANY),
        scratch_shapes=[vmem(a.shape, a.dtype) for a in (*of_kernel, *ends)]
        + [
            vmem(quarter, BF16),
            vmem((CH, CH), F32),
            vmem((CH, CH), F32),
            vmem((CH * GROUP + GROUP, COLS), F32),
            vmem((GROUP, COLS), F32),
            pltpu.SemaphoreType.DMA((9,)),
            pltpu.SemaphoreType.DMA((7,)),
        ],
        compiler_params=pltpu.CompilerParams(vmem_limit_bytes=60 * MIB),
        name="finish",
    )(*parts, *ends)


def solution(mesh):
    placed = (P("row", "col", None), P(), P(), P(), P(), P(), P(), P())
    return jax.shard_map(
        shards, mesh=mesh, in_specs=placed, out_specs=P("row", "col", None), check_vma=False
    )
```

```python
import jax
import jax.numpy as jnp
from jax import lax
from jax.experimental import pallas as pl
from jax.experimental.pallas import tpu as pltpu
from jax.sharding import PartitionSpec as P

F32, BF16 = jnp.float32, jnp.bfloat16
ROWS, COLS, N_ROW, N_COL, CH = 64, 128, 16, 8, 128
DEV = N_ROW * N_COL
GROUP, HALF = 16, 32
MIB = 1 << 20
NT = (((1,), (1,)), ((), ()))
TN = (((0,), (0,)), ((), ()))
NN = (((1,), (0,)), ((), ()))
RIGHT, LEFT = 0, 1
SIDES = (
    (0, 0, 16), (0, 16, 16), (0, 32, 16), (0, 48, 16), (0, 64, 32), (0, 96, 32),
    (1, 0, 32), (1, 48, 32), (1, 32, 16), (1, 80, 16), (1, 96, 32),
)
MIXED = ((0, 0, 32), (0, 32, 32), (1, 0, 32), (1, 32, 16), (1, 48, 16))
FLIGHTS = len(SIDES) + len(MIXED)
FIRST_RIGHT, FIRST_LEFT, NEXT_RIGHT, NEXT_LEFT, LAST_LEFT, FIRST_MIXED, NEXT_MIXED = 0, 4, 6, 8, 10, 11, 13


def sigmoid(v):
    return 0.5 * jnp.tanh(0.5 * v) + 0.5


def layer_norm(v, gain, bias):
    mean = jnp.mean(v, axis=-1, keepdims=True)
    centred = v - mean
    var = jnp.mean(centred * centred, axis=-1, keepdims=True)
    return centred * lax.rsqrt(var + 1e-5) * gain + bias


def dot(a, b, dims):
    return lax.dot_general(a, b, dims, preferred_element_type=F32)


def each_target(row, col, body):
    y, zh, k = row // 4, lax.rem(row // 2, 2), lax.rem(row, 2)
    x, zl = col // 2, lax.rem(col, 2)
    sign = 1 - 2 * k
    turns = [sign * a + 4 for a in range(4)]
    xs = [lax.rem(x + turn, 4) * 2 for turn in turns]
    ys = [lax.rem(y + turn, 4) * 4 for turn in turns]

    def sixteen(core, c, skip):
        core_at = lax.rem(k + core, 2)
        z = [lax.rem(zh * 2 + zl + sign * c + 4 + turn, 4) for turn in turns]
        z_rows = [(at // 2) * 2 + core_at for at in z]
        z_cols = [lax.rem(at, 2) for at in z]
        for b in range(4):
            for a in range(4):
                if not (skip and a == 0 and b == 0):
                    ab = (a + b) % 4
                    body(ys[ab] + z_rows[ab], xs[a] + z_cols[ab])

    def step(p, carry):
        sixteen(p // 4, lax.rem(p, 4), False)
        return carry

    sixteen(0, 0, True)
    lax.fori_loop(1, 8, step, 0)


def back_rows(mixed, cur, gate, new, gain_t, bias_t, weight, tl, ts, ready=None, after=None):
    m = mixed.astype(F32)
    mean = jnp.mean(m, axis=0)
    centred = m - mean[None]
    var = jnp.mean(centred * centred, axis=0)
    ts[...] = lax.rsqrt(var + 1e-5)
    tl[0 : CH * GROUP] = centred.reshape(CH * GROUP, COLS)
    if ready is not None:
        ready()
    for i in range(GROUP):
        c = tl[pl.ds(i, CH, stride=GROUP), :]
        nm = (c * ts[pl.ds(i, 1), :] * gain_t[...] + bias_t[...]).astype(BF16)
        change = dot(nm, weight[...], TN)
        new[i] = (cur[i].astype(F32) + gate[i] * change).astype(BF16)
        if after is not None:
            after(i)


def kernel(
    pair_h, ng_h, nb_h, pw_h, gw_h, og_h, ob_h, ow_h, out_h, last_mixed, last_gate, last_cur,
    cur, normed, gate, sides, all_sides, lt, acc, m_all, m_in,
    ng, nb, pw, gw, og, ob, ow, wt, gain_t, bias_t, tl, tr, ts,
    load_sem, param_sem, send_sem, recv_sem, out_sem, ahead_sem,
):
    row, col = lax.axis_index("row"), lax.axis_index("col")
    me = row * N_COL + col

    def load(g):
        rows = pl.ds(g * GROUP, GROUP)
        return pltpu.make_async_copy(pair_h.at[rows], cur.at[0, rows], load_sem.at[g])

    first = pl.ds(2, 2)
    params = [
        pltpu.make_async_copy(src, dst, param_sem.at[k])
        for k, (src, dst) in enumerate(
            (
                (pw_h.at[0, first], pw.at[0, first]),
                (ng_h, ng),
                (nb_h, nb),
                (pw_h.at[0, pl.ds(0, 2)], pw.at[0, pl.ds(0, 2)]),
                (pw_h.at[1], pw.at[1]),
                (gw_h, gw),
                (og_h, og),
                (ob_h, ob),
                (ow_h, ow),
            )
        )
    ]
    load(0).start()
    for copy in params[:3]:
        copy.start()

    barrier = pltpu.get_barrier_semaphore()

    def greet(r, c):
        pl.semaphore_signal(
            barrier, inc=1, device_id=(r, c), device_id_type=pl.DeviceIdType.MESH
        )

    each_target(row, col, greet)
    for g in range(1, ROWS // GROUP):
        load(g).start()
    for copy in params[3:]:
        copy.start()
    for copy in params[:3]:
        copy.wait()
    for k in range(2, 4):
        wt[0, k * CH : (k + 1) * CH] = pw[0, k].T

    def norm_rows(u, base):
        x = cur[u, pl.ds(base, 2)].reshape(2 * COLS, CH).astype(F32)
        n = layer_norm(x, ng[u : u + 1], nb[u : u + 1]).astype(BF16)
        normed[pl.ds(base, 2)] = n.reshape(2, COLS, CH)
        return n

    def project(u, k, n):
        first = 256 * (1 - k)
        p = dot(wt[u, first : first + 256], n, NT)
        return sigmoid(p[0:128]) * p[128:256]

    def keep(u, first, wide):
        rows = pl.ds(pl.multiple_of(first, GROUP), GROUP)
        sides[u, :, rows, :] = wide[0 : CH * GROUP].reshape(CH, GROUP, COLS).astype(BF16)

    def front_group(u, k, base, first, fresh=True):
        for i in range(0, GROUP, 2):
            if fresh:
                n = norm_rows(u, base + i)
            else:
                n = normed[pl.ds(base + i, 2)].reshape(2 * COLS, CH)
            side = project(u, k, n)
            for r in range(2):
                (tr, tl)[k][pl.ds(i + r, CH, stride=GROUP), :] = side[:, r * COLS : (r + 1) * COLS]
        keep(u, first, (tr, tl)[k])

    def left_by_parts(half):
        def eight(p):
            for q in range(8):
                rows = [half * HALF + p * 8 + q + r * GROUP for r in range(2)]
                order = [(r, c) for part in range(2) for r in rows for c in (part, part + 2)]
                n = jnp.concatenate([normed[r, c * 32 : (c + 1) * 32] for r, c in order], axis=0)
                side = project(1, LEFT, n)
                for part, wide in enumerate((tl, tr)):
                    wide[pl.ds(p * 8 + q, CH, stride=GROUP), :] = side[
                        :, part * COLS : (part + 1) * COLS
                    ]

        loop(2, eight)
        keep(1, half * 48 + 32, tl)
        keep(1, half * 16 + 96, tr)

    def gate_rows(u, step):
        n = normed[pl.ds(step * 4, 4)].reshape(4 * COLS, CH)
        gate[pl.ds(step * 4, 4)] = sigmoid(dot(n, gw[u], NN)).reshape(4, COLS, CH)

    def back_group(u, g):
        base = g * GROUP
        back_rows(
            m_in[u, :, pl.ds(pl.multiple_of(base, GROUP), GROUP), :],
            cur.at[u, pl.ds(base, GROUP)],
            gate.at[pl.ds(base, GROUP)],
            cur.at[1 - u, pl.ds(base, GROUP)],
            gain_t.at[u], bias_t.at[u], ow.at[u], tl, ts,
        )

    def loop(count, body):
        def step(i, carry):
            body(i)
            return carry

        lax.fori_loop(0, count, step, 0)

    def rows_of(flight):
        return (*SIDES, *MIXED)[flight][2]

    def spread(flight, g=0):
        u, first, rows = (*SIDES, *MIXED)[flight]
        if isinstance(g, int) and g == 0:
            start = first
        else:
            start = pl.multiple_of(first + g * ((*SIDES, *MIXED)[flight + 1][1] - first), GROUP)
        part = pl.ds(start, rows)
        if flight < len(SIDES):
            src_at = lambda r, c: sides.at[u, r * N_COL + c, part]
            dst = all_sides.at[u, col, row, part]
        else:
            src_at = lambda r, c: m_all.at[u, c, r, part]
            dst = last_mixed.at[me] if flight == FLIGHTS - 1 else m_in.at[u, me, part]
        index = flight + g
        pltpu.make_async_copy(src_at(row, col), dst, recv_sem.at[index]).start()

        def send(r, c):
            pltpu.make_async_remote_copy(
                src_ref=src_at(r, c),
                dst_ref=dst,
                send_sem=send_sem.at[index],
                recv_sem=recv_sem.at[index],
                device_id=(r, c),
                device_id_type=pl.DeviceIdType.MESH,
            ).start()

        each_target(row, col, send)

    def arrived(flight, g=0):
        size = m_in.at[0, :, pl.ds(0, rows_of(flight))]
        pltpu.make_async_copy(size, size, recv_sem.at[flight + g]).wait()

    def sent(flight):
        size = m_in.at[0, pl.ds(0, DEV - 1), pl.ds(0, rows_of(flight))]
        pltpu.make_async_copy(size, size, send_sem.at[flight]).wait()

    def put_mixed(u, half, jb, out):
        out = out.astype(BF16)
        rows = pl.ds(half * HALF, HALF)
        for k in range(2):
            m_all[u, 2 * jb + k, :, rows, :] = out[:, k * COLS : (k + 1) * COLS].reshape(
                N_ROW, HALF, COLS
            )

    def side_rows(u, c, first, rows=GROUP):
        return all_sides[u, c, :, pl.ds(first, rows), :].reshape(N_ROW * rows, COLS)

    def mix_outgoing(half):
        first = pl.multiple_of(64 + half * HALF, HALF)
        a = jnp.concatenate([side_rows(0, c, first, HALF) for c in range(N_COL)], axis=1)

        def block(jb):
            b = jnp.concatenate(
                [all_sides[0, c, pl.ds(4 * jb, 4), 0:64].reshape(256, COLS) for c in range(N_COL)],
                axis=1,
            )
            put_mixed(0, half, jb, dot(a, b, NT))

        loop(4, block)

    def turn(half, part):
        def block(c):
            t = side_rows(1, c, half * 48 + 32 if part == 0 else half * 16 + 96).T
            for r in range(2):
                lt[half, pl.ds(2 * c, 2), part * HALF : (part + 1) * HALF, r * 256 : r * 256 + 256] = (
                    t[r * 64 : (r + 1) * 64].reshape(2, HALF, 256)
                )

        loop(N_COL, block)

    def mix_incoming(half, k):
        a = lt[k, :, half * HALF : (half + 1) * HALF, :].reshape(512, 512)

        def block(jb):
            b = jnp.concatenate(
                [
                    jnp.concatenate(
                        [
                            side_rows(1, 2 * jb + c, k * 48 + r * GROUP) for r in range(2)
                        ],
                        axis=0,
                    )
                    for c in range(2)
                ],
                axis=1,
            )
            if k == 0:
                acc[half, jb] = dot(a, b, NN)
            else:
                put_mixed(1, half, jb, acc[half, jb] + dot(a, b, NN))

        loop(4, block)


    def open_right(g):
        load(g).wait()
        front_group(0, RIGHT, g * GROUP, g * GROUP)

        @pl.when(g == 0)
        def _():
            pl.semaphore_wait(barrier, DEV - 1)

        spread(FIRST_RIGHT, g)

    loop(ROWS // GROUP, open_right)
    for copy in params[3:]:
        copy.wait()
    for k in range(2):
        wt[0, k * CH : (k + 1) * CH] = pw[0, k].T

    def open_left(half):
        def group(g):
            base = half * HALF + g * GROUP
            front_group(0, LEFT, base, 64 + base, False)

        loop(2, group)
        spread(FIRST_LEFT, half)

    loop(2, open_left)
    for k in range(4):
        wt[1, k * CH : (k + 1) * CH] = pw[1, k].T
    for u in range(2):
        gain_t[u] = jnp.broadcast_to(og[u : u + 1], (CH, CH)).T
        bias_t[u] = jnp.broadcast_to(ob[u : u + 1], (CH, CH)).T
    loop(ROWS // 4, lambda s: gate_rows(0, s))
    for g in range(ROWS // GROUP):
        arrived(FIRST_RIGHT, g)

    def outgoing(half):
        arrived(FIRST_LEFT, half)
        mix_outgoing(half)
        spread(FIRST_MIXED, half)

    loop(2, outgoing)

    def turnover(half):
        arrived(FIRST_MIXED, half)

        def group(g):
            back_group(0, 2 * half + g)
            front_group(1, RIGHT, half * HALF + g * GROUP, half * 48 + g * GROUP)

        loop(2, group)
        spread(NEXT_RIGHT, half)
        left_by_parts(half)
        spread(NEXT_LEFT, half)

    loop(2, turnover)
    spread(LAST_LEFT)
    loop(ROWS // 4, lambda s: gate_rows(1, s))
    last = pl.ds(HALF + GROUP, GROUP)
    ahead = [
        pltpu.make_async_copy(src, dst, ahead_sem.at[k])
        for k, (src, dst) in enumerate(((gate.at[last], last_gate), (cur.at[1, last], last_cur)))
    ]
    for copy in ahead:
        copy.start()
    for half in range(2):
        arrived(NEXT_RIGHT, half)
        arrived(NEXT_LEFT, half)
        turn(half, 0)
        mix_incoming(0, half)
    spread(NEXT_MIXED)
    arrived(LAST_LEFT)
    for half in range(2):
        turn(half, 1)
        mix_incoming(1, half)
    spread(NEXT_MIXED + 1)
    spread(NEXT_MIXED + 2)

    def store(g):
        rows = pl.ds(g * GROUP, GROUP)
        return pltpu.make_async_copy(cur.at[0, rows], out_h.at[rows], out_sem.at[g])

    def close(g):
        @pl.when(g == 0)
        def _():
            arrived(NEXT_MIXED)

        @pl.when(g == 2)
        def _():
            arrived(NEXT_MIXED + 1)

        back_group(1, g)
        store(g).start()

    loop(3, close)
    for flight in range(FLIGHTS):
        sent(flight)
    for copy in (*ahead, store(0), store(1), store(2)):
        copy.wait()
    arrived(NEXT_MIXED + 2)


def finish(
    done_h, mixed_h, gate_h, cur_h, og_h, ob_h, ow_h, out_h,
    done, mixed, gate, cur, og, ob, ow, new, gain_t, bias_t, tl, ts, sem, out_sem,
):
    loads = [
        pltpu.make_async_copy(src, dst, sem.at[k])
        for k, (src, dst) in enumerate(
            (
                (mixed_h, mixed), (og_h, og), (ob_h, ob), (ow_h, ow), (cur_h, cur), (gate_h, gate),
                (done_h, done),
            )
        )
    ]
    for copy in loads:
        copy.start()
    for copy in loads[1:4]:
        copy.wait()
    gain_t[...] = jnp.broadcast_to(og[1:2], (CH, CH)).T
    bias_t[...] = jnp.broadcast_to(ob[1:2], (CH, CH)).T
    kept = pl.ds(0, ROWS - GROUP)
    carried = pltpu.make_async_copy(done, out_h.at[kept], out_sem.at[0])
    loads[0].wait()

    def ready():
        for copy in loads[4:6]:
            copy.wait()

    ends = [
        pltpu.make_async_copy(
            new.at[pl.ds(g * 8, 8)], out_h.at[pl.ds(48 + g * 8, 8)], out_sem.at[1 + g]
        )
        for g in range(2)
    ]

    def after(i):
        if i % 8 == 7:
            ends[i // 8].start()

    back_rows(mixed[...], cur, gate, new, gain_t, bias_t, ow.at[1], tl, ts, ready, after)
    loads[6].wait()
    carried.start()
    for copy in (carried, *ends):
        copy.wait()


def shards(*args):
    pieces = (2, DEV, ROWS, COLS)
    planes = (2, N_COL, N_ROW, ROWS, COLS)
    vmem = pltpu.VMEM
    scratch = [
        vmem((2, ROWS, COLS, CH), BF16),
        vmem((ROWS, COLS, CH), BF16),
        vmem((ROWS, COLS, CH), F32),
        vmem((2, DEV, 2 * ROWS, COLS), BF16),
        vmem((2, N_COL, N_ROW, 2 * ROWS, COLS), BF16),
        vmem((2, N_ROW, ROWS, 512), BF16),
        vmem((2, 4, 512, 256), F32),
        vmem(planes, BF16),
        vmem(pieces, BF16),
    ]
    scratch += [vmem(a.shape, a.dtype) for a in args[1:]]
    scratch += [
        vmem((2, 4 * CH, CH), BF16),
        vmem((2, CH, CH), F32),
        vmem((2, CH, CH), F32),
        vmem((CH * GROUP + GROUP, COLS), F32),
        vmem((CH * GROUP + GROUP, COLS), F32),
        vmem((GROUP, COLS), F32),
        pltpu.SemaphoreType.DMA((ROWS // GROUP,)),
        pltpu.SemaphoreType.DMA((9,)),
        pltpu.SemaphoreType.DMA((FLIGHTS,)),
        pltpu.SemaphoreType.DMA((FLIGHTS,)),
        pltpu.SemaphoreType.DMA((3,)),
        pltpu.SemaphoreType.DMA((2,)),
    ]
    quarter = (GROUP, COLS, CH)
    of_kernel = [
        jax.ShapeDtypeStruct((ROWS - GROUP, COLS, CH), BF16),
        jax.ShapeDtypeStruct((DEV, GROUP, COLS), BF16),
        jax.ShapeDtypeStruct(quarter, F32),
        jax.ShapeDtypeStruct(quarter, BF16),
    ]
    parts = pl.pallas_call(
        kernel,
        out_shape=of_kernel,
        in_specs=[pl.BlockSpec(memory_space=pl.ANY)] * 8,
        out_specs=[pl.BlockSpec(memory_space=pl.ANY)] * 4,
        scratch_shapes=scratch,
        compiler_params=pltpu.CompilerParams(
            collective_id=0, has_side_effects=True, vmem_limit_bytes=60 * MIB
        ),
        name="triangle",
    )(*args)
    ends = args[5:]
    return pl.pallas_call(
        finish,
        out_shape=jax.ShapeDtypeStruct((ROWS, COLS, CH), BF16),
        in_specs=[pl.BlockSpec(memory_space=pl.ANY)] * 7,
        out_specs=pl.BlockSpec(memory_space=pl.ANY),
        scratch_shapes=[vmem(a.shape, a.dtype) for a in (*of_kernel, *ends)]
        + [
            vmem(quarter, BF16),
            vmem((CH, CH), F32),
            vmem((CH, CH), F32),
            vmem((CH * GROUP + GROUP, COLS), F32),
            vmem((GROUP, COLS), F32),
            pltpu.SemaphoreType.DMA((7,)),
            pltpu.SemaphoreType.DMA((3,)),
        ],
        compiler_params=pltpu.CompilerParams(vmem_limit_bytes=60 * MIB),
        name="finish",
    )(*parts, *ends)


def solution(mesh):
    placed = (P("row", "col", None), P(), P(), P(), P(), P(), P(), P())
    return jax.shard_map(
        shards, mesh=mesh, in_specs=placed, out_specs=P("row", "col", None), check_vma=False
    )
```
